32 devices in a mesh: grp: 16 (over z, y, core), tp: 2 (over x).
Axes of the slice: x: 2, y: 2, z: 4, core: 2. Of those that a mesh axis runs over, the one named last changes fastest.
Arguments:
- queries: bfloat16 [16, 2, 512, 2048], P('grp', None, None, 'tp'), may hold values from -9 to 9
- fresh_kv: bfloat16 [16, 2, 512, 2, 2048], P('grp', None, None, None, 'tp'), may hold values from -9 to 9
- stale_kv: bfloat16 [16, 2, 512, 2, 2048], P('grp', None, None, None, 'tp'), may hold values from -6 to 6
- text_kv: bfloat16 [16, 2, 256, 2, 2048], P('grp', None, None, None, 'tp'), may hold values from -6 to 6
- w_velocity: bfloat16 [2048, 64], P('tp'), may hold values from -2.390625 to 2.390625
- latent: float32 [16, 2, 512, 64], P('grp', None, 'tp'), may hold values from -6 to 6
- live_counts: int32 [16, 2], replicated, may hold values from 128 to 512, as said below
- refresh_rows: int32 [16, 2, 64], replicated, may hold values from 0 to 511, as said below
- request_list: int32 [16], replicated, may hold values from 0 to 15, each once
- timesteps: int32 [16, 2], replicated, may hold values from 0 to 999, as said below
Outputs:
- next_stale: bfloat16 [16, 2, 512, 2, 2048], P('grp', None, None, None, 'tp')
- velocity: float32 [16, 2, 512, 64], P('grp', None, 'tp')
- latent_next: float32 [16, 2, 512, 64], P('grp', None, 'tp')
The draws below stay inside these ranges and needn't reach their ends.
Inputs may be any that keep to these rules, and one draw needn't show every extreme that they name: `live_counts`: 512 is reached in every draw. `refresh_rows`: rows within one list are distinct. `timesteps`: the next timestep is below the current one. `request_list`: each request appears once.
All inputs are finite; a program needn't handle non-finite values.
Results may differ from the reference program's by a relative error of at most 0.0045.
Values may be sent and summed in bfloat16 or wider, within the bound.
No kernel may reach another device: no remote copies, remote signals or barrier semaphores. Data moves between devices by JAX's collectives and lax.ppermute only.
A program may use at most 128 MiB of HBM per device.

```python
import math
import jax
import jax.numpy as jnp
from jax import lax

HEADS = 16
HD = 128
INNER = 2048
CH = 64
IMG_DEV = 512
TXT_DEV = 256
REQ_DEV = 2
RECOMP = 64
GROUPS = 16
REQUESTS = 16
N_GRP = 16


def draw_queries(key, part):
    shape = (GROUPS, REQ_DEV, IMG_DEV, HEADS * HD)
    base = 1.2 * jnp.clip(jax.random.normal(jax.random.fold_in(key, 1), shape, jnp.float32), -6.0, 6.0)
    return base.astype(jnp.bfloat16)


def draw_fresh_kv(key, part):
    shape = (GROUPS, REQ_DEV, IMG_DEV, 2, HEADS * HD)
    base = jnp.clip(jax.random.normal(jax.random.fold_in(key, 2), shape, jnp.float32), -6.0, 6.0)
    return base.astype(jnp.bfloat16)


def draw_live_counts(key, part):
    counts = jax.random.randint(jax.random.fold_in(key, 3), (GROUPS * REQ_DEV,), IMG_DEV // 4, IMG_DEV + 1)
    chosen = jax.random.randint(jax.random.fold_in(key, 4), (), 0, GROUPS * REQ_DEV)
    counts = jnp.where(jnp.arange(GROUPS * REQ_DEV) == chosen, IMG_DEV, counts)
    return counts.reshape(GROUPS, REQ_DEV).astype(jnp.int32)


def draw_refresh_rows(key, part):
    streams = jax.random.split(jax.random.fold_in(key, 5), GROUPS * REQ_DEV)
    row_lists = jax.vmap(lambda stream: jax.random.permutation(stream, IMG_DEV)[:RECOMP])(streams)
    return row_lists.reshape(GROUPS, REQ_DEV, RECOMP).astype(jnp.int32)


def draw_timesteps(key, part):
    starts = jax.random.randint(jax.random.fold_in(key, 6), (REQUESTS,), 400, 1000)
    strides = jax.random.randint(jax.random.fold_in(key, 8), (REQUESTS,), 100, 400)
    return jnp.stack([starts, starts - strides], axis=1).astype(jnp.int32)


def block_scale(rng, extent, cuts, smallest, top_value):
    def one(position, blocks):
        draws = jax.random.uniform(jax.random.fold_in(jax.random.fold_in(rng, 6), position), (blocks,), jnp.float32, smallest / len(cuts), top_value / len(cuts))
        return jnp.repeat(jnp.exp(draws), extent[position] // blocks).reshape((-1,) + (1,) * (len(extent) - position - 1))

    level = one(*cuts[0])
    for cut in cuts[1:]:
        level = level * one(*cut)
    return level


def gaussian(stream_key, extent, spread, limit, pieces=(), kind=jnp.bfloat16):
    drawn = spread * jax.random.normal(stream_key, extent, jnp.float32)
    if pieces:
        drawn = drawn * block_scale(stream_key, extent, pieces, -0.22, 0.18)
    return jnp.clip(drawn, -limit, limit).astype(kind)


def setup_inputs(seed: int = 0) -> dict:
    key_of = jax.random.split(jax.random.key(seed), 11)
    queries = draw_queries(jax.random.fold_in(key_of[10], 71), 0)
    fresh_kv = draw_fresh_kv(jax.random.fold_in(key_of[10], 71), 0)
    stale_kv = gaussian(key_of[2], (GROUPS, REQ_DEV, IMG_DEV, 2, INNER), 1.0, 6.0, ((0, 16), (4, 2)))
    text_kv = gaussian(key_of[3], (GROUPS, REQ_DEV, TXT_DEV, 2, INNER), 1.0, 6.0, ((0, 16), (4, 2)))
    w_velocity = gaussian(key_of[4], (INNER, CH), 0.4, 2.390625, ((0, 2),))
    latent = gaussian(key_of[5], (GROUPS, REQ_DEV, IMG_DEV, CH), 1.0, 6.0, ((0, 16), (2, 2)), jnp.float32)
    live_counts = draw_live_counts(jax.random.fold_in(key_of[10], 71), 0)
    refresh_rows = draw_refresh_rows(jax.random.fold_in(key_of[10], 71), 0)
    request_list = jax.random.permutation(key_of[8], REQUESTS).astype(jnp.int32)
    timesteps = draw_timesteps(jax.random.fold_in(key_of[10], 71), 0)
    return dict(queries=queries, fresh_kv=fresh_kv, stale_kv=stale_kv, text_kv=text_kv, w_velocity=w_velocity, latent=latent, live_counts=live_counts, refresh_rows=refresh_rows, request_list=request_list, timesteps=timesteps)


def slot_velocity(slot_query, own_kv, partner_kv, text_pair, own_live, partner_live, w_velocity):
    key_rows = jnp.concatenate([own_kv[:, 0], partner_kv[:, 0], text_pair[:, 0]], axis=0)
    value_rows = jnp.concatenate([own_kv[:, 1], partner_kv[:, 1], text_pair[:, 1]], axis=0)
    row_ids = jnp.arange(IMG_DEV, dtype=jnp.int32)
    live_mask = jnp.concatenate([row_ids < own_live, row_ids < partner_live, jnp.ones((2 * TXT_DEV,), dtype=bool)])
    query_float = slot_query.astype(jnp.float32).reshape(IMG_DEV, HEADS, HD)
    key_float = key_rows.astype(jnp.float32).reshape(-1, HEADS, HD)
    value_float = value_rows.astype(jnp.float32).reshape(-1, HEADS, HD)
    scores = jnp.einsum('qhd,khd->hqk', query_float, key_float) * (1.0 / math.sqrt(HD))
    scores = jnp.where(live_mask[None, None, :], scores, -jnp.inf)
    row_top = lax.optimization_barrier(jnp.max(scores, axis=2, keepdims=True))
    weights = jnp.exp(scores - row_top)
    totals = lax.optimization_barrier(jnp.sum(weights, axis=2))
    rounded = weights.astype(jnp.bfloat16).astype(jnp.float32)
    blended = jnp.einsum('hqk,khd->qhd', rounded, value_float) / jnp.transpose(totals)[:, :, None]
    blended = blended.reshape(IMG_DEV, HEADS * HD).astype(jnp.bfloat16)
    velocity = jnp.dot(blended, w_velocity, preferred_element_type=jnp.float32)
    return jnp.where((row_ids < own_live)[:, None], velocity, 0.0)

def reference(queries, fresh_kv, stale_kv, text_kv, w_velocity, latent, live_counts, refresh_rows, request_list, timesteps):
    half_groups = N_GRP // 2

    def per_group(group_index):
        partner = (group_index + half_groups) % N_GRP
        partner_fresh = fresh_kv[partner]
        velocities = []
        latents = []
        for slot_index in range(REQ_DEV):
            listed = refresh_rows[partner, slot_index].astype(jnp.int32)
            repaired = stale_kv[group_index, slot_index].at[listed].set(partner_fresh[slot_index][listed])
            text_pair = jnp.concatenate([text_kv[group_index, slot_index], text_kv[partner, slot_index]], axis=0)
            velocity = slot_velocity(queries[group_index, slot_index], fresh_kv[group_index, slot_index], repaired, text_pair, live_counts[group_index, slot_index], live_counts[partner, slot_index], w_velocity)
            request_id = request_list[group_index % half_groups * REQ_DEV + slot_index]
            times = timesteps[request_id]
            step_size = (times[1] - times[0]).astype(jnp.float32) / 1000.0
            velocities.append(velocity)
            latents.append(latent[group_index, slot_index] + step_size * velocity)
        return (jnp.stack(velocities), jnp.stack(latents))
    velocity, latent_next = lax.map(per_group, jnp.arange(N_GRP, dtype=jnp.int32))
    next_stale = jnp.roll(fresh_kv, half_groups, axis=0)
    return (next_stale, velocity, latent_next)
```

```python
import functools
import math

import jax
import jax.numpy as jnp
from jax import lax
from jax.experimental import pallas as pl
from jax.experimental.pallas import tpu as pltpu
from jax.sharding import PartitionSpec as P

HD = 128
HBM = pltpu.MemorySpace.HBM
SMEM = pltpu.MemorySpace.SMEM
VMEM_LIMIT = 50 * 1024 * 1024


def from_behind(block, axis, distance):
    devices = range(lax.axis_size(axis))
    route = [((i - distance) % len(devices), i) for i in devices]
    return lax.ppermute(block, axis, route)


def send_order(lists, img_rows):
    count = lists.shape[2]
    zone = count + jnp.arange(count, dtype=jnp.int32)
    order = jnp.arange(count, dtype=jnp.int32)
    earlier = order[:, None] >= order[None, :]
    free = jnp.logical_not(jnp.any(lists[..., :, None] == zone, axis=2))
    outside = lists >= 2 * count
    free_rank = jnp.sum(jnp.where(earlier, free[..., None, :], False).astype(jnp.int32), axis=3)
    outside_rank = jnp.sum(jnp.where(earlier, outside[..., None, :], False).astype(jnp.int32), axis=3)
    match = (
        outside[..., :, None]
        & free[..., None, :]
        & (outside_rank[..., :, None] == free_rank[..., None, :])
    )
    listed_at = jnp.sum(jnp.where(match, lists[..., :, None], 0), axis=2)
    zone_source = jnp.where(listed_at > 0, listed_at, zone)
    place = jnp.sum(jnp.where(match, zone, 0), axis=3)
    tail = jnp.arange(2 * count, img_rows, dtype=jnp.int32)
    moved = jnp.sum(
        jnp.where(lists[..., :, None] == tail, place[..., :, None], 0), axis=2
    )
    tail_source = jnp.where(moved > 0, moved, tail)
    head = jnp.broadcast_to(order, lists.shape)
    return jnp.concatenate([head, zone_source, tail_source], axis=2)


def pick_rows_kernel(slots, first, rows, total, order_ref, fresh_ref, *rest):
    out_ref, sem = rest[-2], rest[-1]
    for out_slot, slot in enumerate(slots):

        def issue(i, carry):
            source = order_ref[slot * total + first + i]
            pltpu.make_async_copy(fresh_ref.at[slot, source], out_ref.at[out_slot, i], sem).start()
            return carry

        lax.fori_loop(0, rows, issue, 0, unroll=8)
    pltpu.make_async_copy(out_ref, out_ref, sem).wait()


def pick_rows(order, fresh, slots, first, rows, after=()):
    total = fresh.shape[1]
    size = len(slots) * rows * fresh.shape[2] * fresh.shape[3]
    return pl.pallas_call(
        functools.partial(pick_rows_kernel, slots, first, rows, total),
        out_shape=jax.ShapeDtypeStruct((len(slots), rows) + fresh.shape[2:], fresh.dtype),
        in_specs=[pl.BlockSpec(memory_space=SMEM)] + [pl.BlockSpec(memory_space=HBM)] * (1 + len(after)),
        out_specs=pl.BlockSpec(memory_space=HBM),
        scratch_shapes=[pltpu.SemaphoreType.DMA],
        cost_estimate=pl.CostEstimate(flops=0, bytes_accessed=4 * size, transcendentals=0),
        name="pick_rows",
    )(order, fresh, *after)


def place_rows_kernel(pieces, total, order_ref, *rest):
    refs, out_ref, sem = rest[: len(pieces)], rest[-2], rest[-1]
    for (slots, first, rows), piece_ref in zip(pieces, refs):
        for in_slot, slot in enumerate(slots):

            def issue(i, carry):
                target = order_ref[slot * total + first + i]
                pltpu.make_async_copy(piece_ref.at[in_slot, i], out_ref.at[slot, target], sem).start()
                return carry

            lax.fori_loop(0, rows, issue, 0, unroll=8)
    for piece_ref in refs:
        pltpu.make_async_copy(piece_ref, piece_ref, sem).wait()


def place_rows(order, parts, pieces, shape, whole=None):
    total = shape[1]
    size = sum(math.prod(part.shape) for part in parts)
    extra = () if whole is None else (whole,)
    return pl.pallas_call(
        functools.partial(place_rows_kernel, pieces, total),
        out_shape=jax.ShapeDtypeStruct(shape, parts[0].dtype),
        in_specs=[pl.BlockSpec(memory_space=SMEM)]
        + [pl.BlockSpec(memory_space=HBM)] * (len(parts) + len(extra)),
        out_specs=pl.BlockSpec(memory_space=HBM),
        scratch_shapes=[pltpu.SemaphoreType.DMA],
        input_output_aliases={} if whole is None else {1 + len(parts): 0},
        cost_estimate=pl.CostEstimate(flops=0, bytes_accessed=4 * size, transcendentals=0),
        name="place_rows",
    )(order, *parts, *extra)


def across(a, b):
    return lax.dot_general(a, b, (((1,), (1,)), ((), ())), preferred_element_type=jnp.float32)


def text_kernel(k_ref, v_ref, w_ref, out_ref):
    rows = k_ref.shape[1]
    channels = w_ref.shape[0]
    out_ref[0, 0, :rows, :] = k_ref[0]
    projected = across(w_ref[...], v_ref[0]).astype(out_ref.dtype)
    for part in range(rows // HD):
        start = rows + part * channels
        out_ref[0, 0, start : start + channels, :] = projected[:, part * HD : (part + 1) * HD]


def project_text(keys, values, w_t):
    slots, rows, width = keys.shape
    heads = width // HD
    channels = w_t.shape[0]
    packed = rows + channels * rows // HD
    block = pl.BlockSpec((1, rows, HD), lambda s, h: (s, 0, h))
    return pl.pallas_call(
        text_kernel,
        grid=(slots, heads),
        out_shape=jax.ShapeDtypeStruct((slots, heads, packed, HD), keys.dtype),
        in_specs=[block, block, pl.BlockSpec((channels, HD), lambda s, h: (0, h))],
        out_specs=pl.BlockSpec((1, 1, packed, HD), lambda s, h: (s, h, 0, 0)),
        cost_estimate=pl.CostEstimate(
            flops=2 * slots * rows * width * channels, bytes_accessed=4 * keys.size * 2, transcendentals=0
        ),
        name="project_text",
    )(keys, values, w_t)


def attention_kernel(text_rows, *refs):
    (q_ref, kf_ref, vf_ref, ks_ref, vs_ref, kh_ref, vh_ref, own_ref, other_ref, w_ref, bias_ref) = refs[:11]
    out_ref, scores_ref = refs[11], refs[12]
    head = pl.program_id(1)
    query = q_ref[0]
    w_t = w_ref[...]
    channels = w_t.shape[0]
    scale = 1.0 / math.sqrt(HD)
    pieces = []
    for k_ref, v_ref in ((kf_ref, vf_ref), (ks_ref, vs_ref), (kh_ref, vh_ref)):
        rows = k_ref.shape[1]
        step = min(rows, 256)
        for start in range(0, rows, step):
            pieces.append((k_ref.at[0, start : start + step], v_ref.at[0, start : start + step], step))
    for t_ref in (own_ref, other_ref):
        pieces.append((t_ref.at[0, 0, :text_rows], t_ref, text_rows))
    top = None
    at = 0
    for k_ref, _, rows in pieces:
        scores = across(k_ref[...], query) * scale + bias_ref[0, at : at + rows]
        scores_ref[at : at + rows, :] = scores
        piece_top = jnp.max(scores, axis=0, keepdims=True)
        top = piece_top if top is None else jnp.maximum(top, piece_top)
        at += rows
    total = jnp.zeros_like(top)
    blended = jnp.zeros((channels, query.shape[0]), jnp.float32)
    at = 0
    for _, v_ref, rows in pieces:
        weights = jnp.exp(scores_ref[at : at + rows, :] - top)
        total += jnp.sum(weights, axis=0, keepdims=True)
        rounded = weights.astype(jnp.bfloat16)
        if v_ref.shape[-2] == rows and len(v_ref.shape) == 2:
            projected = across(w_t, v_ref[...]).astype(jnp.bfloat16)
            blended += jnp.dot(projected, rounded, preferred_element_type=jnp.float32)
        else:
            for part in range(rows // HD):
                start = rows + part * channels
                blended += jnp.dot(
                    v_ref[0, 0, start : start + channels, :],
                    rounded[part * HD : (part + 1) * HD],
                    preferred_element_type=jnp.float32,
                )
        at += rows
    term = blended / total

    @pl.when(head == 0)
    def _():
        out_ref[0] = term

    @pl.when(head != 0)
    def _():
        out_ref[0] += term


def attention(queries, fresh_k, fresh_v, stale_k, stale_v, hot_k, hot_v, text_own, text_other, w_t, bias):
    slots, rows, width = queries.shape
    heads = width // HD
    channels = w_t.shape[0]
    key_rows = bias.shape[1]
    text_rows = (text_own.shape[2] * HD) // (HD + channels)

    def wide(array):
        return pl.BlockSpec((1, array.shape[1], HD), lambda s, h: (s, 0, h))

    packed = pl.BlockSpec((1, 1) + text_own.shape[2:], lambda s, h: (s, h, 0, 0))
    many = slots * heads * rows * key_rows
    return pl.pallas_call(
        functools.partial(attention_kernel, text_rows),
        grid=(slots, heads),
        out_shape=jax.ShapeDtypeStruct((slots, channels, rows), jnp.float32),
        in_specs=[wide(a) for a in (queries, fresh_k, fresh_v, stale_k, stale_v, hot_k, hot_v)]
        + [
            packed,
            packed,
            pl.BlockSpec((channels, HD), lambda s, h: (0, h)),
            pl.BlockSpec((1, key_rows, 1), lambda s, h: (s, 0, 0)),
        ],
        out_specs=pl.BlockSpec((1, channels, rows), lambda s, h: (s, 0, 0)),
        scratch_shapes=[pltpu.VMEM((key_rows, rows), jnp.float32)],
        cost_estimate=pl.CostEstimate(
            flops=2 * many * (HD + channels), bytes_accessed=24 * 1024 * 1024, transcendentals=many
        ),
        compiler_params=pltpu.CompilerParams(vmem_limit_bytes=VMEM_LIMIT),
        name="attention",
    )(queries, fresh_k, fresh_v, stale_k, stale_v, hot_k, hot_v, text_own, text_other, w_t, bias)


def shards(
    queries,
    fresh_kv,
    stale_kv,
    text_kv,
    w_velocity,
    latent,
    live_counts,
    refresh_rows,
    request_list,
    timesteps,
):
    half_groups = lax.axis_size("grp") // 2
    my_group = lax.axis_index("grp")
    partner = (my_group + half_groups) % (2 * half_groups)
    queries, fresh, stale, text = queries[0], fresh_kv[0], stale_kv[0], text_kv[0]
    slots, img_rows = queries.shape[:2]
    listed_count = refresh_rows.shape[2]
    hot_rows = 2 * listed_count
    last_rows = 128
    split = img_rows - last_rows
    both = tuple(range(slots))

    raw = fresh[:, :listed_count]
    raw_in = from_behind(raw, "grp", half_groups)

    w_t = w_velocity.T
    text_own = project_text(text[:, :, 0], text[:, :, 1], w_t)

    my_list = lax.dynamic_index_in_dim(refresh_rows, my_group, 0, keepdims=False)
    partner_list = lax.dynamic_index_in_dim(refresh_rows, partner, 0, keepdims=False)
    orders = send_order(jnp.stack([my_list, partner_list]), img_rows)
    my_order, partner_order = orders[0].reshape(-1), orders[1].reshape(-1)

    zone = pick_rows(my_order, fresh, both, listed_count, listed_count)
    zone_in = from_behind(zone, "grp", half_groups)
    text_in = from_behind(text_own, "grp", half_groups)
    pieces = [(both[:-1], hot_rows, img_rows - hot_rows), (both[-1:], hot_rows, split - hot_rows)]
    early = pick_rows(my_order, fresh, *pieces[0], after=(zone_in,))
    early_in = from_behind(early, "grp", half_groups)
    late = pick_rows(my_order, fresh, *pieces[1], after=(text_in,))
    late_in = from_behind(late, "grp", half_groups)
    last_piece = (both[-1:], split, last_rows)
    last = pick_rows(my_order, fresh, *last_piece, after=(early_in,))
    last_in = from_behind(last, "grp", half_groups)

    my_live = lax.dynamic_index_in_dim(live_counts, my_group, 0, keepdims=False)
    partner_live = lax.dynamic_index_in_dim(live_counts, partner, 0, keepdims=False)
    row_ids = jnp.arange(img_rows, dtype=jnp.int32)
    hot_source = orders[1][:, :hot_rows]
    stale_listed = jnp.any(partner_list[:, :, None] == row_ids, axis=1)
    hot_listed = jnp.any(partner_list[:, :, None] == hot_source[:, None, :], axis=1)
    live = jnp.concatenate(
        [
            row_ids < my_live[:, None],
            (row_ids < partner_live[:, None]) & jnp.logical_not(stale_listed),
            (hot_source < partner_live[:, None]) & hot_listed,
            jnp.ones((slots, 2 * text.shape[1]), dtype=bool),
        ],
        axis=1,
    )
    bias = jnp.where(live, 0.0, -jnp.inf).astype(jnp.float32)[:, :, None]
    hot = jnp.concatenate([raw_in, zone_in], axis=1)
    partial = attention(
        queries,
        fresh[:, :, 0],
        fresh[:, :, 1],
        stale[:, :, 0],
        stale[:, :, 1],
        hot[:, :, 0],
        hot[:, :, 1],
        text_own,
        text_in,
        w_t,
        bias,
    )

    tp_count = lax.axis_size("tp")
    tp_index = lax.axis_index("tp")
    share = img_rows // tp_count
    if tp_count == 2:
        mine = lax.dynamic_slice_in_dim(partial, tp_index * share, share, 2)
        theirs = lax.dynamic_slice_in_dim(partial, (1 - tp_index) * share, share, 2)
        summed = mine + from_behind(theirs, "tp", 1)
    else:
        summed = lax.psum_scatter(partial, "tp", scatter_dimension=2, tiled=True)
    summed = jnp.swapaxes(summed, 1, 2)
    share_ids = tp_index * share + jnp.arange(share, dtype=jnp.int32)
    live_rows = share_ids[None, :] < my_live[:, None]
    velocity = jnp.where(live_rows[:, :, None], summed, 0.0)
    pair_index = my_group % half_groups
    request_ids = lax.dynamic_slice_in_dim(request_list, pair_index * slots, slots)
    matches = (
        request_ids[:, None] == jnp.arange(timesteps.shape[0], dtype=jnp.int32)[None, :]
    ).astype(jnp.int32)
    times = jnp.sum(matches[:, :, None] * timesteps[None], axis=1)
    step_size = (times[:, 1] - times[:, 0]).astype(jnp.float32) / 1000.0
    latent_next = latent[0] + step_size[:, None, None] * velocity

    next_stale = place_rows(
        partner_order,
        (raw_in, zone_in, early_in, late_in),
        [(both, 0, listed_count), (both, listed_count, listed_count)] + pieces,
        fresh.shape,
    )
    next_stale = place_rows(partner_order, (last_in,), [last_piece], fresh.shape, whole=next_stale)
    return (next_stale[None], velocity[None], latent_next[None])


def solution(mesh):
    return jax.shard_map(
        shards,
        mesh=mesh,
        in_specs=(
            P("grp", None, None, "tp"),
            P("grp", None, None, None, "tp"),
            P("grp", None, None, None, "tp"),
            P("grp", None, None, None, "tp"),
            P("tp", None),
            P("grp", None, "tp", None),
            P(),
            P(),
            P(),
            P(),
        ),
        out_specs=(
            P("grp", None, None, None, "tp"),
            P("grp", None, "tp", None),
            P("grp", None, "tp", None),
        ),
        check_vma=False,
    )
```

```python
import functools
import math

import jax
import jax.numpy as jnp
from jax import lax
from jax.experimental import pallas as pl
from jax.experimental.pallas import tpu as pltpu
from jax.sharding import PartitionSpec as P

HD = 128
HBM = pltpu.MemorySpace.HBM
SMEM = pltpu.MemorySpace.SMEM
VMEM_LIMIT = 32 * 1024 * 1024


def from_behind(block, axis, distance):
    devices = range(lax.axis_size(axis))
    route = [((i - distance) % len(devices), i) for i in devices]
    return lax.ppermute(block, axis, route)


def swap_places(lists):
    count = lists.shape[2]
    zone = count + jnp.arange(count, dtype=jnp.int32)
    order = jnp.arange(count, dtype=jnp.int32)
    earlier = order[:, None] >= order[None, :]
    free = jnp.logical_not(jnp.any(lists[..., :, None] == zone, axis=2))
    outside = lists >= 2 * count
    free_rank = jnp.sum((earlier & free[..., None, :]).astype(jnp.int32), axis=3)
    outside_rank = jnp.sum((earlier & outside[..., None, :]).astype(jnp.int32), axis=3)
    match = (
        outside[..., :, None]
        & free[..., None, :]
        & (outside_rank[..., :, None] == free_rank[..., None, :])
    )
    places = jnp.sum(jnp.where(match, zone, 0), axis=3)
    sources = jnp.sum(jnp.where(match, lists[..., :, None], 0), axis=2)
    return places, jnp.where(sources > 0, sources, zone)


def swap_rows(list_ref, place_ref, slot, zone_ref, rest_ref):
    count = zone_ref.shape[0]

    def step(k, carry):
        place = place_ref[slot * count + k]

        @pl.when(place > 0)
        def _():
            near = place - count
            far = list_ref[slot * count + k] - 2 * count
            moved = zone_ref[near]
            zone_ref[near] = rest_ref[far]
            rest_ref[far] = moved

        return carry

    lax.fori_loop(0, count, step, 0)


def arrange_kernel(slots, list_ref, place_ref, fresh_ref, *refs):
    zone_out, rest_outs = refs[1], refs[2 : 2 + slots]
    zones, rests, sems = refs[2 + slots :]
    count = zones.shape[1]
    copies_in = []
    for slot in range(slots):
        copies_in.append(
            (
                pltpu.make_async_copy(fresh_ref.at[slot, count : 2 * count], zones.at[slot], sems.at[slot, 0]),
                pltpu.make_async_copy(fresh_ref.at[slot, 2 * count :], rests.at[slot], sems.at[slot, 1]),
            )
        )
        for copy in copies_in[-1]:
            copy.start()
    copies_out = []
    for slot in range(slots):
        for copy in copies_in[slot]:
            copy.wait()
        swap_rows(list_ref, place_ref, slot, zones.at[slot], rests.at[slot])
        copies_out.append(pltpu.make_async_copy(zones.at[slot], zone_out.at[slot], sems.at[slot, 2]))
        copies_out[-1].start()
        copies_out.append(pltpu.make_async_copy(rests.at[slot], rest_outs[slot], sems.at[slot, 3]))
        copies_out[-1].start()
    for copy in copies_out:
        copy.wait()


def arrange(lists, places, fresh, after):
    slots, rows = fresh.shape[:2]
    tail = fresh.shape[2:]
    count = lists.shape[0] // slots
    outs = pl.pallas_call(
        functools.partial(arrange_kernel, slots),
        out_shape=[jax.ShapeDtypeStruct((slots, count) + tail, fresh.dtype)]
        + [jax.ShapeDtypeStruct((rows - 2 * count,) + tail, fresh.dtype)] * slots,
        in_specs=[pl.BlockSpec(memory_space=SMEM)] * 2 + [pl.BlockSpec(memory_space=HBM)] * 2,
        out_specs=[pl.BlockSpec(memory_space=HBM)] * (1 + slots),
        scratch_shapes=[
            pltpu.VMEM((slots, count) + tail, fresh.dtype),
            pltpu.VMEM((slots, rows - 2 * count) + tail, fresh.dtype),
            pltpu.SemaphoreType.DMA((slots, 4)),
        ],
        cost_estimate=pl.CostEstimate(flops=0, bytes_accessed=4 * fresh.size, transcendentals=0),
        compiler_params=pltpu.CompilerParams(vmem_limit_bytes=VMEM_LIMIT),
        name="arrange",
    )(lists, places, fresh, after)
    return outs[0], outs[1:]


def restore_kernel(slot, heads, list_ref, place_ref, raw_ref, zone_ref, rest_ref, *refs):
    out_ref, zone, rest, sems = refs[-4:]
    count = zone.shape[0]
    copies = [pltpu.make_async_copy(raw_ref.at[s], out_ref.at[s, :count], sems.at[4 + s]) for s in heads]
    copy_zone = pltpu.make_async_copy(zone_ref.at[slot], zone, sems.at[0])
    copy_rest = pltpu.make_async_copy(rest_ref, rest, sems.at[1])
    copy_zone.start()
    copy_rest.start()
    for copy in copies:
        copy.start()
    copy_zone.wait()
    copy_rest.wait()
    swap_rows(list_ref, place_ref, slot, zone, rest)
    copies.append(pltpu.make_async_copy(zone, out_ref.at[slot, count : 2 * count], sems.at[2]))
    copies[-1].start()
    copies.append(pltpu.make_async_copy(rest, out_ref.at[slot, 2 * count :], sems.at[3]))
    copies[-1].start()
    for copy in copies:
        copy.wait()


def restore(lists, places, raw, zone, rest, slot, shape, whole=None):
    tail = shape[2:]
    count = zone.shape[1]
    extra = () if whole is None else (whole,)
    heads = range(shape[0]) if whole is None else ()
    return pl.pallas_call(
        functools.partial(restore_kernel, slot, heads),
        out_shape=jax.ShapeDtypeStruct(shape, rest.dtype),
        in_specs=[pl.BlockSpec(memory_space=SMEM)] * 2 + [pl.BlockSpec(memory_space=HBM)] * (3 + len(extra)),
        out_specs=pl.BlockSpec(memory_space=HBM),
        scratch_shapes=[
            pltpu.VMEM((count,) + tail, rest.dtype),
            pltpu.VMEM(rest.shape, rest.dtype),
            pltpu.SemaphoreType.DMA((4 + shape[0],)),
        ],
        input_output_aliases={} if whole is None else {5: 0},
        cost_estimate=pl.CostEstimate(flops=0, bytes_accessed=4 * rest.size, transcendentals=0),
        compiler_params=pltpu.CompilerParams(vmem_limit_bytes=VMEM_LIMIT),
        name="restore",
    )(lists, places, raw, zone, rest, *extra)


def hold_kernel(block_ref, after_ref, out_ref):
    del block_ref, after_ref, out_ref


def hold(block, after):
    return pl.pallas_call(
        hold_kernel,
        out_shape=jax.ShapeDtypeStruct(block.shape, block.dtype),
        in_specs=[pl.BlockSpec(memory_space=HBM)] * 2,
        out_specs=pl.BlockSpec(memory_space=HBM),
        input_output_aliases={0: 0},
        cost_estimate=pl.CostEstimate(flops=0, bytes_accessed=0, transcendentals=0),
        name="hold",
    )(block, after)


def across(a, b):
    return lax.dot_general(a, b, (((1,), (1,)), ((), ())), preferred_element_type=jnp.float32)


def text_kernel(k_ref, v_ref, w_ref, after_ref, out_ref):
    rows = k_ref.shape[1]
    channels = w_ref.shape[0]
    out_ref[0, 0, :rows, :] = k_ref[0]
    projected = across(w_ref[...], v_ref[0]).astype(out_ref.dtype)
    for part in range(rows // HD):
        start = rows + part * channels
        out_ref[0, 0, start : start + channels, :] = projected[:, part * HD : (part + 1) * HD]


def project_text(keys, values, w_t, after):
    slots, rows, width = keys.shape
    heads = width // HD
    channels = w_t.shape[0]
    packed = rows + channels * rows // HD
    block = pl.BlockSpec((1, rows, HD), lambda s, h: (s, 0, h))
    return pl.pallas_call(
        text_kernel,
        grid=(slots, heads),
        out_shape=jax.ShapeDtypeStruct((slots, heads, packed, HD), keys.dtype),
        in_specs=[block, block, pl.BlockSpec((channels, HD), lambda s, h: (0, h)), pl.BlockSpec(memory_space=HBM)],
        out_specs=pl.BlockSpec((1, 1, packed, HD), lambda s, h: (s, h, 0, 0)),
        cost_estimate=pl.CostEstimate(
            flops=2 * slots * rows * width * channels, bytes_accessed=4 * keys.size * 2, transcendentals=0
        ),
        name="project_text",
    )(keys, values, w_t, after)


def attention_kernel(text_rows, *refs):
    (q_ref, kf_ref, vf_ref, ks_ref, vs_ref, kh_ref, vh_ref, own_ref, other_ref, w_ref, bias_ref) = refs[:11]
    out_ref, scores_ref = refs[11], refs[12]
    head = pl.program_id(1)
    query = q_ref[0]
    w_t = w_ref[...]
    channels = w_t.shape[0]
    scale = 1.0 / math.sqrt(HD)
    pieces = []
    for k_ref, v_ref in ((kf_ref, vf_ref), (ks_ref, vs_ref), (kh_ref, vh_ref)):
        rows = k_ref.shape[1]
        step = min(rows, 256)
        for start in range(0, rows, step):
            pieces.append((k_ref.at[0, start : start + step], v_ref.at[0, start : start + step], step))
    for t_ref in (own_ref, other_ref):
        pieces.append((t_ref.at[0, 0, :text_rows], t_ref, text_rows))
    top = None
    at = 0
    for k_ref, _, rows in pieces:
        scores = across(k_ref[...], query) * scale + bias_ref[0, at : at + rows]
        scores_ref[at : at + rows, :] = scores
        piece_top = jnp.max(scores, axis=0, keepdims=True)
        top = piece_top if top is None else jnp.maximum(top, piece_top)
        at += rows
    total = jnp.zeros_like(top)
    blended = jnp.zeros((channels, query.shape[0]), jnp.float32)
    at = 0
    for _, v_ref, rows in pieces:
        weights = jnp.exp(scores_ref[at : at + rows, :] - top)
        total += jnp.sum(weights, axis=0, keepdims=True)
        rounded = weights.astype(jnp.bfloat16)
        if v_ref.shape[-2] == rows and len(v_ref.shape) == 2:
            projected = across(w_t, v_ref[...]).astype(jnp.bfloat16)
            blended += jnp.dot(projected, rounded, preferred_element_type=jnp.float32)
        else:
            for part in range(rows // HD):
                start = rows + part * channels
                blended += jnp.dot(
                    v_ref[0, 0, start : start + channels, :],
                    rounded[part * HD : (part + 1) * HD],
                    preferred_element_type=jnp.float32,
                )
        at += rows
    term = blended / total

    @pl.when(head == 0)
    def _():
        out_ref[0] = term

    @pl.when(head != 0)
    def _():
        out_ref[0] += term


def attention(queries, fresh_k, fresh_v, stale_k, stale_v, hot_k, hot_v, text_own, text_other, w_t, bias):
    slots, rows, width = queries.shape
    heads = width // HD
    channels = w_t.shape[0]
    key_rows = bias.shape[1]
    text_rows = (text_own.shape[2] * HD) // (HD + channels)

    def wide(array):
        return pl.BlockSpec((1, array.shape[1], HD), lambda s, h: (s, 0, h))

    packed = pl.BlockSpec((1, 1) + text_own.shape[2:], lambda s, h: (s, h, 0, 0))
    many = slots * heads * rows * key_rows
    return pl.pallas_call(
        functools.partial(attention_kernel, text_rows),
        grid=(slots, heads),
        out_shape=jax.ShapeDtypeStruct((slots, channels, rows), jnp.float32),
        in_specs=[wide(a) for a in (queries, fresh_k, fresh_v, stale_k, stale_v, hot_k, hot_v)]
        + [
            packed,
            packed,
            pl.BlockSpec((channels, HD), lambda s, h: (0, h)),
            pl.BlockSpec((1, key_rows, 1), lambda s, h: (s, 0, 0)),
        ],
        out_specs=pl.BlockSpec((1, channels, rows), lambda s, h: (s, 0, 0)),
        scratch_shapes=[pltpu.VMEM((key_rows, rows), jnp.float32)],
        cost_estimate=pl.CostEstimate(
            flops=2 * many * (HD + channels), bytes_accessed=24 * 1024 * 1024, transcendentals=many
        ),
        compiler_params=pltpu.CompilerParams(vmem_limit_bytes=VMEM_LIMIT),
        name="attention",
    )(queries, fresh_k, fresh_v, stale_k, stale_v, hot_k, hot_v, text_own, text_other, w_t, bias)


def shards(
    queries,
    fresh_kv,
    stale_kv,
    text_kv,
    w_velocity,
    latent,
    live_counts,
    refresh_rows,
    request_list,
    timesteps,
):
    half_groups = lax.axis_size("grp") // 2
    my_group = lax.axis_index("grp")
    partner = (my_group + half_groups) % (2 * half_groups)
    queries, fresh, stale, text = queries[0], fresh_kv[0], stale_kv[0], text_kv[0]
    slots, img_rows = queries.shape[:2]
    listed_count = refresh_rows.shape[2]

    raw = fresh[:, :listed_count]
    raw_in = from_behind(raw, "grp", half_groups)

    my_list = lax.dynamic_index_in_dim(refresh_rows, my_group, 0, keepdims=False)
    partner_list = lax.dynamic_index_in_dim(refresh_rows, partner, 0, keepdims=False)
    places, sources = swap_places(jnp.stack([my_list, partner_list]))
    mine = (my_list.reshape(-1), places[0].reshape(-1))
    partners = (partner_list.reshape(-1), places[1].reshape(-1))

    zone, rests = arrange(*mine, fresh, raw)
    zone_in = from_behind(zone, "grp", half_groups)
    w_t = w_velocity.T
    text_own = project_text(text[:, :, 0], text[:, :, 1], w_t, raw)
    text_in = from_behind(text_own, "grp", half_groups)
    gates = [raw_in] * (slots - 1) + [text_in]
    rests_in = [from_behind(hold(rest, gate), "grp", half_groups) for rest, gate in zip(rests, gates)]

    my_live = lax.dynamic_index_in_dim(live_counts, my_group, 0, keepdims=False)
    partner_live = lax.dynamic_index_in_dim(live_counts, partner, 0, keepdims=False)
    row_ids = jnp.arange(img_rows, dtype=jnp.int32)
    hot_source = jnp.concatenate(
        [jnp.broadcast_to(row_ids[:listed_count], partner_list.shape), sources[1]], axis=1
    )
    stale_listed = jnp.any(partner_list[:, :, None] == row_ids, axis=1)
    hot_listed = jnp.any(partner_list[:, :, None] == hot_source[:, None, :], axis=1)
    live = jnp.concatenate(
        [
            row_ids < my_live[:, None],
            (row_ids < partner_live[:, None]) & jnp.logical_not(stale_listed),
            (hot_source < partner_live[:, None]) & hot_listed,
            jnp.ones((slots, 2 * text.shape[1]), dtype=bool),
        ],
        axis=1,
    )
    bias = jnp.where(live, 0.0, -jnp.inf).astype(jnp.float32)[:, :, None]
    hot = jnp.concatenate([raw_in, zone_in], axis=1)
    partial = attention(
        queries,
        fresh[:, :, 0],
        fresh[:, :, 1],
        stale[:, :, 0],
        stale[:, :, 1],
        hot[:, :, 0],
        hot[:, :, 1],
        text_own,
        text_in,
        w_t,
        bias,
    )

    tp_count = lax.axis_size("tp")
    tp_index = lax.axis_index("tp")
    share = img_rows // tp_count
    if tp_count == 2:
        mine = lax.dynamic_slice_in_dim(partial, tp_index * share, share, 2)
        theirs = lax.dynamic_slice_in_dim(partial, (1 - tp_index) * share, share, 2)
        summed = mine + from_behind(theirs, "tp", 1)
    else:
        summed = lax.psum_scatter(partial, "tp", scatter_dimension=2, tiled=True)
    summed = jnp.swapaxes(summed, 1, 2)
    share_ids = tp_index * share + jnp.arange(share, dtype=jnp.int32)
    live_rows = share_ids[None, :] < my_live[:, None]
    velocity = jnp.where(live_rows[:, :, None], summed, 0.0)
    pair_index = my_group % half_groups
    request_ids = lax.dynamic_slice_in_dim(request_list, pair_index * slots, slots)
    matches = (
        request_ids[:, None] == jnp.arange(timesteps.shape[0], dtype=jnp.int32)[None, :]
    ).astype(jnp.int32)
    times = jnp.sum(matches[:, :, None] * timesteps[None], axis=1)
    step_size = (times[:, 1] - times[:, 0]).astype(jnp.float32) / 1000.0
    latent_next = latent[0] + step_size[:, None, None] * velocity

    next_stale = None
    for slot in range(slots):
        next_stale = restore(*partners, raw_in, zone_in, rests_in[slot], slot, fresh.shape, whole=next_stale)
    return (next_stale[None], velocity[None], latent_next[None])


def solution(mesh):
    return jax.shard_map(
        shards,
        mesh=mesh,
        in_specs=(
            P("grp", None, None, "tp"),
            P("grp", None, None, None, "tp"),
            P("grp", None, None, None, "tp"),
            P("grp", None, None, None, "tp"),
            P("tp", None),
            P("grp", None, "tp", None),
            P(),
            P(),
            P(),
            P(),
        ),
        out_specs=(
            P("grp", None, None, None, "tp"),
            P("grp", None, "tp", None),
            P("grp", None, "tp", None),
        ),
        check_vma=False,
    )
```

```python
import functools
import math

import jax
import jax.numpy as jnp
from jax import lax
from jax.experimental import pallas as pl
from jax.experimental.pallas import tpu as pltpu
from jax.sharding import PartitionSpec as P

HD = 128
HBM = pltpu.MemorySpace.HBM
SMEM = pltpu.MemorySpace.SMEM
VMEM_LIMIT = 32 * 1024 * 1024
WIDE_LIMIT = 60 * 1024 * 1024


def from_behind(block, axis, distance):
    devices = range(lax.axis_size(axis))
    route = [((i - distance) % len(devices), i) for i in devices]
    return lax.ppermute(block, axis, route)


def swap_pairs(lists):
    count = lists.shape[2]
    zone = count + jnp.arange(count, dtype=jnp.int32)
    order = jnp.arange(count, dtype=jnp.int32)
    earlier = order[:, None] >= order[None, :]
    free = jnp.logical_not(jnp.any(lists[..., :, None] == zone, axis=2))
    outside = lists >= 2 * count
    free_rank = jnp.sum((earlier & free[..., None, :]).astype(jnp.int32), axis=3)
    outside_rank = jnp.sum((earlier & outside[..., None, :]).astype(jnp.int32), axis=3)
    match = (
        outside[..., :, None]
        & free[..., None, :]
        & (outside_rank[..., :, None] == free_rank[..., None, :])
    )
    near = jnp.sum(jnp.where(match, order, 0), axis=3)
    sources = jnp.sum(jnp.where(match, lists[..., :, None], 0), axis=2)
    return near, jnp.where(outside, lists, -1), jnp.where(sources > 0, sources, zone)


def swap_rows(near_ref, far_ref, slot, zone, piece, start, stop):
    count = zone.shape[0] - 1

    def step(k, carry):
        far = far_ref[slot * count + k]
        here = jnp.logical_and(far >= start, far < stop)
        near_row = jnp.where(here, near_ref[slot * count + k], count)
        far_row = jnp.where(here, far - start, stop - start)
        moved = zone[near_row]
        zone[near_row] = piece[far_row]
        piece[far_row] = moved
        return carry

    lax.fori_loop(0, count, step, 0, unroll=8)


def take_kernel(fresh_ref, out_ref, sem):
    copy = pltpu.make_async_copy(fresh_ref.at[0, :, : out_ref.shape[1]], out_ref, sem)
    copy.start()
    copy.wait()


def take_head(fresh_kv, rows):
    shape = (fresh_kv.shape[1], rows) + fresh_kv.shape[3:]
    return pl.pallas_call(
        take_kernel,
        out_shape=jax.ShapeDtypeStruct(shape, fresh_kv.dtype),
        in_specs=[pl.BlockSpec(memory_space=HBM)],
        out_specs=pl.BlockSpec(memory_space=HBM),
        scratch_shapes=[pltpu.SemaphoreType.DMA],
        cost_estimate=pl.CostEstimate(flops=0, bytes_accessed=4 * math.prod(shape), transcendentals=0),
        compiler_params=pltpu.CompilerParams(vmem_limit_bytes=WIDE_LIMIT),
        name="take_head",
    )(fresh_kv)


def arrange_kernel(slots, pieces, near_ref, far_ref, fresh_ref, after_ref, *refs):
    zone_out, piece_outs = refs[0], refs[1 : 1 + len(pieces)]
    zones, rests, sems = refs[1 + len(pieces) :]
    count = zones.shape[1] - 1
    rest_rows = rests.shape[1] - 1
    copies_in = []
    for slot in range(slots):
        copies_in.append(
            (
                pltpu.make_async_copy(
                    fresh_ref.at[0, slot, count : 2 * count], zones.at[slot, :count], sems.at[slot]
                ),
                pltpu.make_async_copy(
                    fresh_ref.at[0, slot, 2 * count :], rests.at[slot, :rest_rows], sems.at[slots + slot]
                ),
            )
        )
        for copy in copies_in[-1]:
            copy.start()
    copies_out = []
    for slot in range(slots):
        for copy in copies_in[slot]:
            copy.wait()
        swap_rows(
            near_ref, far_ref, slot, zones.at[slot], rests.at[slot], 2 * count, 2 * count + rest_rows
        )
        copies_out.append(
            pltpu.make_async_copy(zones.at[slot, :count], zone_out.at[slot], sems.at[2 * slots + slot])
        )
        copies_out[-1].start()
        for index, (piece_slot, start, stop) in enumerate(pieces):
            if piece_slot == slot:
                source = rests.at[slot, start - 2 * count : stop - 2 * count]
                copies_out.append(
                    pltpu.make_async_copy(source, piece_outs[index], sems.at[3 * slots + index])
                )
                copies_out[-1].start()
    for copy in copies_out:
        copy.wait()


def arrange(near, far, fresh_kv, pieces, after):
    slots, rows = fresh_kv.shape[1:3]
    tail = fresh_kv.shape[3:]
    count = near.shape[0] // slots
    outs = pl.pallas_call(
        functools.partial(arrange_kernel, slots, pieces),
        out_shape=[jax.ShapeDtypeStruct((slots, count) + tail, fresh_kv.dtype)]
        + [jax.ShapeDtypeStruct((stop - start,) + tail, fresh_kv.dtype) for _, start, stop in pieces],
        in_specs=[pl.BlockSpec(memory_space=SMEM)] * 2 + [pl.BlockSpec(memory_space=HBM)] * 2,
        out_specs=[pl.BlockSpec(memory_space=HBM)] * (1 + len(pieces)),
        scratch_shapes=[
            pltpu.VMEM((slots, count + 1) + tail, fresh_kv.dtype),
            pltpu.VMEM((slots, rows - 2 * count + 1) + tail, fresh_kv.dtype),
            pltpu.SemaphoreType.DMA((3 * slots + len(pieces),)),
        ],
        cost_estimate=pl.CostEstimate(flops=0, bytes_accessed=4 * fresh_kv.size, transcendentals=0),
        compiler_params=pltpu.CompilerParams(vmem_limit_bytes=WIDE_LIMIT),
        name="arrange",
    )(near, far, fresh_kv, after)
    return outs[0], outs[1:]


def join_kernel(raw_ref, zone_ref, out_ref, sems):
    count = raw_ref.shape[1]
    copies = [
        pltpu.make_async_copy(raw_ref, out_ref.at[:, :count], sems.at[0]),
        pltpu.make_async_copy(zone_ref, out_ref.at[:, count : 2 * count], sems.at[1]),
    ]
    for copy in copies:
        copy.start()
    for copy in copies:
        copy.wait()


def join_head(raw, zone, shape):
    return pl.pallas_call(
        join_kernel,
        out_shape=jax.ShapeDtypeStruct(shape, raw.dtype),
        in_specs=[pl.BlockSpec(memory_space=HBM)] * 2,
        out_specs=pl.BlockSpec(memory_space=HBM),
        scratch_shapes=[pltpu.SemaphoreType.DMA((2,))],
        cost_estimate=pl.CostEstimate(flops=0, bytes_accessed=8 * raw.size, transcendentals=0),
        name="join_head",
    )(raw, zone)


def restore_kernel(slot, start, stop, near_ref, far_ref, piece_ref, whole_ref, *refs):
    out_ref, zone, piece, sems = refs[-4:]
    count = zone.shape[0] - 1
    inner = [
        pltpu.make_async_copy(piece_ref, piece.at[: stop - start], sems.at[0]),
        pltpu.make_async_copy(out_ref.at[slot, count : 2 * count], zone.at[:count], sems.at[1]),
    ]
    for copy in inner:
        copy.start()
    for copy in inner:
        copy.wait()
    swap_rows(near_ref, far_ref, slot, zone, piece, start, stop)
    outer = [
        pltpu.make_async_copy(piece.at[: stop - start], out_ref.at[slot, start:stop], sems.at[2]),
        pltpu.make_async_copy(zone.at[:count], out_ref.at[slot, count : 2 * count], sems.at[3]),
    ]
    for copy in outer:
        copy.start()
    for copy in outer:
        copy.wait()


def restore(near, far, block, whole, piece, after=()):
    slot, start, stop = piece
    tail = whole.shape[2:]
    count = near.shape[0] // whole.shape[0]
    return pl.pallas_call(
        functools.partial(restore_kernel, slot, start, stop),
        out_shape=jax.ShapeDtypeStruct(whole.shape, whole.dtype),
        in_specs=[pl.BlockSpec(memory_space=SMEM)] * 2 + [pl.BlockSpec(memory_space=HBM)] * (2 + len(after)),
        out_specs=pl.BlockSpec(memory_space=HBM),
        scratch_shapes=[
            pltpu.VMEM((count + 1,) + tail, whole.dtype),
            pltpu.VMEM((stop - start + 1,) + tail, whole.dtype),
            pltpu.SemaphoreType.DMA((4,)),
        ],
        input_output_aliases={3: 0},
        cost_estimate=pl.CostEstimate(flops=0, bytes_accessed=4 * block.size, transcendentals=0),
        compiler_params=pltpu.CompilerParams(vmem_limit_bytes=VMEM_LIMIT),
        name="restore",
    )(near, far, block, whole, *after)


def hold_kernel(block_ref, after_ref, out_ref):
    del block_ref, after_ref, out_ref


def hold(block, after):
    return pl.pallas_call(
        hold_kernel,
        out_shape=jax.ShapeDtypeStruct(block.shape, block.dtype),
        in_specs=[pl.BlockSpec(memory_space=HBM)] * 2,
        out_specs=pl.BlockSpec(memory_space=HBM),
        input_output_aliases={0: 0},
        cost_estimate=pl.CostEstimate(flops=0, bytes_accessed=0, transcendentals=0),
        name="hold",
    )(block, after)


def across(a, b):
    return lax.dot_general(a, b, (((1,), (1,)), ((), ())), preferred_element_type=jnp.float32)


def text_kernel(k_ref, v_ref, w_ref, after_ref, out_ref):
    rows = k_ref.shape[1]
    channels = w_ref.shape[0]
    out_ref[0, 0, :rows, :] = k_ref[0]
    projected = across(w_ref[...], v_ref[0]).astype(out_ref.dtype)
    for part in range(rows // HD):
        start = rows + part * channels
        out_ref[0, 0, start : start + channels, :] = projected[:, part * HD : (part + 1) * HD]


def project_text(keys, values, w_t, after):
    slots, rows, width = keys.shape
    heads = width // HD
    channels = w_t.shape[0]
    packed = rows + channels * rows // HD
    block = pl.BlockSpec((1, rows, HD), lambda s, h: (s, 0, h))
    return pl.pallas_call(
        text_kernel,
        grid=(slots, heads),
        out_shape=jax.ShapeDtypeStruct((slots, heads, packed, HD), keys.dtype),
        in_specs=[block, block, pl.BlockSpec((channels, HD), lambda s, h: (0, h)), pl.BlockSpec(memory_space=HBM)],
        out_specs=pl.BlockSpec((1, 1, packed, HD), lambda s, h: (s, h, 0, 0)),
        cost_estimate=pl.CostEstimate(
            flops=2 * slots * rows * width * channels, bytes_accessed=4 * keys.size * 2, transcendentals=0
        ),
        name="project_text",
    )(keys, values, w_t, after)


def attention_kernel(text_rows, *refs):
    (q_ref, kf_ref, vf_ref, ks_ref, vs_ref, kh_ref, vh_ref, own_ref, other_ref, w_ref, bias_ref) = refs[:11]
    out_ref, scores_ref = refs[11], refs[12]
    head = pl.program_id(1)
    query = q_ref[0]
    w_t = w_ref[...]
    channels = w_t.shape[0]
    scale = 1.0 / math.sqrt(HD)
    pieces = []
    for k_ref, v_ref in ((kf_ref, vf_ref), (ks_ref, vs_ref), (kh_ref, vh_ref)):
        rows = k_ref.shape[1]
        step = min(rows, 256)
        for start in range(0, rows, step):
            pieces.append((k_ref.at[0, start : start + step], v_ref.at[0, start : start + step], step))
    for t_ref in (own_ref, other_ref):
        pieces.append((t_ref.at[0, 0, :text_rows], t_ref, text_rows))
    top = None
    at = 0
    for k_ref, _, rows in pieces:
        scores = across(k_ref[...], query) * scale + bias_ref[0, at : at + rows]
        scores_ref[at : at + rows, :] = scores
        piece_top = jnp.max(scores, axis=0, keepdims=True)
        top = piece_top if top is None else jnp.maximum(top, piece_top)
        at += rows
    total = jnp.zeros_like(top)
    blended = jnp.zeros((channels, query.shape[0]), jnp.float32)
    at = 0
    for _, v_ref, rows in pieces:
        weights = jnp.exp(scores_ref[at : at + rows, :] - top)
        total += jnp.sum(weights, axis=0, keepdims=True)
        rounded = weights.astype(jnp.bfloat16)
        if v_ref.shape[-2] == rows and len(v_ref.shape) == 2:
            projected = across(w_t, v_ref[...]).astype(jnp.bfloat16)
            blended += jnp.dot(projected, rounded, preferred_element_type=jnp.float32)
        else:
            for part in range(rows // HD):
                start = rows + part * channels
                blended += jnp.dot(
                    v_ref[0, 0, start : start + channels, :],
                    rounded[part * HD : (part + 1) * HD],
                    preferred_element_type=jnp.float32,
                )
        at += rows
    term = blended / total

    @pl.when(head == 0)
    def _():
        out_ref[0] = term

    @pl.when(head != 0)
    def _():
        out_ref[0] += term


def attention(queries, fresh_k, fresh_v, stale_k, stale_v, hot_k, hot_v, text_own, text_other, w_t, bias):
    slots, rows, width = queries.shape
    heads = width // HD
    channels = w_t.shape[0]
    key_rows = bias.shape[1]
    text_rows = (text_own.shape[2] * HD) // (HD + channels)

    def wide(array):
        return pl.BlockSpec((1, array.shape[1], HD), lambda s, h: (s, 0, h))

    packed = pl.BlockSpec((1, 1) + text_own.shape[2:], lambda s, h: (s, h, 0, 0))
    many = slots * heads * rows * key_rows
    return pl.pallas_call(
        functools.partial(attention_kernel, text_rows),
        grid=(slots, heads),
        out_shape=jax.ShapeDtypeStruct((slots, channels, rows), jnp.float32),
        in_specs=[wide(a) for a in (queries, fresh_k, fresh_v, stale_k, stale_v, hot_k, hot_v)]
        + [
            packed,
            packed,
            pl.BlockSpec((channels, HD), lambda s, h: (0, h)),
            pl.BlockSpec((1, key_rows, 1), lambda s, h: (s, 0, 0)),
        ],
        out_specs=pl.BlockSpec((1, channels, rows), lambda s, h: (s, 0, 0)),
        scratch_shapes=[pltpu.VMEM((key_rows, rows), jnp.float32)],
        cost_estimate=pl.CostEstimate(
            flops=2 * many * (HD + channels), bytes_accessed=24 * 1024 * 1024, transcendentals=many
        ),
        compiler_params=pltpu.CompilerParams(vmem_limit_bytes=VMEM_LIMIT),
        name="attention",
    )(queries, fresh_k, fresh_v, stale_k, stale_v, hot_k, hot_v, text_own, text_other, w_t, bias)


def shards(
    queries,
    fresh_kv,
    stale_kv,
    text_kv,
    w_velocity,
    latent,
    live_counts,
    refresh_rows,
    request_list,
    timesteps,
):
    half_groups = lax.axis_size("grp") // 2
    my_group = lax.axis_index("grp")
    partner = (my_group + half_groups) % (2 * half_groups)
    queries, fresh, stale, text = queries[0], fresh_kv[0], stale_kv[0], text_kv[0]
    slots, img_rows = queries.shape[:2]
    listed_count = refresh_rows.shape[2]
    hot_rows = 2 * listed_count

    raw = take_head(fresh_kv, listed_count)
    raw_in = from_behind(raw, "grp", half_groups)

    my_list = lax.dynamic_index_in_dim(refresh_rows, my_group, 0, keepdims=False)
    partner_list = lax.dynamic_index_in_dim(refresh_rows, partner, 0, keepdims=False)
    near, far, sources = swap_pairs(jnp.stack([my_list, partner_list]))

    first_cut = hot_rows + (img_rows - hot_rows) * 5 // 8
    last_cut = img_rows - listed_count
    final = slots - 1
    pieces = [(slot, hot_rows, img_rows) for slot in range(final)]
    pieces += [(final, hot_rows, first_cut), (final, first_cut, last_cut), (final, last_cut, img_rows)]
    zone, blocks = arrange(near[0].reshape(-1), far[0].reshape(-1), fresh_kv, pieces, raw)
    zone_in = from_behind(zone, "grp", half_groups)
    w_t = w_velocity.T
    text_own = project_text(text[:, :, 0], text[:, :, 1], w_t, zone)
    text_in = from_behind(text_own, "grp", half_groups)
    arrived, held = [], []
    for index, block in enumerate(blocks):
        if index < final:
            gate = raw_in
        elif index == final:
            gate = text_in
        else:
            gate = arrived[index - 2]
        held.append(hold(block, gate))
        arrived.append(from_behind(held[-1], "grp", half_groups))

    my_live = lax.dynamic_index_in_dim(live_counts, my_group, 0, keepdims=False)
    partner_live = lax.dynamic_index_in_dim(live_counts, partner, 0, keepdims=False)
    row_ids = jnp.arange(img_rows, dtype=jnp.int32)
    hot_source = jnp.concatenate(
        [jnp.broadcast_to(row_ids[:listed_count], partner_list.shape), sources[1]], axis=1
    )
    stale_listed = jnp.any(partner_list[:, :, None] == row_ids, axis=1)
    hot_listed = jnp.any(partner_list[:, :, None] == hot_source[:, None, :], axis=1)
    live = jnp.concatenate(
        [
            row_ids < my_live[:, None],
            (row_ids < partner_live[:, None]) & jnp.logical_not(stale_listed),
            (hot_source < partner_live[:, None]) & hot_listed,
            jnp.ones((slots, 2 * text.shape[1]), dtype=bool),
        ],
        axis=1,
    )
    bias = jnp.where(live, 0.0, -jnp.inf).astype(jnp.float32)[:, :, None]
    hot = join_head(raw_in, zone_in, (slots, hot_rows) + fresh.shape[2:])
    partial = attention(
        queries,
        fresh[:, :, 0],
        fresh[:, :, 1],
        stale[:, :, 0],
        stale[:, :, 1],
        hot[:, :, 0],
        hot[:, :, 1],
        text_own,
        text_in,
        w_t,
        bias,
    )

    tp_count = lax.axis_size("tp")
    tp_index = lax.axis_index("tp")
    share = img_rows // tp_count
    if tp_count == 2:
        mine = lax.dynamic_slice_in_dim(partial, tp_index * share, share, 2)
        theirs = lax.dynamic_slice_in_dim(partial, (1 - tp_index) * share, share, 2)
        summed = mine + from_behind(theirs, "tp", 1)
    else:
        summed = lax.psum_scatter(partial, "tp", scatter_dimension=2, tiled=True)
    summed = jnp.swapaxes(summed, 1, 2)
    share_ids = tp_index * share + jnp.arange(share, dtype=jnp.int32)
    live_rows = share_ids[None, :] < my_live[:, None]
    velocity = jnp.where(live_rows[:, :, None], summed, 0.0)
    pair_index = my_group % half_groups
    request_ids = lax.dynamic_slice_in_dim(request_list, pair_index * slots, slots)
    matches = (
        request_ids[:, None] == jnp.arange(timesteps.shape[0], dtype=jnp.int32)[None, :]
    ).astype(jnp.int32)
    times = jnp.sum(matches[:, :, None] * timesteps[None], axis=1)
    step_size = (times[:, 1] - times[:, 0]).astype(jnp.float32) / 1000.0
    latent_next = latent[0] + step_size[:, None, None] * velocity

    next_stale = join_head(raw_in, zone_in, fresh.shape)
    for index, piece in enumerate(pieces):
        next_stale = restore(
            near[1].reshape(-1), far[1].reshape(-1), arrived[index], next_stale, piece, held[index + 2 : index + 3]
        )
    return (next_stale[None], velocity[None], latent_next[None])


def solution(mesh):
    return jax.shard_map(
        shards,
        mesh=mesh,
        in_specs=(
            P("grp", None, None, "tp"),
            P("grp", None, None, None, "tp"),
            P("grp", None, None, None, "tp"),
            P("grp", None, None, None, "tp"),
            P("tp", None),
            P("grp", None, "tp", None),
            P(),
            P(),
            P(),
            P(),
        ),
        out_specs=(
            P("grp", None, None, None, "tp"),
            P("grp", None, "tp", None),
            P("grp", None, "tp", None),
        ),
        check_vma=False,
    )
```

```python
import functools
import math

import jax
import jax.numpy as jnp
from jax import lax
from jax.experimental import pallas as pl
from jax.experimental.pallas import tpu as pltpu
from jax.sharding import PartitionSpec as P

HD = 128
HBM = pltpu.MemorySpace.HBM
SMEM = pltpu.MemorySpace.SMEM
VMEM_LIMIT = 32 * 1024 * 1024
WIDE_LIMIT = 60 * 1024 * 1024


def from_behind(block, axis, distance):
    devices = range(lax.axis_size(axis))
    route = [((i - distance) % len(devices), i) for i in devices]
    return lax.ppermute(block, axis, route)


def swap_pairs(lists):
    count = lists.shape[2]
    zone = count + jnp.arange(count, dtype=jnp.int32)
    order = jnp.arange(count, dtype=jnp.int32)
    earlier = order[:, None] >= order[None, :]
    free = jnp.logical_not(jnp.any(lists[..., :, None] == zone, axis=2))
    outside = lists >= 2 * count
    free_rank = jnp.sum((earlier & free[..., None, :]).astype(jnp.int32), axis=3)
    outside_rank = jnp.sum((earlier & outside[..., None, :]).astype(jnp.int32), axis=3)
    match = (
        outside[..., :, None]
        & free[..., None, :]
        & (outside_rank[..., :, None] == free_rank[..., None, :])
    )
    near = jnp.sum(jnp.where(match, order, 0), axis=3)
    sources = jnp.sum(jnp.where(match, lists[..., :, None], 0), axis=2)
    return near, jnp.where(outside, lists, -1), jnp.where(sources > 0, sources, zone)


def swap_rows(near_ref, far_ref, slot, zone, piece, start, stop):
    count = zone.shape[0] - 1

    def step(k, carry):
        far = far_ref[slot * count + k]
        here = jnp.logical_and(far >= start, far < stop)
        near_row = jnp.where(here, near_ref[slot * count + k], count)
        far_row = jnp.where(here, far - start, stop - start)
        moved = zone[near_row]
        zone[near_row] = piece[far_row]
        piece[far_row] = moved
        return carry

    lax.fori_loop(0, count, step, 0, unroll=8)


def relay(copies, sems):
    inner = [pltpu.make_async_copy(c[0], c[1], sems.at[0, i]) for i, c in enumerate(copies)]
    outer = [pltpu.make_async_copy(c[1], c[2], sems.at[1, i]) for i, c in enumerate(copies)]
    for copy in inner:
        copy.start()
    for arrive, leave in zip(inner, outer):
        arrive.wait()
        leave.start()
    for copy in outer:
        copy.wait()


def take_kernel(fresh_ref, out_ref, stage, sems):
    slots, rows = out_ref.shape[:2]
    relay([(fresh_ref.at[0, s, :rows], stage.at[s], out_ref.at[s]) for s in range(slots)], sems)


def take_head(fresh_kv, rows):
    shape = (fresh_kv.shape[1], rows) + fresh_kv.shape[3:]
    return pl.pallas_call(
        take_kernel,
        out_shape=jax.ShapeDtypeStruct(shape, fresh_kv.dtype),
        in_specs=[pl.BlockSpec(memory_space=HBM)],
        out_specs=pl.BlockSpec(memory_space=HBM),
        scratch_shapes=[pltpu.VMEM(shape, fresh_kv.dtype), pltpu.SemaphoreType.DMA((2, shape[0]))],
        cost_estimate=pl.CostEstimate(flops=0, bytes_accessed=4 * math.prod(shape), transcendentals=0),
        compiler_params=pltpu.CompilerParams(vmem_limit_bytes=WIDE_LIMIT),
        name="take_head",
    )(fresh_kv)


def arrange_kernel(slots, pieces, near_ref, far_ref, fresh_ref, after_ref, *refs):
    zone_out, piece_outs = refs[0], refs[1 : 1 + len(pieces)]
    zones, rests, sems = refs[1 + len(pieces) :]
    count = zones.shape[1] - 1
    rest_rows = rests.shape[1] - 1
    copies_in = []
    for slot in range(slots):
        copies_in.append(
            (
                pltpu.make_async_copy(
                    fresh_ref.at[0, slot, count : 2 * count], zones.at[slot, :count], sems.at[slot]
                ),
                pltpu.make_async_copy(
                    fresh_ref.at[0, slot, 2 * count :], rests.at[slot, :rest_rows], sems.at[slots + slot]
                ),
            )
        )
        for copy in copies_in[-1]:
            copy.start()
    copies_out = []
    for slot in range(slots):
        for copy in copies_in[slot]:
            copy.wait()
        swap_rows(
            near_ref, far_ref, slot, zones.at[slot], rests.at[slot], 2 * count, 2 * count + rest_rows
        )
        copies_out.append(
            pltpu.make_async_copy(zones.at[slot, :count], zone_out.at[slot], sems.at[2 * slots + slot])
        )
        copies_out[-1].start()
        for index, (piece_slot, start, stop) in enumerate(pieces):
            if piece_slot == slot:
                source = rests.at[slot, start - 2 * count : stop - 2 * count]
                copies_out.append(
                    pltpu.make_async_copy(source, piece_outs[index], sems.at[3 * slots + index])
                )
                copies_out[-1].start()
    for copy in copies_out:
        copy.wait()


def arrange(near, far, fresh_kv, pieces, after):
    slots, rows = fresh_kv.shape[1:3]
    tail = fresh_kv.shape[3:]
    count = near.shape[0] // slots
    outs = pl.pallas_call(
        functools.partial(arrange_kernel, slots, pieces),
        out_shape=[jax.ShapeDtypeStruct((slots, count) + tail, fresh_kv.dtype)]
        + [jax.ShapeDtypeStruct((stop - start,) + tail, fresh_kv.dtype) for _, start, stop in pieces],
        in_specs=[pl.BlockSpec(memory_space=SMEM)] * 2 + [pl.BlockSpec(memory_space=HBM)] * 2,
        out_specs=[pl.BlockSpec(memory_space=HBM)] * (1 + len(pieces)),
        scratch_shapes=[
            pltpu.VMEM((slots, count + 1) + tail, fresh_kv.dtype),
            pltpu.VMEM((slots, rows - 2 * count + 1) + tail, fresh_kv.dtype),
            pltpu.SemaphoreType.DMA((3 * slots + len(pieces),)),
        ],
        cost_estimate=pl.CostEstimate(flops=0, bytes_accessed=4 * fresh_kv.size, transcendentals=0),
        compiler_params=pltpu.CompilerParams(vmem_limit_bytes=WIDE_LIMIT),
        name="arrange",
    )(near, far, fresh_kv, after)
    return outs[0], outs[1:]


def join_kernel(raw_ref, zone_ref, out_ref, stage, sems):
    count = raw_ref.shape[1]
    relay(
        [
            (raw_ref, stage.at[0], out_ref.at[:, :count]),
            (zone_ref, stage.at[1], out_ref.at[:, count : 2 * count]),
        ],
        sems,
    )


def join_head(raw, zone, shape):
    return pl.pallas_call(
        join_kernel,
        out_shape=jax.ShapeDtypeStruct(shape, raw.dtype),
        in_specs=[pl.BlockSpec(memory_space=HBM)] * 2,
        out_specs=pl.BlockSpec(memory_space=HBM),
        scratch_shapes=[pltpu.VMEM((2,) + raw.shape, raw.dtype), pltpu.SemaphoreType.DMA((2, 2))],
        cost_estimate=pl.CostEstimate(flops=0, bytes_accessed=8 * raw.size, transcendentals=0),
        compiler_params=pltpu.CompilerParams(vmem_limit_bytes=VMEM_LIMIT),
        name="join_head",
    )(raw, zone)


def restore_kernel(slot, start, stop, near_ref, far_ref, piece_ref, whole_ref, *refs):
    out_ref, zone, piece, sems = refs[-4:]
    count = zone.shape[0] - 1
    inner = [
        pltpu.make_async_copy(piece_ref, piece.at[: stop - start], sems.at[0]),
        pltpu.make_async_copy(out_ref.at[slot, count : 2 * count], zone.at[:count], sems.at[1]),
    ]
    for copy in inner:
        copy.start()
    for copy in inner:
        copy.wait()
    swap_rows(near_ref, far_ref, slot, zone, piece, start, stop)
    outer = [
        pltpu.make_async_copy(piece.at[: stop - start], out_ref.at[slot, start:stop], sems.at[2]),
        pltpu.make_async_copy(zone.at[:count], out_ref.at[slot, count : 2 * count], sems.at[3]),
    ]
    for copy in outer:
        copy.start()
    for copy in outer:
        copy.wait()


def restore(near, far, block, whole, piece, after=()):
    slot, start, stop = piece
    tail = whole.shape[2:]
    count = near.shape[0] // whole.shape[0]
    return pl.pallas_call(
        functools.partial(restore_kernel, slot, start, stop),
        out_shape=jax.ShapeDtypeStruct(whole.shape, whole.dtype),
        in_specs=[pl.BlockSpec(memory_space=SMEM)] * 2 + [pl.BlockSpec(memory_space=HBM)] * (2 + len(after)),
        out_specs=pl.BlockSpec(memory_space=HBM),
        scratch_shapes=[
            pltpu.VMEM((count + 1,) + tail, whole.dtype),
            pltpu.VMEM((stop - start + 1,) + tail, whole.dtype),
            pltpu.SemaphoreType.DMA((4,)),
        ],
        input_output_aliases={3: 0},
        cost_estimate=pl.CostEstimate(flops=0, bytes_accessed=4 * block.size, transcendentals=0),
        compiler_params=pltpu.CompilerParams(vmem_limit_bytes=VMEM_LIMIT),
        name="restore",
    )(near, far, block, whole, *after)


def hold_kernel(block_ref, after_ref, out_ref):
    del block_ref, after_ref, out_ref


def hold(block, after):
    return pl.pallas_call(
        hold_kernel,
        out_shape=jax.ShapeDtypeStruct(block.shape, block.dtype),
        in_specs=[pl.BlockSpec(memory_space=HBM)] * 2,
        out_specs=pl.BlockSpec(memory_space=HBM),
        input_output_aliases={0: 0},
        cost_estimate=pl.CostEstimate(flops=0, bytes_accessed=0, transcendentals=0),
        name="hold",
    )(block, after)


def across(a, b):
    return lax.dot_general(a, b, (((1,), (1,)), ((), ())), preferred_element_type=jnp.float32)


def text_kernel(k_ref, v_ref, w_ref, after_ref, out_ref):
    rows = k_ref.shape[1]
    channels = w_ref.shape[0]
    out_ref[0, 0, :rows, :] = k_ref[0]
    projected = across(w_ref[...], v_ref[0]).astype(out_ref.dtype)
    for part in range(rows // HD):
        start = rows + part * channels
        out_ref[0, 0, start : start + channels, :] = projected[:, part * HD : (part + 1) * HD]


def project_text(keys, values, w_t, after):
    slots, rows, width = keys.shape
    heads = width // HD
    channels = w_t.shape[0]
    packed = rows + channels * rows // HD
    block = pl.BlockSpec((1, rows, HD), lambda s, h: (s, 0, h))
    return pl.pallas_call(
        text_kernel,
        grid=(slots, heads),
        out_shape=jax.ShapeDtypeStruct((slots, heads, packed, HD), keys.dtype),
        in_specs=[block, block, pl.BlockSpec((channels, HD), lambda s, h: (0, h)), pl.BlockSpec(memory_space=HBM)],
        out_specs=pl.BlockSpec((1, 1, packed, HD), lambda s, h: (s, h, 0, 0)),
        cost_estimate=pl.CostEstimate(
            flops=2 * slots * rows * width * channels, bytes_accessed=4 * keys.size * 2, transcendentals=0
        ),
        name="project_text",
    )(keys, values, w_t, after)


def attention_kernel(text_rows, *refs):
    (q_ref, kf_ref, vf_ref, ks_ref, vs_ref, kh_ref, vh_ref, own_ref, other_ref, w_ref, bias_ref) = refs[:11]
    out_ref, scores_ref = refs[11], refs[12]
    head = pl.program_id(1)
    query = q_ref[0]
    w_t = w_ref[...]
    channels = w_t.shape[0]
    scale = 1.0 / math.sqrt(HD)
    pieces = []
    for k_ref, v_ref in ((kf_ref, vf_ref), (ks_ref, vs_ref), (kh_ref, vh_ref)):
        rows = k_ref.shape[1]
        step = min(rows, 256)
        for start in range(0, rows, step):
            pieces.append((k_ref.at[0, start : start + step], v_ref.at[0, start : start + step], step))
    for t_ref in (own_ref, other_ref):
        pieces.append((t_ref.at[0, 0, :text_rows], t_ref, text_rows))
    top = None
    at = 0
    for k_ref, _, rows in pieces:
        scores = across(k_ref[...], query) * scale + bias_ref[0, at : at + rows]
        scores_ref[at : at + rows, :] = scores
        piece_top = jnp.max(scores, axis=0, keepdims=True)
        top = piece_top if top is None else jnp.maximum(top, piece_top)
        at += rows
    total = jnp.zeros_like(top)
    blended = jnp.zeros((channels, query.shape[0]), jnp.float32)
    at = 0
    for _, v_ref, rows in pieces:
        weights = jnp.exp(scores_ref[at : at + rows, :] - top)
        total += jnp.sum(weights, axis=0, keepdims=True)
        rounded = weights.astype(jnp.bfloat16)
        if v_ref.shape[-2] == rows and len(v_ref.shape) == 2:
            projected = across(w_t, v_ref[...]).astype(jnp.bfloat16)
            blended += jnp.dot(projected, rounded, preferred_element_type=jnp.float32)
        else:
            for part in range(rows // HD):
                start = rows + part * channels
                blended += jnp.dot(
                    v_ref[0, 0, start : start + channels, :],
                    rounded[part * HD : (part + 1) * HD],
                    preferred_element_type=jnp.float32,
                )
        at += rows
    term = blended / total

    @pl.when(head == 0)
    def _():
        out_ref[0] = term

    @pl.when(head != 0)
    def _():
        out_ref[0] += term


def attention(queries, fresh_k, fresh_v, stale_k, stale_v, hot_k, hot_v, text_own, text_other, w_t, bias):
    slots, rows, width = queries.shape
    heads = width // HD
    channels = w_t.shape[0]
    key_rows = bias.shape[1]
    text_rows = (text_own.shape[2] * HD) // (HD + channels)

    def wide(array):
        return pl.BlockSpec((1, array.shape[1], HD), lambda s, h: (s, 0, h))

    packed = pl.BlockSpec((1, 1) + text_own.shape[2:], lambda s, h: (s, h, 0, 0))
    many = slots * heads * rows * key_rows
    return pl.pallas_call(
        functools.partial(attention_kernel, text_rows),
        grid=(slots, heads),
        out_shape=jax.ShapeDtypeStruct((slots, channels, rows), jnp.float32),
        in_specs=[wide(a) for a in (queries, fresh_k, fresh_v, stale_k, stale_v, hot_k, hot_v)]
        + [
            packed,
            packed,
            pl.BlockSpec((channels, HD), lambda s, h: (0, h)),
            pl.BlockSpec((1, key_rows, 1), lambda s, h: (s, 0, 0)),
        ],
        out_specs=pl.BlockSpec((1, channels, rows), lambda s, h: (s, 0, 0)),
        scratch_shapes=[pltpu.VMEM((key_rows, rows), jnp.float32)],
        cost_estimate=pl.CostEstimate(
            flops=2 * many * (HD + channels), bytes_accessed=24 * 1024 * 1024, transcendentals=many
        ),
        compiler_params=pltpu.CompilerParams(vmem_limit_bytes=VMEM_LIMIT),
        name="attention",
    )(queries, fresh_k, fresh_v, stale_k, stale_v, hot_k, hot_v, text_own, text_other, w_t, bias)


def shards(
    queries,
    fresh_kv,
    stale_kv,
    text_kv,
    w_velocity,
    latent,
    live_counts,
    refresh_rows,
    request_list,
    timesteps,
):
    half_groups = lax.axis_size("grp") // 2
    my_group = lax.axis_index("grp")
    partner = (my_group + half_groups) % (2 * half_groups)
    queries, fresh, stale, text = queries[0], fresh_kv[0], stale_kv[0], text_kv[0]
    slots, img_rows = queries.shape[:2]
    listed_count = refresh_rows.shape[2]
    hot_rows = 2 * listed_count

    raw = take_head(fresh_kv, listed_count)
    raw_in = from_behind(raw, "grp", half_groups)

    my_list = lax.dynamic_index_in_dim(refresh_rows, my_group, 0, keepdims=False)
    partner_list = lax.dynamic_index_in_dim(refresh_rows, partner, 0, keepdims=False)
    near, far, sources = swap_pairs(jnp.stack([my_list, partner_list]))

    first_cut = hot_rows + (img_rows - hot_rows) * 5 // 8
    last_cut = img_rows - listed_count
    final = slots - 1
    pieces = [(slot, hot_rows, img_rows) for slot in range(final)]
    pieces += [(final, hot_rows, first_cut), (final, first_cut, last_cut), (final, last_cut, img_rows)]
    zone, blocks = arrange(near[0].reshape(-1), far[0].reshape(-1), fresh_kv, pieces, raw)
    zone_in = from_behind(zone, "grp", half_groups)
    w_t = w_velocity.T
    text_own = project_text(text[:, :, 0], text[:, :, 1], w_t, zone)
    text_in = from_behind(text_own, "grp", half_groups)
    arrived, held = [], []
    for index, block in enumerate(blocks):
        if index < final:
            gate = raw_in
        elif index == final:
            gate = text_in
        else:
            gate = arrived[index - 2]
        held.append(hold(block, gate))
        arrived.append(from_behind(held[-1], "grp", half_groups))

    my_live = lax.dynamic_index_in_dim(live_counts, my_group, 0, keepdims=False)
    partner_live = lax.dynamic_index_in_dim(live_counts, partner, 0, keepdims=False)
    row_ids = jnp.arange(img_rows, dtype=jnp.int32)
    hot_source = jnp.concatenate(
        [jnp.broadcast_to(row_ids[:listed_count], partner_list.shape), sources[1]], axis=1
    )
    stale_listed = jnp.any(partner_list[:, :, None] == row_ids, axis=1)
    hot_listed = jnp.any(partner_list[:, :, None] == hot_source[:, None, :], axis=1)
    live = jnp.concatenate(
        [
            row_ids < my_live[:, None],
            (row_ids < partner_live[:, None]) & jnp.logical_not(stale_listed),
            (hot_source < partner_live[:, None]) & hot_listed,
            jnp.ones((slots, 2 * text.shape[1]), dtype=bool),
        ],
        axis=1,
    )
    bias = jnp.where(live, 0.0, -jnp.inf).astype(jnp.float32)[:, :, None]
    hot = join_head(raw_in, zone_in, (slots, hot_rows) + fresh.shape[2:])
    partial = attention(
        queries,
        fresh[:, :, 0],
        fresh[:, :, 1],
        stale[:, :, 0],
        stale[:, :, 1],
        hot[:, :, 0],
        hot[:, :, 1],
        text_own,
        text_in,
        w_t,
        bias,
    )

    tp_count = lax.axis_size("tp")
    tp_index = lax.axis_index("tp")
    share = img_rows // tp_count
    if tp_count == 2:
        mine = lax.dynamic_slice_in_dim(partial, tp_index * share, share, 2)
        theirs = lax.dynamic_slice_in_dim(partial, (1 - tp_index) * share, share, 2)
        summed = mine + from_behind(theirs, "tp", 1)
    else:
        summed = lax.psum_scatter(partial, "tp", scatter_dimension=2, tiled=True)
    summed = jnp.swapaxes(summed, 1, 2)
    share_ids = tp_index * share + jnp.arange(share, dtype=jnp.int32)
    live_rows = share_ids[None, :] < my_live[:, None]
    velocity = jnp.where(live_rows[:, :, None], summed, 0.0)
    pair_index = my_group % half_groups
    request_ids = lax.dynamic_slice_in_dim(request_list, pair_index * slots, slots)
    matches = (
        request_ids[:, None] == jnp.arange(timesteps.shape[0], dtype=jnp.int32)[None, :]
    ).astype(jnp.int32)
    times = jnp.sum(matches[:, :, None] * timesteps[None], axis=1)
    step_size = (times[:, 1] - times[:, 0]).astype(jnp.float32) / 1000.0
    latent_next = latent[0] + step_size[:, None, None] * velocity

    next_stale = join_head(raw_in, zone_in, fresh.shape)
    for index, piece in enumerate(pieces):
        next_stale = restore(
            near[1].reshape(-1), far[1].reshape(-1), arrived[index], next_stale, piece, held[index + 2 : index + 3]
        )
    return (next_stale[None], velocity[None], latent_next[None])


def solution(mesh):
    return jax.shard_map(
        shards,
        mesh=mesh,
        in_specs=(
            P("grp", None, None, "tp"),
            P("grp", None, None, None, "tp"),
            P("grp", None, None, None, "tp"),
            P("grp", None, None, None, "tp"),
            P("tp", None),
            P("grp", None, "tp", None),
            P(),
            P(),
            P(),
            P(),
        ),
        out_specs=(
            P("grp", None, None, None, "tp"),
            P("grp", None, "tp", None),
            P("grp", None, "tp", None),
        ),
        check_vma=False,
    )
```

```python
import functools
import math

import jax
import jax.numpy as jnp
from jax import lax
from jax.experimental import pallas as pl
from jax.experimental.pallas import tpu as pltpu
from jax.sharding import PartitionSpec as P

HD = 128
HBM = pltpu.MemorySpace.HBM
SMEM = pltpu.MemorySpace.SMEM
VMEM_LIMIT = 32 * 1024 * 1024
WIDE_LIMIT = 60 * 1024 * 1024


def from_behind(block, axis, distance):
    devices = range(lax.axis_size(axis))
    route = [((i - distance) % len(devices), i) for i in devices]
    return lax.ppermute(block, axis, route)


def swap_pairs(lists):
    count = lists.shape[2]
    zone = count + jnp.arange(count, dtype=jnp.int32)
    order = jnp.arange(count, dtype=jnp.int32)
    earlier = order[:, None] >= order[None, :]
    free = jnp.logical_not(jnp.any(lists[..., :, None] == zone, axis=2))
    outside = lists >= 2 * count
    free_rank = jnp.sum((earlier & free[..., None, :]).astype(jnp.int32), axis=3)
    outside_rank = jnp.sum((earlier & outside[..., None, :]).astype(jnp.int32), axis=3)
    match = (
        outside[..., :, None]
        & free[..., None, :]
        & (outside_rank[..., :, None] == free_rank[..., None, :])
    )
    near = jnp.sum(jnp.where(match, order, 0), axis=3)
    sources = jnp.sum(jnp.where(match, lists[..., :, None], 0), axis=2)
    return near, jnp.where(outside, lists, -1), jnp.where(sources > 0, sources, zone)


def swap_rows(pairs, slots, slot, zone, piece, start, stop):
    count = zone.shape[0] - 1

    def step(k, carry):
        far = pairs[(slots + slot) * count + k]
        here = jnp.logical_and(far >= start, far < stop)
        near_row = jnp.where(here, pairs[slot * count + k], count)
        far_row = jnp.where(here, far - start, stop - start)
        moved = zone[near_row]
        zone[near_row] = piece[far_row]
        piece[far_row] = moved
        return carry

    lax.fori_loop(0, count, step, 0, unroll=8)


def relay(copies, sems):
    inner = [pltpu.make_async_copy(c[0], c[1], sems.at[0, i]) for i, c in enumerate(copies)]
    outer = [pltpu.make_async_copy(c[1], c[2], sems.at[1, i]) for i, c in enumerate(copies)]
    for copy in inner:
        copy.start()
    for arrive, leave in zip(inner, outer):
        arrive.wait()
        leave.start()
    for copy in outer:
        copy.wait()


def arrange_kernel(slots, pieces, pairs_ref, fresh_ref, after_ref, *refs):
    zone_out, piece_outs = refs[0], refs[1 : 1 + len(pieces)]
    pairs, zones, rests, sems = refs[1 + len(pieces) :]
    count = zones.shape[1] - 1
    rest_rows = rests.shape[1] - 1
    copy_pairs = pltpu.make_async_copy(pairs_ref, pairs, sems.at[3 * slots + len(pieces)])
    copy_pairs.start()
    copies_in = []
    for slot in range(slots):
        copies_in.append(
            (
                pltpu.make_async_copy(
                    fresh_ref.at[0, slot, count : 2 * count], zones.at[slot, :count], sems.at[slot]
                ),
                pltpu.make_async_copy(
                    fresh_ref.at[0, slot, 2 * count :], rests.at[slot, :rest_rows], sems.at[slots + slot]
                ),
            )
        )
        for copy in copies_in[-1]:
            copy.start()
    copy_pairs.wait()
    copies_out = []
    for slot in range(slots):
        for copy in copies_in[slot]:
            copy.wait()
        swap_rows(pairs, slots, slot, zones.at[slot], rests.at[slot], 2 * count, 2 * count + rest_rows)
        copies_out.append(
            pltpu.make_async_copy(zones.at[slot, :count], zone_out.at[slot], sems.at[2 * slots + slot])
        )
        copies_out[-1].start()
        for index, (piece_slot, start, stop) in enumerate(pieces):
            if piece_slot == slot:
                source = rests.at[slot, start - 2 * count : stop - 2 * count]
                copies_out.append(
                    pltpu.make_async_copy(source, piece_outs[index], sems.at[3 * slots + index])
                )
                copies_out[-1].start()
    for copy in copies_out:
        copy.wait()


def arrange(pairs, fresh_kv, pieces, after):
    slots, rows = fresh_kv.shape[1:3]
    tail = fresh_kv.shape[3:]
    count = pairs.shape[0] // (2 * slots)
    outs = pl.pallas_call(
        functools.partial(arrange_kernel, slots, pieces),
        out_shape=[jax.ShapeDtypeStruct((slots, count) + tail, fresh_kv.dtype)]
        + [jax.ShapeDtypeStruct((stop - start,) + tail, fresh_kv.dtype) for _, start, stop in pieces],
        in_specs=[pl.BlockSpec(memory_space=HBM)] * 3,
        out_specs=[pl.BlockSpec(memory_space=HBM)] * (1 + len(pieces)),
        scratch_shapes=[
            pltpu.SMEM(pairs.shape, pairs.dtype),
            pltpu.VMEM((slots, count + 1) + tail, fresh_kv.dtype),
            pltpu.VMEM((slots, rows - 2 * count + 1) + tail, fresh_kv.dtype),
            pltpu.SemaphoreType.DMA((3 * slots + len(pieces) + 1,)),
        ],
        cost_estimate=pl.CostEstimate(flops=0, bytes_accessed=4 * fresh_kv.size, transcendentals=0),
        compiler_params=pltpu.CompilerParams(vmem_limit_bytes=WIDE_LIMIT),
        name="arrange",
    )(pairs, fresh_kv, after)
    return outs[0], outs[1:]


def join_kernel(raw_ref, zone_ref, out_ref, stage, sems):
    count = raw_ref.shape[1]
    relay(
        [
            (raw_ref, stage.at[0], out_ref.at[:, :count]),
            (zone_ref, stage.at[1], out_ref.at[:, count : 2 * count]),
        ],
        sems,
    )


def join_head(raw, zone, shape):
    return pl.pallas_call(
        join_kernel,
        out_shape=jax.ShapeDtypeStruct(shape, raw.dtype),
        in_specs=[pl.BlockSpec(memory_space=HBM)] * 2,
        out_specs=pl.BlockSpec(memory_space=HBM),
        scratch_shapes=[pltpu.VMEM((2,) + raw.shape, raw.dtype), pltpu.SemaphoreType.DMA((2, 2))],
        cost_estimate=pl.CostEstimate(flops=0, bytes_accessed=8 * raw.size, transcendentals=0),
        compiler_params=pltpu.CompilerParams(vmem_limit_bytes=VMEM_LIMIT),
        name="join_head",
    )(raw, zone)


def restore_kernel(slot, start, stop, pairs_ref, piece_ref, whole_ref, *refs):
    out_ref, pairs, zone, piece, sems = refs[-5:]
    count = zone.shape[0] - 1
    inner = [
        pltpu.make_async_copy(pairs_ref, pairs, sems.at[4]),
        pltpu.make_async_copy(piece_ref, piece.at[: stop - start], sems.at[0]),
        pltpu.make_async_copy(out_ref.at[slot, count : 2 * count], zone.at[:count], sems.at[1]),
    ]
    for copy in inner:
        copy.start()
    for copy in inner:
        copy.wait()
    swap_rows(pairs, out_ref.shape[0], slot, zone, piece, start, stop)
    outer = [
        pltpu.make_async_copy(piece.at[: stop - start], out_ref.at[slot, start:stop], sems.at[2]),
        pltpu.make_async_copy(zone.at[:count], out_ref.at[slot, count : 2 * count], sems.at[3]),
    ]
    for copy in outer:
        copy.start()
    for copy in outer:
        copy.wait()


def restore(pairs, block, whole, piece, after=()):
    slot, start, stop = piece
    tail = whole.shape[2:]
    count = pairs.shape[0] // (2 * whole.shape[0])
    return pl.pallas_call(
        functools.partial(restore_kernel, slot, start, stop),
        out_shape=jax.ShapeDtypeStruct(whole.shape, whole.dtype),
        in_specs=[pl.BlockSpec(memory_space=HBM)] * (3 + len(after)),
        out_specs=pl.BlockSpec(memory_space=HBM),
        scratch_shapes=[
            pltpu.SMEM(pairs.shape, pairs.dtype),
            pltpu.VMEM((count + 1,) + tail, whole.dtype),
            pltpu.VMEM((stop - start + 1,) + tail, whole.dtype),
            pltpu.SemaphoreType.DMA((5,)),
        ],
        input_output_aliases={2: 0},
        cost_estimate=pl.CostEstimate(flops=0, bytes_accessed=4 * block.size, transcendentals=0),
        compiler_params=pltpu.CompilerParams(vmem_limit_bytes=VMEM_LIMIT),
        name="restore",
    )(pairs, block, whole, *after)


def hold_kernel(block_ref, after_ref, out_ref):
    del block_ref, after_ref, out_ref


def hold(block, after):
    return pl.pallas_call(
        hold_kernel,
        out_shape=jax.ShapeDtypeStruct(block.shape, block.dtype),
        in_specs=[pl.BlockSpec(memory_space=HBM)] * 2,
        out_specs=pl.BlockSpec(memory_space=HBM),
        input_output_aliases={0: 0},
        cost_estimate=pl.CostEstimate(flops=0, bytes_accessed=0, transcendentals=0),
        name="hold",
    )(block, after)


def across(a, b):
    return lax.dot_general(a, b, (((1,), (1,)), ((), ())), preferred_element_type=jnp.float32)


def text_kernel(k_ref, v_ref, w_ref, after_ref, out_ref):
    rows = k_ref.shape[1]
    channels = w_ref.shape[0]
    out_ref[0, 0, :rows, :] = k_ref[0]
    projected = across(w_ref[...], v_ref[0]).astype(out_ref.dtype)
    for part in range(rows // HD):
        start = rows + part * channels
        out_ref[0, 0, start : start + channels, :] = projected[:, part * HD : (part + 1) * HD]


def project_text(keys, values, w_t, after):
    slots, rows, width = keys.shape
    heads = width // HD
    channels = w_t.shape[0]
    packed = rows + channels * rows // HD
    block = pl.BlockSpec((1, rows, HD), lambda s, h: (s, 0, h))
    return pl.pallas_call(
        text_kernel,
        grid=(slots, heads),
        out_shape=jax.ShapeDtypeStruct((slots, heads, packed, HD), keys.dtype),
        in_specs=[block, block, pl.BlockSpec((channels, HD), lambda s, h: (0, h)), pl.BlockSpec(memory_space=HBM)],
        out_specs=pl.BlockSpec((1, 1, packed, HD), lambda s, h: (s, h, 0, 0)),
        cost_estimate=pl.CostEstimate(
            flops=2 * slots * rows * width * channels, bytes_accessed=4 * keys.size * 2, transcendentals=0
        ),
        name="project_text",
    )(keys, values, w_t, after)


def attention_kernel(text_rows, *refs):
    (q_ref, kf_ref, vf_ref, ks_ref, vs_ref, kh_ref, vh_ref, own_ref, other_ref, w_ref, bias_ref) = refs[:11]
    out_ref, scores_ref = refs[11], refs[12]
    head = pl.program_id(1)
    query = q_ref[0]
    w_t = w_ref[...]
    channels = w_t.shape[0]
    scale = 1.0 / math.sqrt(HD)
    pieces = []
    for k_ref, v_ref in ((kf_ref, vf_ref), (ks_ref, vs_ref), (kh_ref, vh_ref)):
        rows = k_ref.shape[1]
        step = min(rows, 256)
        for start in range(0, rows, step):
            pieces.append((k_ref.at[0, start : start + step], v_ref.at[0, start : start + step], step))
    for t_ref in (own_ref, other_ref):
        pieces.append((t_ref.at[0, 0, :text_rows], t_ref, text_rows))
    top = None
    at = 0
    for k_ref, _, rows in pieces:
        scores = across(k_ref[...], query) * scale + bias_ref[0, at : at + rows]
        scores_ref[at : at + rows, :] = scores
        piece_top = jnp.max(scores, axis=0, keepdims=True)
        top = piece_top if top is None else jnp.maximum(top, piece_top)
        at += rows
    total = jnp.zeros_like(top)
    blended = jnp.zeros((channels, query.shape[0]), jnp.float32)
    at = 0
    for _, v_ref, rows in pieces:
        weights = jnp.exp(scores_ref[at : at + rows, :] - top)
        total += jnp.sum(weights, axis=0, keepdims=True)
        rounded = weights.astype(jnp.bfloat16)
        if v_ref.shape[-2] == rows and len(v_ref.shape) == 2:
            projected = across(w_t, v_ref[...]).astype(jnp.bfloat16)
            blended += jnp.dot(projected, rounded, preferred_element_type=jnp.float32)
        else:
            for part in range(rows // HD):
                start = rows + part * channels
                blended += jnp.dot(
                    v_ref[0, 0, start : start + channels, :],
                    rounded[part * HD : (part + 1) * HD],
                    preferred_element_type=jnp.float32,
                )
        at += rows
    term = blended / total

    @pl.when(head == 0)
    def _():
        out_ref[0] = term

    @pl.when(head != 0)
    def _():
        out_ref[0] += term


def attention(queries, fresh_k, fresh_v, stale_k, stale_v, hot_k, hot_v, text_own, text_other, w_t, bias):
    slots, rows, width = queries.shape
    heads = width // HD
    channels = w_t.shape[0]
    key_rows = bias.shape[1]
    text_rows = (text_own.shape[2] * HD) // (HD + channels)

    def wide(array):
        return pl.BlockSpec((1, array.shape[1], HD), lambda s, h: (s, 0, h))

    packed = pl.BlockSpec((1, 1) + text_own.shape[2:], lambda s, h: (s, h, 0, 0))
    many = slots * heads * rows * key_rows
    return pl.pallas_call(
        functools.partial(attention_kernel, text_rows),
        grid=(slots, heads),
        out_shape=jax.ShapeDtypeStruct((slots, channels, rows), jnp.float32),
        in_specs=[wide(a) for a in (queries, fresh_k, fresh_v, stale_k, stale_v, hot_k, hot_v)]
        + [
            packed,
            packed,
            pl.BlockSpec((channels, HD), lambda s, h: (0, h)),
            pl.BlockSpec((1, key_rows, 1), lambda s, h: (s, 0, 0)),
        ],
        out_specs=pl.BlockSpec((1, channels, rows), lambda s, h: (s, 0, 0)),
        scratch_shapes=[pltpu.VMEM((key_rows, rows), jnp.float32)],
        cost_estimate=pl.CostEstimate(
            flops=2 * many * (HD + channels), bytes_accessed=24 * 1024 * 1024, transcendentals=many
        ),
        compiler_params=pltpu.CompilerParams(vmem_limit_bytes=VMEM_LIMIT),
        name="attention",
    )(queries, fresh_k, fresh_v, stale_k, stale_v, hot_k, hot_v, text_own, text_other, w_t, bias)


def shards(
    queries,
    fresh_kv,
    stale_kv,
    text_kv,
    w_velocity,
    latent,
    live_counts,
    refresh_rows,
    request_list,
    timesteps,
):
    half_groups = lax.axis_size("grp") // 2
    my_group = lax.axis_index("grp")
    partner = (my_group + half_groups) % (2 * half_groups)
    queries, fresh, stale, text = queries[0], fresh_kv[0], stale_kv[0], text_kv[0]
    slots, img_rows = queries.shape[:2]
    listed_count = refresh_rows.shape[2]
    hot_rows = 2 * listed_count

    raw = fresh_kv[0, :, :listed_count]
    raw_in = from_behind(raw, "grp", half_groups)

    my_list = lax.dynamic_index_in_dim(refresh_rows, my_group, 0, keepdims=False)
    partner_list = lax.dynamic_index_in_dim(refresh_rows, partner, 0, keepdims=False)
    near, far, sources = swap_pairs(jnp.stack([my_list, partner_list]))
    pairs = jnp.stack([near, far], axis=1).reshape(2, -1)

    first_cut = hot_rows + (img_rows - hot_rows) * 5 // 8
    last_cut = img_rows - listed_count
    final = slots - 1
    pieces = [(slot, hot_rows, img_rows) for slot in range(final)]
    pieces += [(final, hot_rows, first_cut), (final, first_cut, last_cut), (final, last_cut, img_rows)]
    zone, blocks = arrange(pairs[0], fresh_kv, pieces, raw)
    zone_in = from_behind(zone, "grp", half_groups)
    w_t = w_velocity.T
    text_own = project_text(text[:, :, 0], text[:, :, 1], w_t, zone)
    text_in = from_behind(text_own, "grp", half_groups)
    arrived, held = [], []
    for index, block in enumerate(blocks):
        if index < final:
            gate = raw_in
        elif index == final:
            gate = text_in
        else:
            gate = arrived[index - 2]
        held.append(hold(block, gate))
        arrived.append(from_behind(held[-1], "grp", half_groups))

    my_live = lax.dynamic_index_in_dim(live_counts, my_group, 0, keepdims=False)
    partner_live = lax.dynamic_index_in_dim(live_counts, partner, 0, keepdims=False)
    row_ids = jnp.arange(img_rows, dtype=jnp.int32)
    hot_source = jnp.concatenate(
        [jnp.broadcast_to(row_ids[:listed_count], partner_list.shape), sources[1]], axis=1
    )
    stale_listed = jnp.any(partner_list[:, :, None] == row_ids, axis=1)
    hot_listed = jnp.any(partner_list[:, :, None] == hot_source[:, None, :], axis=1)
    live = jnp.concatenate(
        [
            row_ids < my_live[:, None],
            (row_ids < partner_live[:, None]) & jnp.logical_not(stale_listed),
            (hot_source < partner_live[:, None]) & hot_listed,
            jnp.ones((slots, 2 * text.shape[1]), dtype=bool),
        ],
        axis=1,
    )
    bias = jnp.where(live, 0.0, -jnp.inf).astype(jnp.float32)[:, :, None]
    hot = join_head(raw_in, zone_in, (slots, hot_rows) + fresh.shape[2:])
    partial = attention(
        queries,
        fresh[:, :, 0],
        fresh[:, :, 1],
        stale[:, :, 0],
        stale[:, :, 1],
        hot[:, :, 0],
        hot[:, :, 1],
        text_own,
        text_in,
        w_t,
        bias,
    )

    tp_count = lax.axis_size("tp")
    tp_index = lax.axis_index("tp")
    share = img_rows // tp_count
    if tp_count == 2:
        mine = lax.dynamic_slice_in_dim(partial, tp_index * share, share, 2)
        theirs = lax.dynamic_slice_in_dim(partial, (1 - tp_index) * share, share, 2)
        summed = mine + from_behind(theirs, "tp", 1)
    else:
        summed = lax.psum_scatter(partial, "tp", scatter_dimension=2, tiled=True)
    summed = jnp.swapaxes(summed, 1, 2)
    share_ids = tp_index * share + jnp.arange(share, dtype=jnp.int32)
    live_rows = share_ids[None, :] < my_live[:, None]
    velocity = jnp.where(live_rows[:, :, None], summed, 0.0)
    pair_index = my_group % half_groups
    request_ids = lax.dynamic_slice_in_dim(request_list, pair_index * slots, slots)
    matches = (
        request_ids[:, None] == jnp.arange(timesteps.shape[0], dtype=jnp.int32)[None, :]
    ).astype(jnp.int32)
    times = jnp.sum(matches[:, :, None] * timesteps[None], axis=1)
    step_size = (times[:, 1] - times[:, 0]).astype(jnp.float32) / 1000.0
    latent_next = latent[0] + step_size[:, None, None] * velocity

    next_stale = join_head(raw_in, zone_in, fresh.shape)
    for index, piece in enumerate(pieces):
        next_stale = restore(pairs[1], arrived[index], next_stale, piece, held[index + 2 : index + 3])
    return (next_stale[None], velocity[None], latent_next[None])


def solution(mesh):
    return jax.shard_map(
        shards,
        mesh=mesh,
        in_specs=(
            P("grp", None, None, "tp"),
            P("grp", None, None, None, "tp"),
            P("grp", None, None, None, "tp"),
            P("grp", None, None, None, "tp"),
            P("tp", None),
            P("grp", None, "tp", None),
            P(),
            P(),
            P(),
            P(),
        ),
        out_specs=(
            P("grp", None, None, None, "tp"),
            P("grp", None, "tp", None),
            P("grp", None, "tp", None),
        ),
        check_vma=False,
    )
```

```python
import functools
import math

import jax
import jax.numpy as jnp
from jax import lax
from jax.experimental import pallas as pl
from jax.experimental.pallas import tpu as pltpu
from jax.sharding import PartitionSpec as P

HD = 128
HBM = pltpu.MemorySpace.HBM
SMEM = pltpu.MemorySpace.SMEM
VMEM_LIMIT = 32 * 1024 * 1024
WIDE_LIMIT = 60 * 1024 * 1024


def from_behind(block, axis, distance):
    devices = range(lax.axis_size(axis))
    route = [((i - distance) % len(devices), i) for i in devices]
    return lax.ppermute(block, axis, route)


def swap_pairs(lists):
    count = lists.shape[2]
    zone = count + jnp.arange(count, dtype=jnp.int32)
    order = jnp.arange(count, dtype=jnp.int32)
    earlier = order[:, None] >= order[None, :]
    free = jnp.logical_not(jnp.any(lists[..., :, None] == zone, axis=2))
    outside = lists >= 2 * count
    free_rank = jnp.sum((earlier & free[..., None, :]).astype(jnp.int32), axis=3)
    outside_rank = jnp.sum((earlier & outside[..., None, :]).astype(jnp.int32), axis=3)
    match = (
        outside[..., :, None]
        & free[..., None, :]
        & (outside_rank[..., :, None] == free_rank[..., None, :])
    )
    near = jnp.sum(jnp.where(match, order, 0), axis=3)
    sources = jnp.sum(jnp.where(match, lists[..., :, None], 0), axis=2)
    return near, jnp.where(outside, lists, -1), jnp.where(sources > 0, sources, zone)


def swap_rows(pairs, slots, slot, zone, piece, start, stop):
    count = zone.shape[0] - 1

    def step(k, carry):
        far = pairs[(slots + slot) * count + k]
        here = jnp.logical_and(far >= start, far < stop)
        near_row = jnp.where(here, pairs[slot * count + k], count)
        far_row = jnp.where(here, far - start, stop - start)
        moved = zone[near_row]
        zone[near_row] = piece[far_row]
        piece[far_row] = moved
        return carry

    lax.fori_loop(0, count, step, 0, unroll=8)


def relay(copies, sems):
    inner = [pltpu.make_async_copy(c[0], c[1], sems.at[0, i]) for i, c in enumerate(copies)]
    outer = [pltpu.make_async_copy(c[1], c[2], sems.at[1, i]) for i, c in enumerate(copies)]
    for copy in inner:
        copy.start()
    for arrive, leave in zip(inner, outer):
        arrive.wait()
        leave.start()
    for copy in outer:
        copy.wait()


def arrange_kernel(slots, pieces, pairs_ref, fresh_ref, after_ref, *refs):
    zone_out, piece_outs = refs[0], refs[1 : 1 + len(pieces)]
    pairs, zones, rests, sems = refs[1 + len(pieces) :]
    count = zones.shape[1] - 1
    rest_rows = rests.shape[1] - 1
    copy_pairs = pltpu.make_async_copy(pairs_ref, pairs, sems.at[3 * slots + len(pieces)])
    copy_pairs.start()
    copies_in = []
    for slot in range(slots):
        copies_in.append(
            (
                pltpu.make_async_copy(
                    fresh_ref.at[0, slot, count : 2 * count], zones.at[slot, :count], sems.at[slot]
                ),
                pltpu.make_async_copy(
                    fresh_ref.at[0, slot, 2 * count :], rests.at[slot, :rest_rows], sems.at[slots + slot]
                ),
            )
        )
        for copy in copies_in[-1]:
            copy.start()
    copy_pairs.wait()
    copies_out = []
    for slot in range(slots):
        for copy in copies_in[slot]:
            copy.wait()
        swap_rows(pairs, slots, slot, zones.at[slot], rests.at[slot], 2 * count, 2 * count + rest_rows)
        copies_out.append(
            pltpu.make_async_copy(zones.at[slot, :count], zone_out.at[slot], sems.at[2 * slots + slot])
        )
        copies_out[-1].start()
        for index, (piece_slot, start, stop) in enumerate(pieces):
            if piece_slot == slot:
                source = rests.at[slot, start - 2 * count : stop - 2 * count]
                copies_out.append(
                    pltpu.make_async_copy(source, piece_outs[index], sems.at[3 * slots + index])
                )
                copies_out[-1].start()
    for copy in copies_out:
        copy.wait()


def arrange(pairs, fresh_kv, pieces, after):
    slots, rows = fresh_kv.shape[1:3]
    tail = fresh_kv.shape[3:]
    count = pairs.shape[0] // (2 * slots)
    outs = pl.pallas_call(
        functools.partial(arrange_kernel, slots, pieces),
        out_shape=[jax.ShapeDtypeStruct((slots, count) + tail, fresh_kv.dtype)]
        + [jax.ShapeDtypeStruct((stop - start,) + tail, fresh_kv.dtype) for _, start, stop in pieces],
        in_specs=[pl.BlockSpec(memory_space=HBM)] * 3,
        out_specs=[pl.BlockSpec(memory_space=HBM)] * (1 + len(pieces)),
        scratch_shapes=[
            pltpu.SMEM(pairs.shape, pairs.dtype),
            pltpu.VMEM((slots, count + 1) + tail, fresh_kv.dtype),
            pltpu.VMEM((slots, rows - 2 * count + 1) + tail, fresh_kv.dtype),
            pltpu.SemaphoreType.DMA((3 * slots + len(pieces) + 1,)),
        ],
        cost_estimate=pl.CostEstimate(flops=0, bytes_accessed=4 * fresh_kv.size, transcendentals=0),
        compiler_params=pltpu.CompilerParams(vmem_limit_bytes=WIDE_LIMIT),
        name="arrange",
    )(pairs, fresh_kv, after)
    return outs[0], outs[1:]


def join_kernel(raw_ref, zone_ref, out_ref, stage, sems):
    count = raw_ref.shape[1]
    relay(
        [
            (raw_ref, stage.at[0], out_ref.at[:, :count]),
            (zone_ref, stage.at[1], out_ref.at[:, count : 2 * count]),
        ],
        sems,
    )


def join_head(raw, zone, shape):
    return pl.pallas_call(
        join_kernel,
        out_shape=jax.ShapeDtypeStruct(shape, raw.dtype),
        in_specs=[pl.BlockSpec(memory_space=HBM)] * 2,
        out_specs=pl.BlockSpec(memory_space=HBM),
        scratch_shapes=[pltpu.VMEM((2,) + raw.shape, raw.dtype), pltpu.SemaphoreType.DMA((2, 2))],
        cost_estimate=pl.CostEstimate(flops=0, bytes_accessed=8 * raw.size, transcendentals=0),
        compiler_params=pltpu.CompilerParams(vmem_limit_bytes=VMEM_LIMIT),
        name="join_head",
    )(raw, zone)


def restore_kernel(slot, start, stop, pairs_ref, piece_ref, whole_ref, *refs):
    out_ref, pairs, zone, piece, sems = refs[-5:]
    count = zone.shape[0] - 1
    inner = [
        pltpu.make_async_copy(pairs_ref, pairs, sems.at[4]),
        pltpu.make_async_copy(piece_ref, piece.at[: stop - start], sems.at[0]),
        pltpu.make_async_copy(out_ref.at[slot, count : 2 * count], zone.at[:count], sems.at[1]),
    ]
    for copy in inner:
        copy.start()
    for copy in inner:
        copy.wait()
    swap_rows(pairs, out_ref.shape[0], slot, zone, piece, start, stop)
    outer = [
        pltpu.make_async_copy(piece.at[: stop - start], out_ref.at[slot, start:stop], sems.at[2]),
        pltpu.make_async_copy(zone.at[:count], out_ref.at[slot, count : 2 * count], sems.at[3]),
    ]
    for copy in outer:
        copy.start()
    for copy in outer:
        copy.wait()


def restore(pairs, block, whole, piece, after=()):
    slot, start, stop = piece
    tail = whole.shape[2:]
    count = pairs.shape[0] // (2 * whole.shape[0])
    return pl.pallas_call(
        functools.partial(restore_kernel, slot, start, stop),
        out_shape=jax.ShapeDtypeStruct(whole.shape, whole.dtype),
        in_specs=[pl.BlockSpec(memory_space=HBM)] * (3 + len(after)),
        out_specs=pl.BlockSpec(memory_space=HBM),
        scratch_shapes=[
            pltpu.SMEM(pairs.shape, pairs.dtype),
            pltpu.VMEM((count + 1,) + tail, whole.dtype),
            pltpu.VMEM((stop - start + 1,) + tail, whole.dtype),
            pltpu.SemaphoreType.DMA((5,)),
        ],
        input_output_aliases={2: 0},
        cost_estimate=pl.CostEstimate(flops=0, bytes_accessed=4 * block.size, transcendentals=0),
        compiler_params=pltpu.CompilerParams(vmem_limit_bytes=VMEM_LIMIT),
        name="restore",
    )(pairs, block, whole, *after)


def hold_kernel(block_ref, after_ref, out_ref):
    del block_ref, after_ref, out_ref


def hold(block, after):
    return pl.pallas_call(
        hold_kernel,
        out_shape=jax.ShapeDtypeStruct(block.shape, block.dtype),
        in_specs=[pl.BlockSpec(memory_space=HBM)] * 2,
        out_specs=pl.BlockSpec(memory_space=HBM),
        input_output_aliases={0: 0},
        cost_estimate=pl.CostEstimate(flops=0, bytes_accessed=0, transcendentals=0),
        name="hold",
    )(block, after)


def across(a, b):
    return lax.dot_general(a, b, (((1,), (1,)), ((), ())), preferred_element_type=jnp.float32)


def text_kernel(k_ref, v_ref, w_ref, after_ref, out_ref):
    rows = k_ref.shape[1]
    channels = w_ref.shape[0]
    out_ref[0, 0, :rows, :] = k_ref[0]
    projected = across(w_ref[...], v_ref[0]).astype(out_ref.dtype)
    for part in range(rows // HD):
        start = rows + part * channels
        out_ref[0, 0, start : start + channels, :] = projected[:, part * HD : (part + 1) * HD]


def project_text(keys, values, w_t, after):
    slots, rows, width = keys.shape
    heads = width // HD
    channels = w_t.shape[0]
    packed = rows + channels * rows // HD
    block = pl.BlockSpec((1, rows, HD), lambda s, h: (s, 0, h))
    return pl.pallas_call(
        text_kernel,
        grid=(slots, heads),
        out_shape=jax.ShapeDtypeStruct((slots, heads, packed, HD), keys.dtype),
        in_specs=[block, block, pl.BlockSpec((channels, HD), lambda s, h: (0, h)), pl.BlockSpec(memory_space=HBM)],
        out_specs=pl.BlockSpec((1, 1, packed, HD), lambda s, h: (s, h, 0, 0)),
        cost_estimate=pl.CostEstimate(
            flops=2 * slots * rows * width * channels, bytes_accessed=4 * keys.size * 2, transcendentals=0
        ),
        name="project_text",
    )(keys, values, w_t, after)


def attention_kernel(text_rows, *refs):
    (q_ref, kf_ref, vf_ref, ks_ref, vs_ref, kh_ref, vh_ref, own_ref, other_ref, w_ref, bias_ref) = refs[:11]
    out_ref, scores_ref = refs[11], refs[12]
    head = pl.program_id(1)
    query = q_ref[0]
    w_t = w_ref[...]
    channels = w_t.shape[0]
    scale = 1.0 / math.sqrt(HD)
    pieces = []
    for k_ref, v_ref in ((kf_ref, vf_ref), (ks_ref, vs_ref), (kh_ref, vh_ref)):
        rows = k_ref.shape[1]
        step = min(rows, 256)
        for start in range(0, rows, step):
            pieces.append((k_ref.at[0, start : start + step], v_ref.at[0, start : start + step], step))
    for t_ref in (own_ref, other_ref):
        pieces.append((t_ref.at[0, 0, :text_rows], t_ref, text_rows))
    top = None
    at = 0
    for k_ref, _, rows in pieces:
        scores = across(k_ref[...], query) * scale + bias_ref[0, at : at + rows]
        scores_ref[at : at + rows, :] = scores
        piece_top = jnp.max(scores, axis=0, keepdims=True)
        top = piece_top if top is None else jnp.maximum(top, piece_top)
        at += rows
    total = jnp.zeros_like(top)
    blended = jnp.zeros((channels, query.shape[0]), jnp.float32)
    at = 0
    for _, v_ref, rows in pieces:
        weights = jnp.exp(scores_ref[at : at + rows, :] - top)
        total += jnp.sum(weights, axis=0, keepdims=True)
        rounded = weights.astype(jnp.bfloat16)
        if v_ref.shape[-2] == rows and len(v_ref.shape) == 2:
            projected = across(w_t, v_ref[...]).astype(jnp.bfloat16)
            blended += jnp.dot(projected, rounded, preferred_element_type=jnp.float32)
        else:
            for part in range(rows // HD):
                start = rows + part * channels
                blended += jnp.dot(
                    v_ref[0, 0, start : start + channels, :],
                    rounded[part * HD : (part + 1) * HD],
                    preferred_element_type=jnp.float32,
                )
        at += rows
    term = blended / total

    @pl.when(head == 0)
    def _():
        out_ref[0] = term

    @pl.when(head != 0)
    def _():
        out_ref[0] += term


def attention(queries, fresh_k, fresh_v, stale_k, stale_v, hot_k, hot_v, text_own, text_other, w_t, bias):
    slots, rows, width = queries.shape
    heads = width // HD
    channels = w_t.shape[0]
    key_rows = bias.shape[1]
    text_rows = (text_own.shape[2] * HD) // (HD + channels)

    def wide(array):
        return pl.BlockSpec((1, array.shape[1], HD), lambda s, h: (s, 0, h))

    packed = pl.BlockSpec((1, 1) + text_own.shape[2:], lambda s, h: (s, h, 0, 0))
    many = slots * heads * rows * key_rows
    return pl.pallas_call(
        functools.partial(attention_kernel, text_rows),
        grid=(slots, heads),
        out_shape=jax.ShapeDtypeStruct((slots, channels, rows), jnp.float32),
        in_specs=[wide(a) for a in (queries, fresh_k, fresh_v, stale_k, stale_v, hot_k, hot_v)]
        + [
            packed,
            packed,
            pl.BlockSpec((channels, HD), lambda s, h: (0, h)),
            pl.BlockSpec((1, key_rows, 1), lambda s, h: (s, 0, 0)),
        ],
        out_specs=pl.BlockSpec((1, channels, rows), lambda s, h: (s, 0, 0)),
        scratch_shapes=[pltpu.VMEM((key_rows, rows), jnp.float32)],
        cost_estimate=pl.CostEstimate(
            flops=2 * many * (HD + channels), bytes_accessed=24 * 1024 * 1024, transcendentals=many
        ),
        compiler_params=pltpu.CompilerParams(vmem_limit_bytes=VMEM_LIMIT),
        name="attention",
    )(queries, fresh_k, fresh_v, stale_k, stale_v, hot_k, hot_v, text_own, text_other, w_t, bias)


def shards(
    queries,
    fresh_kv,
    stale_kv,
    text_kv,
    w_velocity,
    latent,
    live_counts,
    refresh_rows,
    request_list,
    timesteps,
):
    half_groups = lax.axis_size("grp") // 2
    my_group = lax.axis_index("grp")
    partner = (my_group + half_groups) % (2 * half_groups)
    queries, fresh, stale, text = queries[0], fresh_kv[0], stale_kv[0], text_kv[0]
    slots, img_rows = queries.shape[:2]
    listed_count = refresh_rows.shape[2]
    hot_rows = 2 * listed_count

    raw = fresh_kv[0, :, :listed_count]
    raw_in = from_behind(raw, "grp", half_groups)

    my_list = lax.dynamic_index_in_dim(refresh_rows, my_group, 0, keepdims=False)
    partner_list = lax.dynamic_index_in_dim(refresh_rows, partner, 0, keepdims=False)
    near, far, sources = swap_pairs(jnp.stack([my_list, partner_list]))
    pairs = jnp.stack([near, far], axis=1).reshape(2, -1)

    first_cut = hot_rows + (img_rows - hot_rows) * 5 // 8
    last_cut = img_rows - listed_count
    final = slots - 1
    pieces = [(slot, hot_rows, img_rows) for slot in range(final)]
    pieces += [(final, hot_rows, first_cut), (final, first_cut, last_cut), (final, last_cut, img_rows)]
    zone, blocks = arrange(pairs[0], fresh_kv, pieces, raw)
    zone_in = from_behind(zone, "grp", half_groups)
    w_t = w_velocity.T
    text_own = project_text(text[:, :, 0], text[:, :, 1], w_t, zone)
    text_in = from_behind(text_own, "grp", half_groups)
    arrived, held = [], []
    for index, block in enumerate(blocks):
        if index < final:
            gate = raw_in
        elif index == final:
            gate = text_in
        else:
            gate = arrived[index - 2]
        held.append(hold(block, gate))
        if index < final:
            round_about = half_groups + half_groups // 2
            arrived.append(from_behind(from_behind(held[-1], "grp", round_about), "grp", round_about))
        else:
            arrived.append(from_behind(held[-1], "grp", half_groups))

    my_live = lax.dynamic_index_in_dim(live_counts, my_group, 0, keepdims=False)
    partner_live = lax.dynamic_index_in_dim(live_counts, partner, 0, keepdims=False)
    row_ids = jnp.arange(img_rows, dtype=jnp.int32)
    hot_source = jnp.concatenate(
        [jnp.broadcast_to(row_ids[:listed_count], partner_list.shape), sources[1]], axis=1
    )
    stale_listed = jnp.any(partner_list[:, :, None] == row_ids, axis=1)
    hot_listed = jnp.any(partner_list[:, :, None] == hot_source[:, None, :], axis=1)
    live = jnp.concatenate(
        [
            row_ids < my_live[:, None],
            (row_ids < partner_live[:, None]) & jnp.logical_not(stale_listed),
            (hot_source < partner_live[:, None]) & hot_listed,
            jnp.ones((slots, 2 * text.shape[1]), dtype=bool),
        ],
        axis=1,
    )
    bias = jnp.where(live, 0.0, -jnp.inf).astype(jnp.float32)[:, :, None]
    hot = join_head(raw_in, zone_in, (slots, hot_rows) + fresh.shape[2:])
    partial = attention(
        queries,
        fresh[:, :, 0],
        fresh[:, :, 1],
        stale[:, :, 0],
        stale[:, :, 1],
        hot[:, :, 0],
        hot[:, :, 1],
        text_own,
        text_in,
        w_t,
        bias,
    )

    tp_count = lax.axis_size("tp")
    tp_index = lax.axis_index("tp")
    share = img_rows // tp_count
    if tp_count == 2:
        mine = lax.dynamic_slice_in_dim(partial, tp_index * share, share, 2)
        theirs = lax.dynamic_slice_in_dim(partial, (1 - tp_index) * share, share, 2)
        summed = mine + from_behind(theirs, "tp", 1)
    else:
        summed = lax.psum_scatter(partial, "tp", scatter_dimension=2, tiled=True)
    summed = jnp.swapaxes(summed, 1, 2)
    share_ids = tp_index * share + jnp.arange(share, dtype=jnp.int32)
    live_rows = share_ids[None, :] < my_live[:, None]
    velocity = jnp.where(live_rows[:, :, None], summed, 0.0)
    pair_index = my_group % half_groups
    request_ids = lax.dynamic_slice_in_dim(request_list, pair_index * slots, slots)
    matches = (
        request_ids[:, None] == jnp.arange(timesteps.shape[0], dtype=jnp.int32)[None, :]
    ).astype(jnp.int32)
    times = jnp.sum(matches[:, :, None] * timesteps[None], axis=1)
    step_size = (times[:, 1] - times[:, 0]).astype(jnp.float32) / 1000.0
    latent_next = latent[0] + step_size[:, None, None] * velocity

    next_stale = join_head(raw_in, zone_in, fresh.shape)
    for index, piece in enumerate(pieces):
        next_stale = restore(pairs[1], arrived[index], next_stale, piece, held[index + 2 : index + 3])
    return (next_stale[None], velocity[None], latent_next[None])


def solution(mesh):
    return jax.shard_map(
        shards,
        mesh=mesh,
        in_specs=(
            P("grp", None, None, "tp"),
            P("grp", None, None, None, "tp"),
            P("grp", None, None, None, "tp"),
            P("grp", None, None, None, "tp"),
            P("tp", None),
            P("grp", None, "tp", None),
            P(),
            P(),
            P(),
            P(),
        ),
        out_specs=(
            P("grp", None, None, None, "tp"),
            P("grp", None, "tp", None),
            P("grp", None, "tp", None),
        ),
        check_vma=False,
    )
```

```python
import functools
import math

import jax
import jax.numpy as jnp
from jax import lax
from jax.experimental import pallas as pl
from jax.experimental.pallas import tpu as pltpu
from jax.sharding import PartitionSpec as P

HD = 128
HBM = pltpu.MemorySpace.HBM
SMEM = pltpu.MemorySpace.SMEM
VMEM_LIMIT = 32 * 1024 * 1024
WIDE_LIMIT = 60 * 1024 * 1024


def from_behind(block, axis, distance):
    devices = range(lax.axis_size(axis))
    route = [((i - distance) % len(devices), i) for i in devices]
    return lax.ppermute(block, axis, route)


def swap_pairs(lists):
    count = lists.shape[2]
    zone = count + jnp.arange(count, dtype=jnp.int32)
    order = jnp.arange(count, dtype=jnp.int32)
    earlier = order[:, None] >= order[None, :]
    free = jnp.logical_not(jnp.any(lists[..., :, None] == zone, axis=2))
    outside = lists >= 2 * count
    free_rank = jnp.sum((earlier & free[..., None, :]).astype(jnp.int32), axis=3)
    outside_rank = jnp.sum((earlier & outside[..., None, :]).astype(jnp.int32), axis=3)
    match = (
        outside[..., :, None]
        & free[..., None, :]
        & (outside_rank[..., :, None] == free_rank[..., None, :])
    )
    near = jnp.sum(jnp.where(match, order, 0), axis=3)
    sources = jnp.sum(jnp.where(match, lists[..., :, None], 0), axis=2)
    return near, jnp.where(outside, lists, -1), jnp.where(sources > 0, sources, zone)


def swap_rows(pairs, slots, slot, zone, piece, start, stop):
    count = zone.shape[0] - 1

    def step(k, carry):
        far = pairs[(slots + slot) * count + k]
        here = jnp.logical_and(far >= start, far < stop)
        near_row = jnp.where(here, pairs[slot * count + k], count)
        far_row = jnp.where(here, far - start, stop - start)
        moved = zone[near_row]
        zone[near_row] = piece[far_row]
        piece[far_row] = moved
        return carry

    lax.fori_loop(0, count, step, 0, unroll=8)


def relay(copies, sems):
    inner = [pltpu.make_async_copy(c[0], c[1], sems.at[0, i]) for i, c in enumerate(copies)]
    outer = [pltpu.make_async_copy(c[1], c[2], sems.at[1, i]) for i, c in enumerate(copies)]
    for copy in inner:
        copy.start()
    for arrive, leave in zip(inner, outer):
        arrive.wait()
        leave.start()
    for copy in outer:
        copy.wait()


def arrange_kernel(slots, pieces, pairs_ref, fresh_ref, *refs):
    refs = refs[slots:]
    zone_outs, piece_outs = refs[:slots], refs[slots : slots + len(pieces)]
    pairs, zones, rests, sems = refs[slots + len(pieces) :]
    count = zones.shape[1] - 1
    rest_rows = rests.shape[1] - 1
    copy_pairs = pltpu.make_async_copy(pairs_ref, pairs, sems.at[3 * slots + len(pieces)])
    copy_pairs.start()
    copies_in = []
    for slot in range(slots):
        copies_in.append(
            (
                pltpu.make_async_copy(
                    fresh_ref.at[0, slot, count : 2 * count], zones.at[slot, :count], sems.at[slot]
                ),
                pltpu.make_async_copy(
                    fresh_ref.at[0, slot, 2 * count :], rests.at[slot, :rest_rows], sems.at[slots + slot]
                ),
            )
        )
        for copy in copies_in[-1]:
            copy.start()
    copy_pairs.wait()
    copies_out = []
    for slot in range(slots):
        for copy in copies_in[slot]:
            copy.wait()
        swap_rows(pairs, slots, slot, zones.at[slot], rests.at[slot], 2 * count, 2 * count + rest_rows)
        copies_out.append(
            pltpu.make_async_copy(zones.at[slot, :count], zone_outs[slot], sems.at[2 * slots + slot])
        )
        copies_out[-1].start()
        for index, (piece_slot, start, stop) in enumerate(pieces):
            if piece_slot == slot:
                source = rests.at[slot, start - 2 * count : stop - 2 * count]
                copies_out.append(
                    pltpu.make_async_copy(source, piece_outs[index], sems.at[3 * slots + index])
                )
                copies_out[-1].start()
    for copy in copies_out:
        copy.wait()


def arrange(pairs, fresh_kv, pieces, after):
    slots, rows = fresh_kv.shape[1:3]
    tail = fresh_kv.shape[3:]
    count = pairs.shape[0] // (2 * slots)
    outs = pl.pallas_call(
        functools.partial(arrange_kernel, slots, pieces),
        out_shape=[jax.ShapeDtypeStruct((count,) + tail, fresh_kv.dtype)] * slots
        + [jax.ShapeDtypeStruct((stop - start,) + tail, fresh_kv.dtype) for _, start, stop in pieces],
        in_specs=[pl.BlockSpec(memory_space=HBM)] * (2 + slots),
        out_specs=[pl.BlockSpec(memory_space=HBM)] * (slots + len(pieces)),
        scratch_shapes=[
            pltpu.SMEM(pairs.shape, pairs.dtype),
            pltpu.VMEM((slots, count + 1) + tail, fresh_kv.dtype),
            pltpu.VMEM((slots, rows - 2 * count + 1) + tail, fresh_kv.dtype),
            pltpu.SemaphoreType.DMA((3 * slots + len(pieces) + 1,)),
        ],
        cost_estimate=pl.CostEstimate(flops=0, bytes_accessed=4 * fresh_kv.size, transcendentals=0),
        compiler_params=pltpu.CompilerParams(vmem_limit_bytes=WIDE_LIMIT),
        name="arrange",
    )(pairs, fresh_kv, *after)
    return outs[:slots], outs[slots:]


def join_kernel(places, *refs):
    count = len(places)
    out_ref, stage, sems = refs[count:]
    rows = stage.shape[1]
    targets = [out_ref.at[slot, start : start + rows] for slot, start in places]
    inner = [pltpu.make_async_copy(refs[i], stage.at[i], sems.at[i]) for i in range(count)]
    outer = [pltpu.make_async_copy(stage.at[i], targets[i], sems.at[count + i]) for i in range(count)]
    for copy in inner:
        copy.start()
    for arrive, leave in zip(inner, outer):
        arrive.wait()
        leave.start()
    for copy in outer:
        copy.wait()


def join_head(blocks, places, shape):
    block = blocks[0]
    return pl.pallas_call(
        functools.partial(join_kernel, places),
        out_shape=jax.ShapeDtypeStruct(shape, block.dtype),
        in_specs=[pl.BlockSpec(memory_space=HBM)] * len(blocks),
        out_specs=pl.BlockSpec(memory_space=HBM),
        scratch_shapes=[
            pltpu.VMEM((len(blocks),) + block.shape, block.dtype),
            pltpu.SemaphoreType.DMA((2 * len(blocks),)),
        ],
        cost_estimate=pl.CostEstimate(
            flops=0, bytes_accessed=4 * len(blocks) * block.size, transcendentals=0
        ),
        compiler_params=pltpu.CompilerParams(vmem_limit_bytes=VMEM_LIMIT),
        name="join_head",
    )(*blocks)


def restore_kernel(pieces, pairs_ref, *refs):
    number = len(pieces)
    piece_refs = refs[:number]
    out_ref, pairs, zones, stage, sems = refs[-5:]
    slots = out_ref.shape[0]
    count = zones.shape[1] - 1
    copy_pairs = pltpu.make_async_copy(pairs_ref, pairs, sems.at[4 * number])
    copy_pairs.start()
    inner, outer = [], []
    for i, (slot, start, stop) in enumerate(pieces):
        block, head = stage.at[i, : stop - start], zones.at[i, :count]
        head_out = out_ref.at[slot, count : 2 * count]
        inner.append(pltpu.make_async_copy(piece_refs[i], block, sems.at[4 * i]))
        inner.append(pltpu.make_async_copy(head_out, head, sems.at[4 * i + 1]))
        outer.append(pltpu.make_async_copy(block, out_ref.at[slot, start:stop], sems.at[4 * i + 2]))
        outer.append(pltpu.make_async_copy(head, head_out, sems.at[4 * i + 3]))
    for copy in inner:
        copy.start()
    copy_pairs.wait()
    for i, (slot, start, stop) in enumerate(pieces):
        inner[2 * i].wait()
        inner[2 * i + 1].wait()
        swap_rows(pairs, slots, slot, zones.at[i], stage.at[i], start, stop)
        outer[2 * i].start()
        outer[2 * i + 1].start()
    for copy in outer:
        copy.wait()


def restore(pairs, blocks, whole, pieces):
    tail = whole.shape[2:]
    number = len(pieces)
    count = pairs.shape[0] // (2 * whole.shape[0])
    rows = max(stop - start for _, start, stop in pieces)
    return pl.pallas_call(
        functools.partial(restore_kernel, pieces),
        out_shape=jax.ShapeDtypeStruct(whole.shape, whole.dtype),
        in_specs=[pl.BlockSpec(memory_space=HBM)] * (2 + number),
        out_specs=pl.BlockSpec(memory_space=HBM),
        scratch_shapes=[
            pltpu.SMEM(pairs.shape, pairs.dtype),
            pltpu.VMEM((number, count + 1) + tail, whole.dtype),
            pltpu.VMEM((number, rows + 1) + tail, whole.dtype),
            pltpu.SemaphoreType.DMA((4 * number + 1,)),
        ],
        input_output_aliases={1 + number: 0},
        cost_estimate=pl.CostEstimate(
            flops=0, bytes_accessed=4 * number * blocks[0].size, transcendentals=0
        ),
        compiler_params=pltpu.CompilerParams(vmem_limit_bytes=VMEM_LIMIT),
        name="restore",
    )(pairs, *blocks, whole)


def hold_kernel(block_ref, after_ref, out_ref):
    del block_ref, after_ref, out_ref


def hold(block, after):
    return pl.pallas_call(
        hold_kernel,
        out_shape=jax.ShapeDtypeStruct(block.shape, block.dtype),
        in_specs=[pl.BlockSpec(memory_space=HBM)] * 2,
        out_specs=pl.BlockSpec(memory_space=HBM),
        input_output_aliases={0: 0},
        cost_estimate=pl.CostEstimate(flops=0, bytes_accessed=0, transcendentals=0),
        name="hold",
    )(block, after)


def across(a, b):
    return lax.dot_general(a, b, (((1,), (1,)), ((), ())), preferred_element_type=jnp.float32)


def text_kernel(k_ref, v_ref, w_ref, after_ref, out_ref):
    rows, width = k_ref.shape
    channels = w_ref.shape[0]
    for head in range(width // HD):
        columns = slice(head * HD, (head + 1) * HD)
        out_ref[head, :rows, :] = k_ref[:, columns]
        projected = across(w_ref[:, columns], v_ref[:, columns]).astype(out_ref.dtype)
        for part in range(rows // HD):
            start = rows + part * channels
            out_ref[head, start : start + channels, :] = projected[:, part * HD : (part + 1) * HD]


def project_text(keys, values, w_t, after):
    rows, width = keys.shape
    heads = width // HD
    channels = w_t.shape[0]
    packed = rows + channels * rows // HD
    return pl.pallas_call(
        text_kernel,
        out_shape=jax.ShapeDtypeStruct((heads, packed, HD), keys.dtype),
        in_specs=[pl.BlockSpec(memory_space=pltpu.VMEM)] * 3 + [pl.BlockSpec(memory_space=HBM)],
        out_specs=pl.BlockSpec(memory_space=pltpu.VMEM),
        cost_estimate=pl.CostEstimate(
            flops=2 * rows * width * channels, bytes_accessed=4 * keys.size * 2, transcendentals=0
        ),
        compiler_params=pltpu.CompilerParams(vmem_limit_bytes=VMEM_LIMIT),
        name="project_text",
    )(keys, values, w_t, after)


def attention_kernel(text_rows, *refs):
    (q_ref, kf_ref, vf_ref, ks_ref, vs_ref, kh_ref, vh_ref, own_ref, other_ref, w_ref, bias_ref) = refs[:11]
    out_ref, scores_ref = refs[11], refs[12]
    head = pl.program_id(0)
    query = q_ref[...]
    w_t = w_ref[...]
    channels = w_t.shape[0]
    scale = 1.0 / math.sqrt(HD)
    pieces = []
    for k_ref, v_ref in ((kf_ref, vf_ref), (ks_ref, vs_ref), (kh_ref, vh_ref)):
        rows = k_ref.shape[0]
        step = min(rows, 256)
        for start in range(0, rows, step):
            pieces.append((k_ref.at[start : start + step], v_ref.at[start : start + step], step))
    for t_ref in (own_ref, other_ref):
        pieces.append((t_ref.at[0, :text_rows], t_ref, text_rows))
    top = None
    at = 0
    for k_ref, _, rows in pieces:
        scores = across(k_ref[...], query) * scale + bias_ref[at : at + rows]
        scores_ref[at : at + rows, :] = scores
        piece_top = jnp.max(scores, axis=0, keepdims=True)
        top = piece_top if top is None else jnp.maximum(top, piece_top)
        at += rows
    total = jnp.zeros_like(top)
    blended = jnp.zeros((channels, query.shape[0]), jnp.float32)
    at = 0
    for _, v_ref, rows in pieces:
        weights = jnp.exp(scores_ref[at : at + rows, :] - top)
        total += jnp.sum(weights, axis=0, keepdims=True)
        rounded = weights.astype(jnp.bfloat16)
        if v_ref.shape[-2] == rows and len(v_ref.shape) == 2:
            projected = across(w_t, v_ref[...]).astype(jnp.bfloat16)
            blended += jnp.dot(projected, rounded, preferred_element_type=jnp.float32)
        else:
            for part in range(rows // HD):
                start = rows + part * channels
                blended += jnp.dot(
                    v_ref[0, start : start + channels, :],
                    rounded[part * HD : (part + 1) * HD],
                    preferred_element_type=jnp.float32,
                )
        at += rows
    term = blended / total

    @pl.when(head == 0)
    def _():
        out_ref[...] = term

    @pl.when(head != 0)
    def _():
        out_ref[...] += term


def attention(queries, fresh_k, fresh_v, stale_k, stale_v, hot_k, hot_v, text_own, text_other, w_t, bias):
    rows, width = queries.shape
    heads = width // HD
    channels = w_t.shape[0]
    key_rows = bias.shape[0]
    text_rows = (text_own.shape[1] * HD) // (HD + channels)

    def wide(array):
        return pl.BlockSpec((array.shape[0], HD), lambda h: (0, h))

    packed = pl.BlockSpec((1,) + text_own.shape[1:], lambda h: (h, 0, 0))
    many = heads * rows * key_rows
    return pl.pallas_call(
        functools.partial(attention_kernel, text_rows),
        grid=(heads,),
        out_shape=jax.ShapeDtypeStruct((channels, rows), jnp.float32),
        in_specs=[wide(a) for a in (queries, fresh_k, fresh_v, stale_k, stale_v, hot_k, hot_v)]
        + [
            packed,
            packed,
            pl.BlockSpec((channels, HD), lambda h: (0, h)),
            pl.BlockSpec((key_rows, 1), lambda h: (0, 0)),
        ],
        out_specs=pl.BlockSpec((channels, rows), lambda h: (0, 0)),
        scratch_shapes=[pltpu.VMEM((key_rows, rows), jnp.float32)],
        cost_estimate=pl.CostEstimate(
            flops=2 * many * (HD + channels), bytes_accessed=12 * 1024 * 1024, transcendentals=many
        ),
        compiler_params=pltpu.CompilerParams(vmem_limit_bytes=VMEM_LIMIT),
        name="attention",
    )(queries, fresh_k, fresh_v, stale_k, stale_v, hot_k, hot_v, text_own, text_other, w_t, bias)


def shards(
    queries,
    fresh_kv,
    stale_kv,
    text_kv,
    w_velocity,
    latent,
    live_counts,
    refresh_rows,
    request_list,
    timesteps,
):
    half_groups = lax.axis_size("grp") // 2
    my_group = lax.axis_index("grp")
    partner = (my_group + half_groups) % (2 * half_groups)
    queries, fresh, stale, text = queries[0], fresh_kv[0], stale_kv[0], text_kv[0]
    slots, img_rows = queries.shape[:2]
    listed_count = refresh_rows.shape[2]
    hot_rows = 2 * listed_count

    both = range(slots)

    def pass_on(block, slot):
        if half_groups != 8:
            return [from_behind(block, "grp", half_groups)]
        step = half_groups // 2 if slot % 2 == 0 else half_groups + half_groups // 2
        first = from_behind(block, "grp", step)
        return [first, from_behind(first, "grp", step)]

    raw = [fresh_kv[0, slot, :listed_count] for slot in both]
    raw_way = [pass_on(raw[slot], slot) for slot in both]

    my_list = lax.dynamic_index_in_dim(refresh_rows, my_group, 0, keepdims=False)
    partner_list = lax.dynamic_index_in_dim(refresh_rows, partner, 0, keepdims=False)
    near, far, sources = swap_pairs(jnp.stack([my_list, partner_list]))
    pairs = jnp.stack([near, far], axis=1).reshape(2, -1)

    rest = img_rows - hot_rows
    cuts = [hot_rows, hot_rows + rest // 2, img_rows - listed_count, img_rows]
    layers = [[(slot, start, stop) for slot in both] for start, stop in zip(cuts[:-1], cuts[1:])]
    zone, blocks = arrange(pairs[0], fresh_kv, sum(layers, []), raw)
    zone_way = [pass_on(zone[slot], slot) for slot in both]
    w_t = w_velocity.T
    text_own = [project_text(text[slot, :, 0], text[slot, :, 1], w_t, zone[slot]) for slot in both]
    text_way = [pass_on(text_own[slot], slot) for slot in both]
    layer_way = []
    for index in range(len(layers)):
        ways = []
        for slot in both:
            gate = (text_way[slot][0], text_way[slot][-1], None)[index]
            if gate is None:
                gate = layer_way[index - 1][slot][0]
            ways.append(pass_on(hold(blocks[index * slots + slot], gate), slot))
        layer_way.append(ways)

    my_live = lax.dynamic_index_in_dim(live_counts, my_group, 0, keepdims=False)
    partner_live = lax.dynamic_index_in_dim(live_counts, partner, 0, keepdims=False)
    row_ids = jnp.arange(img_rows, dtype=jnp.int32)
    hot_source = jnp.concatenate(
        [jnp.broadcast_to(row_ids[:listed_count], partner_list.shape), sources[1]], axis=1
    )
    stale_listed = jnp.any(partner_list[:, :, None] == row_ids, axis=1)
    hot_listed = jnp.any(partner_list[:, :, None] == hot_source[:, None, :], axis=1)
    live = jnp.concatenate(
        [
            row_ids < my_live[:, None],
            (row_ids < partner_live[:, None]) & jnp.logical_not(stale_listed),
            (hot_source < partner_live[:, None]) & hot_listed,
            jnp.ones((slots, 2 * text.shape[1]), dtype=bool),
        ],
        axis=1,
    )
    bias = jnp.where(live, 0.0, -jnp.inf).astype(jnp.float32)[:, :, None]
    partials = []
    for slot in both:
        hot = join_head(
            [raw_way[slot][-1], zone_way[slot][-1]], [(0, 0), (0, listed_count)], (1, hot_rows) + fresh.shape[2:]
        )
        partials.append(
            attention(
                queries[slot],
                fresh[slot, :, 0],
                fresh[slot, :, 1],
                stale[slot, :, 0],
                stale[slot, :, 1],
                hot[0, :, 0],
                hot[0, :, 1],
                text_own[slot],
                text_way[slot][-1],
                w_t,
                bias[slot],
            )
        )
    partial = jnp.stack(partials)

    tp_count = lax.axis_size("tp")
    tp_index = lax.axis_index("tp")
    share = img_rows // tp_count
    if tp_count == 2:
        mine = lax.dynamic_slice_in_dim(partial, tp_index * share, share, 2)
        theirs = lax.dynamic_slice_in_dim(partial, (1 - tp_index) * share, share, 2)
        summed = mine + from_behind(theirs, "tp", 1)
    else:
        summed = lax.psum_scatter(partial, "tp", scatter_dimension=2, tiled=True)
    summed = jnp.swapaxes(summed, 1, 2)
    share_ids = tp_index * share + jnp.arange(share, dtype=jnp.int32)
    live_rows = share_ids[None, :] < my_live[:, None]
    velocity = jnp.where(live_rows[:, :, None], summed, 0.0)
    pair_index = my_group % half_groups
    request_ids = lax.dynamic_slice_in_dim(request_list, pair_index * slots, slots)
    matches = (
        request_ids[:, None] == jnp.arange(timesteps.shape[0], dtype=jnp.int32)[None, :]
    ).astype(jnp.int32)
    times = jnp.sum(matches[:, :, None] * timesteps[None], axis=1)
    step_size = (times[:, 1] - times[:, 0]).astype(jnp.float32) / 1000.0
    latent_next = latent[0] + step_size[:, None, None] * velocity

    next_stale = join_head(
        [raw_way[slot][-1] for slot in both] + [zone_way[slot][-1] for slot in both],
        [(slot, 0) for slot in both] + [(slot, listed_count) for slot in both],
        fresh.shape,
    )
    for pieces, ways in zip(layers, layer_way):
        next_stale = restore(pairs[1], [way[-1] for way in ways], next_stale, pieces)
    return (next_stale[None], velocity[None], latent_next[None])


def solution(mesh):
    return jax.shard_map(
        shards,
        mesh=mesh,
        in_specs=(
            P("grp", None, None, "tp"),
            P("grp", None, None, None, "tp"),
            P("grp", None, None, None, "tp"),
            P("grp", None, None, None, "tp"),
            P("tp", None),
            P("grp", None, "tp", None),
            P(),
            P(),
            P(),
            P(),
        ),
        out_specs=(
            P("grp", None, None, None, "tp"),
            P("grp", None, "tp", None),
            P("grp", None, "tp", None),
        ),
        check_vma=False,
    )
```

```python
import functools
import math

import jax
import jax.numpy as jnp
from jax import lax
from jax.experimental import pallas as pl
from jax.experimental.pallas import tpu as pltpu
from jax.sharding import PartitionSpec as P

HD = 128
HBM = pltpu.MemorySpace.HBM
SMEM = pltpu.MemorySpace.SMEM
VMEM_LIMIT = 32 * 1024 * 1024
WIDE_LIMIT = 60 * 1024 * 1024


def from_behind(block, axis, distance):
    devices = range(lax.axis_size(axis))
    route = [((i - distance) % len(devices), i) for i in devices]
    return lax.ppermute(block, axis, route)


def swap_pairs(lists):
    count = lists.shape[2]
    zone = count + jnp.arange(count, dtype=jnp.int32)
    order = jnp.arange(count, dtype=jnp.int32)
    earlier = order[:, None] >= order[None, :]
    free = jnp.logical_not(jnp.any(lists[..., :, None] == zone, axis=2))
    outside = lists >= 2 * count
    free_rank = jnp.sum((earlier & free[..., None, :]).astype(jnp.int32), axis=3)
    outside_rank = jnp.sum((earlier & outside[..., None, :]).astype(jnp.int32), axis=3)
    match = (
        outside[..., :, None]
        & free[..., None, :]
        & (outside_rank[..., :, None] == free_rank[..., None, :])
    )
    near = jnp.sum(jnp.where(match, order, 0), axis=3)
    sources = jnp.sum(jnp.where(match, lists[..., :, None], 0), axis=2)
    return near, jnp.where(outside, lists, -1), jnp.where(sources > 0, sources, zone)


def swap_rows(pairs, slots, slot, zone, piece, start, stop):
    count = zone.shape[0] - 1

    def step(k, carry):
        far = pairs[(slots + slot) * count + k]
        here = jnp.logical_and(far >= start, far < stop)
        near_row = jnp.where(here, pairs[slot * count + k], count)
        far_row = jnp.where(here, far - start, stop - start)
        moved = zone[near_row]
        zone[near_row] = piece[far_row]
        piece[far_row] = moved
        return carry

    lax.fori_loop(0, count, step, 0, unroll=8)


def relay(copies, sems):
    inner = [pltpu.make_async_copy(c[0], c[1], sems.at[0, i]) for i, c in enumerate(copies)]
    outer = [pltpu.make_async_copy(c[1], c[2], sems.at[1, i]) for i, c in enumerate(copies)]
    for copy in inner:
        copy.start()
    for arrive, leave in zip(inner, outer):
        arrive.wait()
        leave.start()
    for copy in outer:
        copy.wait()


def arrange_kernel(slots, pieces, pairs_ref, fresh_ref, after_ref, *refs):
    zone_out, piece_outs = refs[0], refs[1 : 1 + len(pieces)]
    pairs, zones, rests, sems = refs[1 + len(pieces) :]
    count = zones.shape[1] - 1
    rest_rows = rests.shape[1] - 1
    copy_pairs = pltpu.make_async_copy(pairs_ref, pairs, sems.at[3 * slots + len(pieces)])
    copy_pairs.start()
    copies_in = []
    for slot in range(slots):
        copies_in.append(
            (
                pltpu.make_async_copy(
                    fresh_ref.at[0, slot, count : 2 * count], zones.at[slot, :count], sems.at[slot]
                ),
                pltpu.make_async_copy(
                    fresh_ref.at[0, slot, 2 * count :], rests.at[slot, :rest_rows], sems.at[slots + slot]
                ),
            )
        )
        for copy in copies_in[-1]:
            copy.start()
    copy_pairs.wait()
    copies_out = []
    for slot in range(slots):
        for copy in copies_in[slot]:
            copy.wait()
        swap_rows(pairs, slots, slot, zones.at[slot], rests.at[slot], 2 * count, 2 * count + rest_rows)
        copies_out.append(
            pltpu.make_async_copy(zones.at[slot, :count], zone_out.at[slot], sems.at[2 * slots + slot])
        )
        copies_out[-1].start()
        for index, (piece_slot, start, stop) in enumerate(pieces):
            if piece_slot == slot:
                source = rests.at[slot, start - 2 * count : stop - 2 * count]
                copies_out.append(
                    pltpu.make_async_copy(source, piece_outs[index], sems.at[3 * slots + index])
                )
                copies_out[-1].start()
    for copy in copies_out:
        copy.wait()


def arrange(pairs, fresh_kv, pieces, after):
    slots, rows = fresh_kv.shape[1:3]
    tail = fresh_kv.shape[3:]
    count = pairs.shape[0] // (2 * slots)
    outs = pl.pallas_call(
        functools.partial(arrange_kernel, slots, pieces),
        out_shape=[jax.ShapeDtypeStruct((slots, count) + tail, fresh_kv.dtype)]
        + [jax.ShapeDtypeStruct((stop - start,) + tail, fresh_kv.dtype) for _, start, stop in pieces],
        in_specs=[pl.BlockSpec(memory_space=HBM)] * 3,
        out_specs=[pl.BlockSpec(memory_space=HBM)] * (1 + len(pieces)),
        scratch_shapes=[
            pltpu.SMEM(pairs.shape, pairs.dtype),
            pltpu.VMEM((slots, count + 1) + tail, fresh_kv.dtype),
            pltpu.VMEM((slots, rows - 2 * count + 1) + tail, fresh_kv.dtype),
            pltpu.SemaphoreType.DMA((3 * slots + len(pieces) + 1,)),
        ],
        cost_estimate=pl.CostEstimate(flops=0, bytes_accessed=4 * fresh_kv.size, transcendentals=0),
        compiler_params=pltpu.CompilerParams(vmem_limit_bytes=WIDE_LIMIT),
        name="arrange",
    )(pairs, fresh_kv, after)
    return outs[0], outs[1:]


def join_kernel(raw_ref, zone_ref, out_ref, stage, sems):
    count = raw_ref.shape[1]
    relay(
        [
            (raw_ref, stage.at[0], out_ref.at[:, :count]),
            (zone_ref, stage.at[1], out_ref.at[:, count : 2 * count]),
        ],
        sems,
    )


def join_head(raw, zone, shape):
    return pl.pallas_call(
        join_kernel,
        out_shape=jax.ShapeDtypeStruct(shape, raw.dtype),
        in_specs=[pl.BlockSpec(memory_space=HBM)] * 2,
        out_specs=pl.BlockSpec(memory_space=HBM),
        scratch_shapes=[pltpu.VMEM((2,) + raw.shape, raw.dtype), pltpu.SemaphoreType.DMA((2, 2))],
        cost_estimate=pl.CostEstimate(flops=0, bytes_accessed=8 * raw.size, transcendentals=0),
        compiler_params=pltpu.CompilerParams(vmem_limit_bytes=VMEM_LIMIT),
        name="join_head",
    )(raw, zone)


def restore_kernel(slot, start, stop, groups, pairs_ref, end_ref, middle_ref, whole_ref, *refs):
    out_ref, pairs, zone, piece, sems = refs[-5:]
    count = zone.shape[0] - 1
    inner = [
        pltpu.make_async_copy(pairs_ref, pairs, sems.at[4]),
        pltpu.make_async_copy(out_ref.at[slot, count : 2 * count], zone.at[:count], sems.at[1]),
    ]
    for copy in inner:
        copy.start()
    from_end = pltpu.make_async_copy(end_ref, piece.at[: stop - start], sems.at[0])
    from_middle = pltpu.make_async_copy(middle_ref, piece.at[: stop - start], sems.at[0])
    middle = on_the_way(groups)

    @pl.when(middle)
    def _():
        from_middle.start()

    @pl.when(jnp.logical_not(middle))
    def _():
        from_end.start()

    inner.append(from_end)
    for copy in inner:
        copy.wait()
    swap_rows(pairs, out_ref.shape[0], slot, zone, piece, start, stop)
    outer = [
        pltpu.make_async_copy(piece.at[: stop - start], out_ref.at[slot, start:stop], sems.at[2]),
        pltpu.make_async_copy(zone.at[:count], out_ref.at[slot, count : 2 * count], sems.at[3]),
    ]
    for copy in outer:
        copy.start()
    for copy in outer:
        copy.wait()


def restore(pairs, ways, whole, piece, groups, after=()):
    slot, start, stop = piece
    tail = whole.shape[2:]
    count = pairs.shape[0] // (2 * whole.shape[0])
    return pl.pallas_call(
        functools.partial(restore_kernel, slot, start, stop, groups),
        out_shape=jax.ShapeDtypeStruct(whole.shape, whole.dtype),
        in_specs=[pl.BlockSpec(memory_space=HBM)] * (4 + len(after)),
        out_specs=pl.BlockSpec(memory_space=HBM),
        scratch_shapes=[
            pltpu.SMEM(pairs.shape, pairs.dtype),
            pltpu.VMEM((count + 1,) + tail, whole.dtype),
            pltpu.VMEM((stop - start + 1,) + tail, whole.dtype),
            pltpu.SemaphoreType.DMA((5,)),
        ],
        input_output_aliases={3: 0},
        cost_estimate=pl.CostEstimate(flops=0, bytes_accessed=4 * ways[1].size, transcendentals=0),
        compiler_params=pltpu.CompilerParams(vmem_limit_bytes=VMEM_LIMIT),
        name="restore",
    )(pairs, ways[1], ways[2], whole, *after)


def on_the_way(groups):
    place = lax.axis_index("grp") // (groups // 4)
    return jnp.logical_or(place == 1, place == 2)


def either_kernel(groups, end_ref, middle_ref, out_ref, stage, sems):
    middle = on_the_way(groups)
    from_end = pltpu.make_async_copy(end_ref, stage, sems.at[0])
    from_middle = pltpu.make_async_copy(middle_ref, stage, sems.at[0])

    @pl.when(middle)
    def _():
        from_middle.start()

    @pl.when(jnp.logical_not(middle))
    def _():
        from_end.start()

    from_end.wait()
    leave = pltpu.make_async_copy(stage, out_ref, sems.at[1])
    leave.start()
    leave.wait()


def either(end_block, middle_block, groups):
    return pl.pallas_call(
        functools.partial(either_kernel, groups),
        out_shape=jax.ShapeDtypeStruct(end_block.shape, end_block.dtype),
        in_specs=[pl.BlockSpec(memory_space=HBM)] * 2,
        out_specs=pl.BlockSpec(memory_space=HBM),
        scratch_shapes=[pltpu.VMEM(end_block.shape, end_block.dtype), pltpu.SemaphoreType.DMA((2,))],
        cost_estimate=pl.CostEstimate(flops=0, bytes_accessed=4 * end_block.size, transcendentals=0),
        compiler_params=pltpu.CompilerParams(vmem_limit_bytes=VMEM_LIMIT),
        name="either",
    )(end_block, middle_block)


def swap_along(block, groups, couples):
    quarter = groups // 4
    route = []
    for one, other in couples:
        for i in range(quarter):
            route.append((one * quarter + i, other * quarter + i))
            route.append((other * quarter + i, one * quarter + i))
    return lax.ppermute(block, "grp", route)


def pass_along(block, groups):
    if groups != 16:
        direct = from_behind(block, "grp", groups // 2)
        return direct, direct, direct
    crossed = swap_along(block, groups, [(1, 2)])
    outer = swap_along(either(block, crossed, groups), groups, [(0, 1), (2, 3)])
    return crossed, outer, swap_along(outer, groups, [(1, 2)])


def arrived_block(ways, groups):
    return ways[1] if groups != 16 else either(ways[1], ways[2], groups)


def hold_kernel(block_ref, after_ref, out_ref):
    del block_ref, after_ref, out_ref


def hold(block, after):
    return pl.pallas_call(
        hold_kernel,
        out_shape=jax.ShapeDtypeStruct(block.shape, block.dtype),
        in_specs=[pl.BlockSpec(memory_space=HBM)] * 2,
        out_specs=pl.BlockSpec(memory_space=HBM),
        input_output_aliases={0: 0},
        cost_estimate=pl.CostEstimate(flops=0, bytes_accessed=0, transcendentals=0),
        name="hold",
    )(block, after)


def across(a, b):
    return lax.dot_general(a, b, (((1,), (1,)), ((), ())), preferred_element_type=jnp.float32)


def text_kernel(k_ref, v_ref, w_ref, *refs):
    out_ref = refs[-1]
    slots, rows, width = k_ref.shape
    channels = w_ref.shape[0]
    for slot in range(slots):
        for head in range(width // HD):
            columns = slice(head * HD, (head + 1) * HD)
            out_ref[slot, head, :rows, :] = k_ref[slot, :, columns]
            projected = across(w_ref[:, columns], v_ref[slot, :, columns]).astype(out_ref.dtype)
            for part in range(rows // HD):
                start = rows + part * channels
                out_ref[slot, head, start : start + channels, :] = projected[:, part * HD : (part + 1) * HD]


def project_text(keys, values, w_t, after):
    slots, rows, width = keys.shape
    heads = width // HD
    channels = w_t.shape[0]
    packed = rows + channels * rows // HD
    return pl.pallas_call(
        text_kernel,
        out_shape=jax.ShapeDtypeStruct((slots, heads, packed, HD), keys.dtype),
        in_specs=[pl.BlockSpec(memory_space=pltpu.VMEM)] * 3
        + [pl.BlockSpec(memory_space=HBM)] * len(after),
        out_specs=pl.BlockSpec(memory_space=pltpu.VMEM),
        cost_estimate=pl.CostEstimate(
            flops=2 * slots * rows * width * channels, bytes_accessed=4 * keys.size * 2, transcendentals=0
        ),
        compiler_params=pltpu.CompilerParams(vmem_limit_bytes=VMEM_LIMIT),
        name="project_text",
    )(keys, values, w_t, *after)


def attention_kernel(text_rows, *refs):
    (q_ref, kf_ref, vf_ref, ks_ref, vs_ref, kh_ref, vh_ref, own_ref, other_ref, w_ref, bias_ref) = refs[:11]
    out_ref, scores_ref = refs[11], refs[12]
    head = pl.program_id(1)
    query = q_ref[0]
    w_t = w_ref[...]
    channels = w_t.shape[0]
    scale = 1.0 / math.sqrt(HD)
    pieces = []
    for k_ref, v_ref in ((kf_ref, vf_ref), (ks_ref, vs_ref), (kh_ref, vh_ref)):
        rows = k_ref.shape[1]
        step = min(rows, 256)
        for start in range(0, rows, step):
            pieces.append((k_ref.at[0, start : start + step], v_ref.at[0, start : start + step], step))
    for t_ref in (own_ref, other_ref):
        pieces.append((t_ref.at[0, 0, :text_rows], t_ref, text_rows))
    top = None
    at = 0
    for k_ref, _, rows in pieces:
        scores = across(k_ref[...], query) * scale + bias_ref[0, at : at + rows]
        scores_ref[at : at + rows, :] = scores
        piece_top = jnp.max(scores, axis=0, keepdims=True)
        top = piece_top if top is None else jnp.maximum(top, piece_top)
        at += rows
    total = jnp.zeros_like(top)
    blended = jnp.zeros((channels, query.shape[0]), jnp.float32)
    at = 0
    for _, v_ref, rows in pieces:
        weights = jnp.exp(scores_ref[at : at + rows, :] - top)
        total += jnp.sum(weights, axis=0, keepdims=True)
        rounded = weights.astype(jnp.bfloat16)
        if v_ref.shape[-2] == rows and len(v_ref.shape) == 2:
            projected = across(w_t, v_ref[...]).astype(jnp.bfloat16)
            blended += jnp.dot(projected, rounded, preferred_element_type=jnp.float32)
        else:
            for part in range(rows // HD):
                start = rows + part * channels
                blended += jnp.dot(
                    v_ref[0, 0, start : start + channels, :],
                    rounded[part * HD : (part + 1) * HD],
                    preferred_element_type=jnp.float32,
                )
        at += rows
    term = blended / total

    @pl.when(head == 0)
    def _():
        out_ref[0] = term

    @pl.when(head != 0)
    def _():
        out_ref[0] += term


def attention(queries, fresh_k, fresh_v, stale_k, stale_v, hot_k, hot_v, text_own, text_other, w_t, bias):
    slots, rows, width = queries.shape
    heads = width // HD
    channels = w_t.shape[0]
    key_rows = bias.shape[1]
    text_rows = (text_own.shape[2] * HD) // (HD + channels)

    def wide(array):
        return pl.BlockSpec((1, array.shape[1], HD), lambda s, h: (s, 0, h))

    packed = pl.BlockSpec((1, 1) + text_own.shape[2:], lambda s, h: (s, h, 0, 0))
    many = slots * heads * rows * key_rows
    return pl.pallas_call(
        functools.partial(attention_kernel, text_rows),
        grid=(slots, heads),
        out_shape=jax.ShapeDtypeStruct((slots, channels, rows), jnp.float32),
        in_specs=[wide(a) for a in (queries, fresh_k, fresh_v, stale_k, stale_v, hot_k, hot_v)]
        + [
            packed,
            packed,
            pl.BlockSpec((channels, HD), lambda s, h: (0, h)),
            pl.BlockSpec((1, key_rows, 1), lambda s, h: (s, 0, 0)),
        ],
        out_specs=pl.BlockSpec((1, channels, rows), lambda s, h: (s, 0, 0)),
        scratch_shapes=[pltpu.VMEM((key_rows, rows), jnp.float32)],
        cost_estimate=pl.CostEstimate(
            flops=2 * many * (HD + channels), bytes_accessed=24 * 1024 * 1024, transcendentals=many
        ),
        compiler_params=pltpu.CompilerParams(vmem_limit_bytes=VMEM_LIMIT),
        name="attention",
    )(queries, fresh_k, fresh_v, stale_k, stale_v, hot_k, hot_v, text_own, text_other, w_t, bias)


def shards(
    queries,
    fresh_kv,
    stale_kv,
    text_kv,
    w_velocity,
    latent,
    live_counts,
    refresh_rows,
    request_list,
    timesteps,
):
    half_groups = lax.axis_size("grp") // 2
    my_group = lax.axis_index("grp")
    partner = (my_group + half_groups) % (2 * half_groups)
    queries, fresh, stale, text = queries[0], fresh_kv[0], stale_kv[0], text_kv[0]
    slots, img_rows = queries.shape[:2]
    listed_count = refresh_rows.shape[2]
    hot_rows = 2 * listed_count

    raw = fresh_kv[0, :, :listed_count]
    groups = 2 * half_groups
    raw_ways = pass_along(raw, groups)

    my_list = lax.dynamic_index_in_dim(refresh_rows, my_group, 0, keepdims=False)
    partner_list = lax.dynamic_index_in_dim(refresh_rows, partner, 0, keepdims=False)
    near, far, sources = swap_pairs(jnp.stack([my_list, partner_list]))
    pairs = jnp.stack([near, far], axis=1).reshape(2, -1)

    first_cut = hot_rows + (img_rows - hot_rows) * 5 // 8
    last_cut = img_rows - listed_count
    final = slots - 1
    pieces = [(slot, hot_rows, img_rows) for slot in range(final)]
    pieces += [(final, hot_rows, first_cut), (final, first_cut, last_cut), (final, last_cut, img_rows)]
    zone, blocks = arrange(pairs[0], fresh_kv, pieces, raw)
    zone_ways = pass_along(zone, groups)
    w_t = w_velocity.T
    text_own = project_text(text[:, :, 0], text[:, :, 1], w_t, (zone_ways[0], raw_ways[0]))
    text_ways = pass_along(text_own, groups)
    piece_ways, gate = [], text_ways[0]
    for block in blocks:
        piece_ways.append(pass_along(hold(block, gate), groups))
        gate = piece_ways[-1][0]
    raw_in, zone_in, text_in = (arrived_block(ways, groups) for ways in (raw_ways, zone_ways, text_ways))

    my_live = lax.dynamic_index_in_dim(live_counts, my_group, 0, keepdims=False)
    partner_live = lax.dynamic_index_in_dim(live_counts, partner, 0, keepdims=False)
    row_ids = jnp.arange(img_rows, dtype=jnp.int32)
    hot_source = jnp.concatenate(
        [jnp.broadcast_to(row_ids[:listed_count], partner_list.shape), sources[1]], axis=1
    )
    stale_listed = jnp.any(partner_list[:, :, None] == row_ids, axis=1)
    hot_listed = jnp.any(partner_list[:, :, None] == hot_source[:, None, :], axis=1)
    live = jnp.concatenate(
        [
            row_ids < my_live[:, None],
            (row_ids < partner_live[:, None]) & jnp.logical_not(stale_listed),
            (hot_source < partner_live[:, None]) & hot_listed,
            jnp.ones((slots, 2 * text.shape[1]), dtype=bool),
        ],
        axis=1,
    )
    bias = jnp.where(live, 0.0, -jnp.inf).astype(jnp.float32)[:, :, None]
    hot = join_head(raw_in, zone_in, (slots, hot_rows) + fresh.shape[2:])
    partial = attention(
        queries,
        fresh[:, :, 0],
        fresh[:, :, 1],
        stale[:, :, 0],
        stale[:, :, 1],
        hot[:, :, 0],
        hot[:, :, 1],
        text_own,
        text_in,
        w_t,
        bias,
    )

    tp_count = lax.axis_size("tp")
    tp_index = lax.axis_index("tp")
    share = img_rows // tp_count
    if tp_count == 2:
        mine = lax.dynamic_slice_in_dim(partial, tp_index * share, share, 2)
        theirs = lax.dynamic_slice_in_dim(partial, (1 - tp_index) * share, share, 2)
        summed = mine + from_behind(theirs, "tp", 1)
    else:
        summed = lax.psum_scatter(partial, "tp", scatter_dimension=2, tiled=True)
    summed = jnp.swapaxes(summed, 1, 2)
    share_ids = tp_index * share + jnp.arange(share, dtype=jnp.int32)
    live_rows = share_ids[None, :] < my_live[:, None]
    velocity = jnp.where(live_rows[:, :, None], summed, 0.0)
    pair_index = my_group % half_groups
    request_ids = lax.dynamic_slice_in_dim(request_list, pair_index * slots, slots)
    matches = (
        request_ids[:, None] == jnp.arange(timesteps.shape[0], dtype=jnp.int32)[None, :]
    ).astype(jnp.int32)
    times = jnp.sum(matches[:, :, None] * timesteps[None], axis=1)
    step_size = (times[:, 1] - times[:, 0]).astype(jnp.float32) / 1000.0
    latent_next = latent[0] + step_size[:, None, None] * velocity

    next_stale = join_head(raw_in, zone_in, fresh.shape)
    for index, piece in enumerate(pieces):
        next_stale = restore(pairs[1], piece_ways[index], next_stale, piece, groups)
    return (next_stale[None], velocity[None], latent_next[None])


def solution(mesh):
    return jax.shard_map(
        shards,
        mesh=mesh,
        in_specs=(
            P("grp", None, None, "tp"),
            P("grp", None, None, None, "tp"),
            P("grp", None, None, None, "tp"),
            P("grp", None, None, None, "tp"),
            P("tp", None),
            P("grp", None, "tp", None),
            P(),
            P(),
            P(),
            P(),
        ),
        out_specs=(
            P("grp", None, None, None, "tp"),
            P("grp", None, "tp", None),
            P("grp", None, "tp", None),
        ),
        check_vma=False,
    )
```

```python
import functools
import math

import jax
import jax.numpy as jnp
from jax import lax
from jax.experimental import pallas as pl
from jax.experimental.pallas import tpu as pltpu
from jax.sharding import PartitionSpec as P

HD = 128
HBM = pltpu.MemorySpace.HBM
SMEM = pltpu.MemorySpace.SMEM
VMEM_LIMIT = 32 * 1024 * 1024
WIDE_LIMIT = 60 * 1024 * 1024


def from_behind(block, axis, distance):
    devices = range(lax.axis_size(axis))
    route = [((i - distance) % len(devices), i) for i in devices]
    return lax.ppermute(block, axis, route)


def swap_pairs(lists):
    count = lists.shape[2]
    zone = count + jnp.arange(count, dtype=jnp.int32)
    order = jnp.arange(count, dtype=jnp.int32)
    earlier = order[:, None] >= order[None, :]
    free = jnp.logical_not(jnp.any(lists[..., :, None] == zone, axis=2))
    outside = lists >= 2 * count
    free_rank = jnp.sum((earlier & free[..., None, :]).astype(jnp.int32), axis=3)
    outside_rank = jnp.sum((earlier & outside[..., None, :]).astype(jnp.int32), axis=3)
    match = (
        outside[..., :, None]
        & free[..., None, :]
        & (outside_rank[..., :, None] == free_rank[..., None, :])
    )
    near = jnp.sum(jnp.where(match, order, 0), axis=3)
    sources = jnp.sum(jnp.where(match, lists[..., :, None], 0), axis=2)
    return near, jnp.where(outside, lists, -1), jnp.where(sources > 0, sources, zone)


def swap_rows(pairs, slots, slot, zone, piece, start, stop):
    count = zone.shape[0] - 1

    def step(k, carry):
        far = pairs[(slots + slot) * count + k]
        here = jnp.logical_and(far >= start, far < stop)
        near_row = jnp.where(here, pairs[slot * count + k], count)
        far_row = jnp.where(here, far - start, stop - start)
        moved = zone[near_row]
        zone[near_row] = piece[far_row]
        piece[far_row] = moved
        return carry

    lax.fori_loop(0, count, step, 0, unroll=8)


def relay(copies, sems):
    inner = [pltpu.make_async_copy(c[0], c[1], sems.at[0, i]) for i, c in enumerate(copies)]
    outer = [pltpu.make_async_copy(c[1], c[2], sems.at[1, i]) for i, c in enumerate(copies)]
    for copy in inner:
        copy.start()
    for arrive, leave in zip(inner, outer):
        arrive.wait()
        leave.start()
    for copy in outer:
        copy.wait()


def arrange_kernel(slots, pieces, pairs_ref, fresh_ref, after_ref, *refs):
    zone_out, piece_outs = refs[0], refs[1 : 1 + len(pieces)]
    pairs, zones, rests, sems = refs[1 + len(pieces) :]
    count = zones.shape[1] - 1
    rest_rows = rests.shape[1] - 1
    copy_pairs = pltpu.make_async_copy(pairs_ref, pairs, sems.at[3 * slots + len(pieces)])
    copy_pairs.start()
    copies_in = []
    for slot in range(slots):
        copies_in.append(
            (
                pltpu.make_async_copy(
                    fresh_ref.at[0, slot, count : 2 * count], zones.at[slot, :count], sems.at[slot]
                ),
                pltpu.make_async_copy(
                    fresh_ref.at[0, slot, 2 * count :], rests.at[slot, :rest_rows], sems.at[slots + slot]
                ),
            )
        )
        for copy in copies_in[-1]:
            copy.start()
    copy_pairs.wait()
    copies_out = []
    for slot in range(slots):
        for copy in copies_in[slot]:
            copy.wait()
        swap_rows(pairs, slots, slot, zones.at[slot], rests.at[slot], 2 * count, 2 * count + rest_rows)
        copies_out.append(
            pltpu.make_async_copy(zones.at[slot, :count], zone_out.at[slot], sems.at[2 * slots + slot])
        )
        copies_out[-1].start()
        for index, (piece_slot, start, stop) in enumerate(pieces):
            if piece_slot == slot:
                source = rests.at[slot, start - 2 * count : stop - 2 * count]
                copies_out.append(
                    pltpu.make_async_copy(source, piece_outs[index], sems.at[3 * slots + index])
                )
                copies_out[-1].start()
    for copy in copies_out:
        copy.wait()


def arrange(pairs, fresh_kv, pieces, after):
    slots, rows = fresh_kv.shape[1:3]
    tail = fresh_kv.shape[3:]
    count = pairs.shape[0] // (2 * slots)
    outs = pl.pallas_call(
        functools.partial(arrange_kernel, slots, pieces),
        out_shape=[jax.ShapeDtypeStruct((slots, count) + tail, fresh_kv.dtype)]
        + [jax.ShapeDtypeStruct((stop - start,) + tail, fresh_kv.dtype) for _, start, stop in pieces],
        in_specs=[pl.BlockSpec(memory_space=HBM)] * 3,
        out_specs=[pl.BlockSpec(memory_space=HBM)] * (1 + len(pieces)),
        scratch_shapes=[
            pltpu.SMEM(pairs.shape, pairs.dtype),
            pltpu.VMEM((slots, count + 1) + tail, fresh_kv.dtype),
            pltpu.VMEM((slots, rows - 2 * count + 1) + tail, fresh_kv.dtype),
            pltpu.SemaphoreType.DMA((3 * slots + len(pieces) + 1,)),
        ],
        cost_estimate=pl.CostEstimate(flops=0, bytes_accessed=4 * fresh_kv.size, transcendentals=0),
        compiler_params=pltpu.CompilerParams(vmem_limit_bytes=WIDE_LIMIT),
        name="arrange",
    )(pairs, fresh_kv, after)
    return outs[0], outs[1:]


def join_kernel(raw_ref, zone_ref, out_ref, stage, sems):
    count = raw_ref.shape[1]
    relay(
        [
            (raw_ref, stage.at[0], out_ref.at[:, :count]),
            (zone_ref, stage.at[1], out_ref.at[:, count : 2 * count]),
        ],
        sems,
    )


def join_head(raw, zone, shape):
    return pl.pallas_call(
        join_kernel,
        out_shape=jax.ShapeDtypeStruct(shape, raw.dtype),
        in_specs=[pl.BlockSpec(memory_space=HBM)] * 2,
        out_specs=pl.BlockSpec(memory_space=HBM),
        scratch_shapes=[pltpu.VMEM((2,) + raw.shape, raw.dtype), pltpu.SemaphoreType.DMA((2, 2))],
        cost_estimate=pl.CostEstimate(flops=0, bytes_accessed=8 * raw.size, transcendentals=0),
        compiler_params=pltpu.CompilerParams(vmem_limit_bytes=VMEM_LIMIT),
        name="join_head",
    )(raw, zone)


def restore_kernel(slot, start, stop, groups, pairs_ref, end_ref, middle_ref, whole_ref, *refs):
    out_ref, pairs, zone, piece, sems = refs[-5:]
    count = zone.shape[0] - 1
    inner = [
        pltpu.make_async_copy(pairs_ref, pairs, sems.at[4]),
        pltpu.make_async_copy(out_ref.at[slot, count : 2 * count], zone.at[:count], sems.at[1]),
    ]
    for copy in inner:
        copy.start()
    from_end = pltpu.make_async_copy(end_ref, piece.at[: stop - start], sems.at[0])
    from_middle = pltpu.make_async_copy(middle_ref, piece.at[: stop - start], sems.at[0])
    middle = on_the_way(groups)

    @pl.when(middle)
    def _():
        from_middle.start()

    @pl.when(jnp.logical_not(middle))
    def _():
        from_end.start()

    inner.append(from_end)
    for copy in inner:
        copy.wait()
    swap_rows(pairs, out_ref.shape[0], slot, zone, piece, start, stop)
    outer = [
        pltpu.make_async_copy(piece.at[: stop - start], out_ref.at[slot, start:stop], sems.at[2]),
        pltpu.make_async_copy(zone.at[:count], out_ref.at[slot, count : 2 * count], sems.at[3]),
    ]
    for copy in outer:
        copy.start()
    for copy in outer:
        copy.wait()


def restore(pairs, ways, whole, piece, groups, after=()):
    slot, start, stop = piece
    tail = whole.shape[2:]
    count = pairs.shape[0] // (2 * whole.shape[0])
    return pl.pallas_call(
        functools.partial(restore_kernel, slot, start, stop, groups),
        out_shape=jax.ShapeDtypeStruct(whole.shape, whole.dtype),
        in_specs=[pl.BlockSpec(memory_space=HBM)] * (4 + len(after)),
        out_specs=pl.BlockSpec(memory_space=HBM),
        scratch_shapes=[
            pltpu.SMEM(pairs.shape, pairs.dtype),
            pltpu.VMEM((count + 1,) + tail, whole.dtype),
            pltpu.VMEM((stop - start + 1,) + tail, whole.dtype),
            pltpu.SemaphoreType.DMA((5,)),
        ],
        input_output_aliases={3: 0},
        cost_estimate=pl.CostEstimate(flops=0, bytes_accessed=4 * ways[1].size, transcendentals=0),
        compiler_params=pltpu.CompilerParams(vmem_limit_bytes=VMEM_LIMIT),
        name="restore",
    )(pairs, *ways, whole, *after)


def on_the_way(groups):
    place = lax.axis_index("grp") // (groups // 4)
    return jnp.logical_or(place == 1, place == 2)


def either_kernel(groups, end_ref, middle_ref, out_ref, stage, sems):
    middle = on_the_way(groups)
    from_end = pltpu.make_async_copy(end_ref, stage, sems.at[0])
    from_middle = pltpu.make_async_copy(middle_ref, stage, sems.at[0])

    @pl.when(middle)
    def _():
        from_middle.start()

    @pl.when(jnp.logical_not(middle))
    def _():
        from_end.start()

    from_end.wait()
    leave = pltpu.make_async_copy(stage, out_ref, sems.at[1])
    leave.start()
    leave.wait()


def either(end_block, middle_block, groups):
    return pl.pallas_call(
        functools.partial(either_kernel, groups),
        out_shape=jax.ShapeDtypeStruct(end_block.shape, end_block.dtype),
        in_specs=[pl.BlockSpec(memory_space=HBM)] * 2,
        out_specs=pl.BlockSpec(memory_space=HBM),
        scratch_shapes=[pltpu.VMEM(end_block.shape, end_block.dtype), pltpu.SemaphoreType.DMA((2,))],
        cost_estimate=pl.CostEstimate(flops=0, bytes_accessed=4 * end_block.size, transcendentals=0),
        compiler_params=pltpu.CompilerParams(vmem_limit_bytes=VMEM_LIMIT),
        name="either",
    )(end_block, middle_block)


def swap_along(block, groups, couples):
    quarter = groups // 4
    route = []
    for one, other in couples:
        for i in range(quarter):
            route.append((one * quarter + i, other * quarter + i))
            route.append((other * quarter + i, one * quarter + i))
    return lax.ppermute(block, "grp", route)


def pass_direct(block, groups):
    direct = from_behind(block, "grp", groups // 2)
    return direct, direct


def pass_around(block, groups):
    if groups != 16:
        return pass_direct(block, groups)
    crossed = swap_along(block, groups, [(0, 3)])
    outer = swap_along(either(crossed, block, groups), groups, [(0, 1), (2, 3)])
    return swap_along(outer, groups, [(0, 3)]), outer


def hold_kernel(block_ref, after_ref, out_ref):
    del block_ref, after_ref, out_ref


def hold(block, after):
    return pl.pallas_call(
        hold_kernel,
        out_shape=jax.ShapeDtypeStruct(block.shape, block.dtype),
        in_specs=[pl.BlockSpec(memory_space=HBM)] * 2,
        out_specs=pl.BlockSpec(memory_space=HBM),
        input_output_aliases={0: 0},
        cost_estimate=pl.CostEstimate(flops=0, bytes_accessed=0, transcendentals=0),
        name="hold",
    )(block, after)


def across(a, b):
    return lax.dot_general(a, b, (((1,), (1,)), ((), ())), preferred_element_type=jnp.float32)


def text_kernel(k_ref, v_ref, w_ref, *refs):
    out_ref = refs[-1]
    slots, rows, width = k_ref.shape
    channels = w_ref.shape[0]
    for slot in range(slots):
        for head in range(width // HD):
            columns = slice(head * HD, (head + 1) * HD)
            out_ref[slot, head, :rows, :] = k_ref[slot, :, columns]
            projected = across(w_ref[:, columns], v_ref[slot, :, columns]).astype(out_ref.dtype)
            for part in range(rows // HD):
                start = rows + part * channels
                out_ref[slot, head, start : start + channels, :] = projected[:, part * HD : (part + 1) * HD]


def project_text(keys, values, w_t, after):
    slots, rows, width = keys.shape
    heads = width // HD
    channels = w_t.shape[0]
    packed = rows + channels * rows // HD
    return pl.pallas_call(
        text_kernel,
        out_shape=jax.ShapeDtypeStruct((slots, heads, packed, HD), keys.dtype),
        in_specs=[pl.BlockSpec(memory_space=pltpu.VMEM)] * 3
        + [pl.BlockSpec(memory_space=HBM)] * len(after),
        out_specs=pl.BlockSpec(memory_space=pltpu.VMEM),
        cost_estimate=pl.CostEstimate(
            flops=2 * slots * rows * width * channels, bytes_accessed=4 * keys.size * 2, transcendentals=0
        ),
        compiler_params=pltpu.CompilerParams(vmem_limit_bytes=VMEM_LIMIT),
        name="project_text",
    )(keys, values, w_t, *after)


def attention_kernel(text_rows, *refs):
    (q_ref, kf_ref, vf_ref, ks_ref, vs_ref, kh_ref, vh_ref, own_ref, other_ref, w_ref, bias_ref) = refs[:11]
    out_ref, scores_ref = refs[11], refs[12]
    head = pl.program_id(1)
    query = q_ref[0]
    w_t = w_ref[...]
    channels = w_t.shape[0]
    scale = 1.0 / math.sqrt(HD)
    pieces = []
    for k_ref, v_ref in ((kf_ref, vf_ref), (ks_ref, vs_ref), (kh_ref, vh_ref)):
        rows = k_ref.shape[1]
        step = min(rows, 256)
        for start in range(0, rows, step):
            pieces.append((k_ref.at[0, start : start + step], v_ref.at[0, start : start + step], step))
    for t_ref in (own_ref, other_ref):
        pieces.append((t_ref.at[0, 0, :text_rows], t_ref, text_rows))
    top = None
    at = 0
    for k_ref, _, rows in pieces:
        scores = across(k_ref[...], query) * scale + bias_ref[0, at : at + rows]
        scores_ref[at : at + rows, :] = scores
        piece_top = jnp.max(scores, axis=0, keepdims=True)
        top = piece_top if top is None else jnp.maximum(top, piece_top)
        at += rows
    total = jnp.zeros_like(top)
    blended = jnp.zeros((channels, query.shape[0]), jnp.float32)
    at = 0
    for _, v_ref, rows in pieces:
        weights = jnp.exp(scores_ref[at : at + rows, :] - top)
        total += jnp.sum(weights, axis=0, keepdims=True)
        rounded = weights.astype(jnp.bfloat16)
        if v_ref.shape[-2] == rows and len(v_ref.shape) == 2:
            projected = across(w_t, v_ref[...]).astype(jnp.bfloat16)
            blended += jnp.dot(projected, rounded, preferred_element_type=jnp.float32)
        else:
            for part in range(rows // HD):
                start = rows + part * channels
                blended += jnp.dot(
                    v_ref[0, 0, start : start + channels, :],
                    rounded[part * HD : (part + 1) * HD],
                    preferred_element_type=jnp.float32,
                )
        at += rows
    term = blended / total

    @pl.when(head == 0)
    def _():
        out_ref[0] = term

    @pl.when(head != 0)
    def _():
        out_ref[0] += term


def attention(queries, fresh_k, fresh_v, stale_k, stale_v, hot_k, hot_v, text_own, text_other, w_t, bias):
    slots, rows, width = queries.shape
    heads = width // HD
    channels = w_t.shape[0]
    key_rows = bias.shape[1]
    text_rows = (text_own.shape[2] * HD) // (HD + channels)

    def wide(array):
        return pl.BlockSpec((1, array.shape[1], HD), lambda s, h: (s, 0, h))

    packed = pl.BlockSpec((1, 1) + text_own.shape[2:], lambda s, h: (s, h, 0, 0))
    many = slots * heads * rows * key_rows
    return pl.pallas_call(
        functools.partial(attention_kernel, text_rows),
        grid=(slots, heads),
        out_shape=jax.ShapeDtypeStruct((slots, channels, rows), jnp.float32),
        in_specs=[wide(a) for a in (queries, fresh_k, fresh_v, stale_k, stale_v, hot_k, hot_v)]
        + [
            packed,
            packed,
            pl.BlockSpec((channels, HD), lambda s, h: (0, h)),
            pl.BlockSpec((1, key_rows, 1), lambda s, h: (s, 0, 0)),
        ],
        out_specs=pl.BlockSpec((1, channels, rows), lambda s, h: (s, 0, 0)),
        scratch_shapes=[pltpu.VMEM((key_rows, rows), jnp.float32)],
        cost_estimate=pl.CostEstimate(
            flops=2 * many * (HD + channels), bytes_accessed=24 * 1024 * 1024, transcendentals=many
        ),
        compiler_params=pltpu.CompilerParams(vmem_limit_bytes=VMEM_LIMIT),
        name="attention",
    )(queries, fresh_k, fresh_v, stale_k, stale_v, hot_k, hot_v, text_own, text_other, w_t, bias)


def shards(
    queries,
    fresh_kv,
    stale_kv,
    text_kv,
    w_velocity,
    latent,
    live_counts,
    refresh_rows,
    request_list,
    timesteps,
):
    half_groups = lax.axis_size("grp") // 2
    my_group = lax.axis_index("grp")
    partner = (my_group + half_groups) % (2 * half_groups)
    queries, fresh, stale, text = queries[0], fresh_kv[0], stale_kv[0], text_kv[0]
    slots, img_rows = queries.shape[:2]
    listed_count = refresh_rows.shape[2]
    hot_rows = 2 * listed_count

    raw = fresh_kv[0, :, :listed_count]
    groups = 2 * half_groups
    raw_in = from_behind(raw, "grp", half_groups)

    my_list = lax.dynamic_index_in_dim(refresh_rows, my_group, 0, keepdims=False)
    partner_list = lax.dynamic_index_in_dim(refresh_rows, partner, 0, keepdims=False)
    near, far, sources = swap_pairs(jnp.stack([my_list, partner_list]))
    pairs = jnp.stack([near, far], axis=1).reshape(2, -1)

    final = slots - 1
    pieces = [(slot, hot_rows, img_rows) for slot in range(slots)]
    zone, blocks = arrange(pairs[0], fresh_kv, pieces, raw)
    zone_in = from_behind(zone, "grp", half_groups)
    w_t = w_velocity.T
    text_own = project_text(text[:, :, 0], text[:, :, 1], w_t, (zone,))
    text_in = from_behind(text_own, "grp", half_groups)
    piece_ways = [pass_direct(hold(block, text_in), groups) for block in blocks[:final]]
    piece_ways.append(pass_around(blocks[final], groups))

    my_live = lax.dynamic_index_in_dim(live_counts, my_group, 0, keepdims=False)
    partner_live = lax.dynamic_index_in_dim(live_counts, partner, 0, keepdims=False)
    row_ids = jnp.arange(img_rows, dtype=jnp.int32)
    hot_source = jnp.concatenate(
        [jnp.broadcast_to(row_ids[:listed_count], partner_list.shape), sources[1]], axis=1
    )
    stale_listed = jnp.any(partner_list[:, :, None] == row_ids, axis=1)
    hot_listed = jnp.any(partner_list[:, :, None] == hot_source[:, None, :], axis=1)
    live = jnp.concatenate(
        [
            row_ids < my_live[:, None],
            (row_ids < partner_live[:, None]) & jnp.logical_not(stale_listed),
            (hot_source < partner_live[:, None]) & hot_listed,
            jnp.ones((slots, 2 * text.shape[1]), dtype=bool),
        ],
        axis=1,
    )
    bias = jnp.where(live, 0.0, -jnp.inf).astype(jnp.float32)[:, :, None]
    hot = join_head(raw_in, zone_in, (slots, hot_rows) + fresh.shape[2:])
    partial = attention(
        queries,
        fresh[:, :, 0],
        fresh[:, :, 1],
        stale[:, :, 0],
        stale[:, :, 1],
        hot[:, :, 0],
        hot[:, :, 1],
        text_own,
        text_in,
        w_t,
        bias,
    )

    tp_count = lax.axis_size("tp")
    tp_index = lax.axis_index("tp")
    share = img_rows // tp_count
    if tp_count == 2:
        mine = lax.dynamic_slice_in_dim(partial, tp_index * share, share, 2)
        theirs = lax.dynamic_slice_in_dim(partial, (1 - tp_index) * share, share, 2)
        summed = mine + from_behind(theirs, "tp", 1)
    else:
        summed = lax.psum_scatter(partial, "tp", scatter_dimension=2, tiled=True)
    summed = jnp.swapaxes(summed, 1, 2)
    share_ids = tp_index * share + jnp.arange(share, dtype=jnp.int32)
    live_rows = share_ids[None, :] < my_live[:, None]
    velocity = jnp.where(live_rows[:, :, None], summed, 0.0)
    pair_index = my_group % half_groups
    request_ids = lax.dynamic_slice_in_dim(request_list, pair_index * slots, slots)
    matches = (
        request_ids[:, None] == jnp.arange(timesteps.shape[0], dtype=jnp.int32)[None, :]
    ).astype(jnp.int32)
    times = jnp.sum(matches[:, :, None] * timesteps[None], axis=1)
    step_size = (times[:, 1] - times[:, 0]).astype(jnp.float32) / 1000.0
    latent_next = latent[0] + step_size[:, None, None] * velocity

    next_stale = join_head(raw_in, zone_in, fresh.shape)
    for index, piece in reversed(list(enumerate(pieces))):
        next_stale = restore(pairs[1], piece_ways[index], next_stale, piece, groups)
    return (next_stale[None], velocity[None], latent_next[None])


def solution(mesh):
    return jax.shard_map(
        shards,
        mesh=mesh,
        in_specs=(
            P("grp", None, None, "tp"),
            P("grp", None, None, None, "tp"),
            P("grp", None, None, None, "tp"),
            P("grp", None, None, None, "tp"),
            P("tp", None),
            P("grp", None, "tp", None),
            P(),
            P(),
            P(),
            P(),
        ),
        out_specs=(
            P("grp", None, None, None, "tp"),
            P("grp", None, "tp", None),
            P("grp", None, "tp", None),
        ),
        check_vma=False,
    )
```

```python
import functools
import math

import jax
import jax.numpy as jnp
from jax import lax
from jax.experimental import pallas as pl
from jax.experimental.pallas import tpu as pltpu
from jax.sharding import PartitionSpec as P

HD = 128
HBM = pltpu.MemorySpace.HBM
SMEM = pltpu.MemorySpace.SMEM
VMEM_LIMIT = 32 * 1024 * 1024
WIDE_LIMIT = 60 * 1024 * 1024


def from_behind(block, axis, distance):
    devices = range(lax.axis_size(axis))
    route = [((i - distance) % len(devices), i) for i in devices]
    return lax.ppermute(block, axis, route)


def swap_pairs(lists):
    count = lists.shape[2]
    zone = count + jnp.arange(count, dtype=jnp.int32)
    order = jnp.arange(count, dtype=jnp.int32)
    earlier = order[:, None] >= order[None, :]
    free = jnp.logical_not(jnp.any(lists[..., :, None] == zone, axis=2))
    outside = lists >= 2 * count
    free_rank = jnp.sum((earlier & free[..., None, :]).astype(jnp.int32), axis=3)
    outside_rank = jnp.sum((earlier & outside[..., None, :]).astype(jnp.int32), axis=3)
    match = (
        outside[..., :, None]
        & free[..., None, :]
        & (outside_rank[..., :, None] == free_rank[..., None, :])
    )
    near = jnp.sum(jnp.where(match, order, 0), axis=3)
    sources = jnp.sum(jnp.where(match, lists[..., :, None], 0), axis=2)
    return near, jnp.where(outside, lists, -1), jnp.where(sources > 0, sources, zone)


def swap_rows(pairs, slots, slot, zone, piece, start, stop):
    count = zone.shape[0] - 1

    def step(k, carry):
        far = pairs[(slots + slot) * count + k]
        here = jnp.logical_and(far >= start, far < stop)
        near_row = jnp.where(here, pairs[slot * count + k], count)
        far_row = jnp.where(here, far - start, stop - start)
        moved = zone[near_row]
        zone[near_row] = piece[far_row]
        piece[far_row] = moved
        return carry

    lax.fori_loop(0, count, step, 0, unroll=8)


def relay(copies, sems):
    inner = [pltpu.make_async_copy(c[0], c[1], sems.at[0, i]) for i, c in enumerate(copies)]
    outer = [pltpu.make_async_copy(c[1], c[2], sems.at[1, i]) for i, c in enumerate(copies)]
    for copy in inner:
        copy.start()
    for arrive, leave in zip(inner, outer):
        arrive.wait()
        leave.start()
    for copy in outer:
        copy.wait()


def arrange_kernel(slots, pieces, pairs_ref, fresh_ref, *refs):
    refs = refs[slots:]
    zone_outs, piece_outs = refs[:slots], refs[slots : slots + len(pieces)]
    pairs, zones, rests, sems = refs[slots + len(pieces) :]
    count = zones.shape[1] - 1
    rest_rows = rests.shape[1] - 1
    copy_pairs = pltpu.make_async_copy(pairs_ref, pairs, sems.at[3 * slots + len(pieces)])
    copy_pairs.start()
    copies_in = []
    for slot in range(slots):
        copies_in.append(
            (
                pltpu.make_async_copy(
                    fresh_ref.at[0, slot, count : 2 * count], zones.at[slot, :count], sems.at[slot]
                ),
                pltpu.make_async_copy(
                    fresh_ref.at[0, slot, 2 * count :], rests.at[slot, :rest_rows], sems.at[slots + slot]
                ),
            )
        )
        for copy in copies_in[-1]:
            copy.start()
    copy_pairs.wait()
    copies_out = []
    for slot in range(slots):
        for copy in copies_in[slot]:
            copy.wait()
        swap_rows(pairs, slots, slot, zones.at[slot], rests.at[slot], 2 * count, 2 * count + rest_rows)
        copies_out.append(
            pltpu.make_async_copy(zones.at[slot, :count], zone_outs[slot], sems.at[2 * slots + slot])
        )
        copies_out[-1].start()
        for index, (piece_slot, start, stop) in enumerate(pieces):
            if piece_slot == slot:
                source = rests.at[slot, start - 2 * count : stop - 2 * count]
                copies_out.append(
                    pltpu.make_async_copy(source, piece_outs[index], sems.at[3 * slots + index])
                )
                copies_out[-1].start()
    for copy in copies_out:
        copy.wait()


def arrange(pairs, fresh_kv, pieces, after):
    slots, rows = fresh_kv.shape[1:3]
    tail = fresh_kv.shape[3:]
    count = pairs.shape[0] // (2 * slots)
    outs = pl.pallas_call(
        functools.partial(arrange_kernel, slots, pieces),
        out_shape=[jax.ShapeDtypeStruct((count,) + tail, fresh_kv.dtype)] * slots
        + [jax.ShapeDtypeStruct((stop - start,) + tail, fresh_kv.dtype) for _, start, stop in pieces],
        in_specs=[pl.BlockSpec(memory_space=HBM)] * (2 + slots),
        out_specs=[pl.BlockSpec(memory_space=HBM)] * (slots + len(pieces)),
        scratch_shapes=[
            pltpu.SMEM(pairs.shape, pairs.dtype),
            pltpu.VMEM((slots, count + 1) + tail, fresh_kv.dtype),
            pltpu.VMEM((slots, rows - 2 * count + 1) + tail, fresh_kv.dtype),
            pltpu.SemaphoreType.DMA((3 * slots + len(pieces) + 1,)),
        ],
        cost_estimate=pl.CostEstimate(flops=0, bytes_accessed=4 * fresh_kv.size, transcendentals=0),
        compiler_params=pltpu.CompilerParams(vmem_limit_bytes=WIDE_LIMIT),
        name="arrange",
    )(pairs, fresh_kv, *after)
    return outs[:slots], outs[slots:]


def join_kernel(places, *refs):
    count = len(places)
    out_ref, stage, sems = refs[count:]
    rows = stage.shape[1]
    targets = [out_ref.at[slot, start : start + rows] for slot, start in places]
    inner = [pltpu.make_async_copy(refs[i], stage.at[i], sems.at[i]) for i in range(count)]
    outer = [pltpu.make_async_copy(stage.at[i], targets[i], sems.at[count + i]) for i in range(count)]
    for copy in inner:
        copy.start()
    for arrive, leave in zip(inner, outer):
        arrive.wait()
        leave.start()
    for copy in outer:
        copy.wait()


def join_head(blocks, places, shape):
    block = blocks[0]
    return pl.pallas_call(
        functools.partial(join_kernel, places),
        out_shape=jax.ShapeDtypeStruct(shape, block.dtype),
        in_specs=[pl.BlockSpec(memory_space=HBM)] * len(blocks),
        out_specs=pl.BlockSpec(memory_space=HBM),
        scratch_shapes=[
            pltpu.VMEM((len(blocks),) + block.shape, block.dtype),
            pltpu.SemaphoreType.DMA((2 * len(blocks),)),
        ],
        cost_estimate=pl.CostEstimate(
            flops=0, bytes_accessed=4 * len(blocks) * block.size, transcendentals=0
        ),
        compiler_params=pltpu.CompilerParams(vmem_limit_bytes=VMEM_LIMIT),
        name="join_head",
    )(*blocks)


def restore_kernel(pieces, pairs_ref, *refs):
    number = len(pieces)
    piece_refs = refs[:number]
    out_ref, pairs, zones, stage, sems = refs[-5:]
    slots = out_ref.shape[0]
    count = zones.shape[1] - 1
    copy_pairs = pltpu.make_async_copy(pairs_ref, pairs, sems.at[4 * number])
    copy_pairs.start()
    inner, outer = [], []
    for i, (slot, start, stop) in enumerate(pieces):
        block, head = stage.at[i, : stop - start], zones.at[i, :count]
        head_out = out_ref.at[slot, count : 2 * count]
        inner.append(pltpu.make_async_copy(piece_refs[i], block, sems.at[4 * i]))
        inner.append(pltpu.make_async_copy(head_out, head, sems.at[4 * i + 1]))
        outer.append(pltpu.make_async_copy(block, out_ref.at[slot, start:stop], sems.at[4 * i + 2]))
        outer.append(pltpu.make_async_copy(head, head_out, sems.at[4 * i + 3]))
    for copy in inner:
        copy.start()
    copy_pairs.wait()
    for i, (slot, start, stop) in enumerate(pieces):
        inner[2 * i].wait()
        inner[2 * i + 1].wait()
        swap_rows(pairs, slots, slot, zones.at[i], stage.at[i], start, stop)
        outer[2 * i].start()
        outer[2 * i + 1].start()
    for copy in outer:
        copy.wait()


def restore(pairs, blocks, whole, pieces):
    tail = whole.shape[2:]
    number = len(pieces)
    count = pairs.shape[0] // (2 * whole.shape[0])
    rows = max(stop - start for _, start, stop in pieces)
    return pl.pallas_call(
        functools.partial(restore_kernel, pieces),
        out_shape=jax.ShapeDtypeStruct(whole.shape, whole.dtype),
        in_specs=[pl.BlockSpec(memory_space=HBM)] * (2 + number),
        out_specs=pl.BlockSpec(memory_space=HBM),
        scratch_shapes=[
            pltpu.SMEM(pairs.shape, pairs.dtype),
            pltpu.VMEM((number, count + 1) + tail, whole.dtype),
            pltpu.VMEM((number, rows + 1) + tail, whole.dtype),
            pltpu.SemaphoreType.DMA((4 * number + 1,)),
        ],
        input_output_aliases={1 + number: 0},
        cost_estimate=pl.CostEstimate(
            flops=0, bytes_accessed=4 * number * blocks[0].size, transcendentals=0
        ),
        compiler_params=pltpu.CompilerParams(vmem_limit_bytes=VMEM_LIMIT),
        name="restore",
    )(pairs, *blocks, whole)


def hold_kernel(block_ref, after_ref, out_ref):
    del block_ref, after_ref, out_ref


def hold(block, after):
    return pl.pallas_call(
        hold_kernel,
        out_shape=jax.ShapeDtypeStruct(block.shape, block.dtype),
        in_specs=[pl.BlockSpec(memory_space=HBM)] * 2,
        out_specs=pl.BlockSpec(memory_space=HBM),
        input_output_aliases={0: 0},
        cost_estimate=pl.CostEstimate(flops=0, bytes_accessed=0, transcendentals=0),
        name="hold",
    )(block, after)


def across(a, b):
    return lax.dot_general(a, b, (((1,), (1,)), ((), ())), preferred_element_type=jnp.float32)


def text_kernel(k_ref, v_ref, w_ref, after_ref, out_ref):
    rows, width = k_ref.shape
    channels = w_ref.shape[0]
    for head in range(width // HD):
        columns = slice(head * HD, (head + 1) * HD)
        out_ref[head, :rows, :] = k_ref[:, columns]
        projected = across(w_ref[:, columns], v_ref[:, columns]).astype(out_ref.dtype)
        for part in range(rows // HD):
            start = rows + part * channels
            out_ref[head, start : start + channels, :] = projected[:, part * HD : (part + 1) * HD]


def project_text(keys, values, w_t, after):
    rows, width = keys.shape
    heads = width // HD
    channels = w_t.shape[0]
    packed = rows + channels * rows // HD
    return pl.pallas_call(
        text_kernel,
        out_shape=jax.ShapeDtypeStruct((heads, packed, HD), keys.dtype),
        in_specs=[pl.BlockSpec(memory_space=pltpu.VMEM)] * 3 + [pl.BlockSpec(memory_space=HBM)],
        out_specs=pl.BlockSpec(memory_space=pltpu.VMEM),
        cost_estimate=pl.CostEstimate(
            flops=2 * rows * width * channels, bytes_accessed=4 * keys.size * 2, transcendentals=0
        ),
        compiler_params=pltpu.CompilerParams(vmem_limit_bytes=VMEM_LIMIT),
        name="project_text",
    )(keys, values, w_t, after)


def attention_kernel(text_rows, *refs):
    (q_ref, kf_ref, vf_ref, ks_ref, vs_ref, kh_ref, vh_ref, own_ref, other_ref, w_ref, bias_ref) = refs[:11]
    out_ref, scores_ref = refs[11], refs[12]
    head = pl.program_id(0)
    query = q_ref[...]
    w_t = w_ref[...]
    channels = w_t.shape[0]
    scale = 1.0 / math.sqrt(HD)
    pieces = []
    for k_ref, v_ref in ((kf_ref, vf_ref), (ks_ref, vs_ref), (kh_ref, vh_ref)):
        rows = k_ref.shape[0]
        step = min(rows, 256)
        for start in range(0, rows, step):
            pieces.append((k_ref.at[start : start + step], v_ref.at[start : start + step], step))
    for t_ref in (own_ref, other_ref):
        pieces.append((t_ref.at[0, :text_rows], t_ref, text_rows))
    top = None
    at = 0
    for k_ref, _, rows in pieces:
        scores = across(k_ref[...], query) * scale + bias_ref[at : at + rows]
        scores_ref[at : at + rows, :] = scores
        piece_top = jnp.max(scores, axis=0, keepdims=True)
        top = piece_top if top is None else jnp.maximum(top, piece_top)
        at += rows
    total = jnp.zeros_like(top)
    blended = jnp.zeros((channels, query.shape[0]), jnp.float32)
    at = 0
    for _, v_ref, rows in pieces:
        weights = jnp.exp(scores_ref[at : at + rows, :] - top)
        total += jnp.sum(weights, axis=0, keepdims=True)
        rounded = weights.astype(jnp.bfloat16)
        if v_ref.shape[-2] == rows and len(v_ref.shape) == 2:
            projected = across(w_t, v_ref[...]).astype(jnp.bfloat16)
            blended += jnp.dot(projected, rounded, preferred_element_type=jnp.float32)
        else:
            for part in range(rows // HD):
                start = rows + part * channels
                blended += jnp.dot(
                    v_ref[0, start : start + channels, :],
                    rounded[part * HD : (part + 1) * HD],
                    preferred_element_type=jnp.float32,
                )
        at += rows
    term = blended / total

    @pl.when(head == 0)
    def _():
        out_ref[...] = term

    @pl.when(head != 0)
    def _():
        out_ref[...] += term


def attention(queries, fresh_k, fresh_v, stale_k, stale_v, hot_k, hot_v, text_own, text_other, w_t, bias):
    rows, width = queries.shape
    heads = width // HD
    channels = w_t.shape[0]
    key_rows = bias.shape[0]
    text_rows = (text_own.shape[1] * HD) // (HD + channels)

    def wide(array):
        return pl.BlockSpec((array.shape[0], HD), lambda h: (0, h))

    packed = pl.BlockSpec((1,) + text_own.shape[1:], lambda h: (h, 0, 0))
    many = heads * rows * key_rows
    return pl.pallas_call(
        functools.partial(attention_kernel, text_rows),
        grid=(heads,),
        out_shape=jax.ShapeDtypeStruct((channels, rows), jnp.float32),
        in_specs=[wide(a) for a in (queries, fresh_k, fresh_v, stale_k, stale_v, hot_k, hot_v)]
        + [
            packed,
            packed,
            pl.BlockSpec((channels, HD), lambda h: (0, h)),
            pl.BlockSpec((key_rows, 1), lambda h: (0, 0)),
        ],
        out_specs=pl.BlockSpec((channels, rows), lambda h: (0, 0)),
        scratch_shapes=[pltpu.VMEM((key_rows, rows), jnp.float32)],
        cost_estimate=pl.CostEstimate(
            flops=2 * many * (HD + channels), bytes_accessed=12 * 1024 * 1024, transcendentals=many
        ),
        compiler_params=pltpu.CompilerParams(vmem_limit_bytes=VMEM_LIMIT),
        name="attention",
    )(queries, fresh_k, fresh_v, stale_k, stale_v, hot_k, hot_v, text_own, text_other, w_t, bias)


def shards(
    queries,
    fresh_kv,
    stale_kv,
    text_kv,
    w_velocity,
    latent,
    live_counts,
    refresh_rows,
    request_list,
    timesteps,
):
    half_groups = lax.axis_size("grp") // 2
    my_group = lax.axis_index("grp")
    partner = (my_group + half_groups) % (2 * half_groups)
    queries, fresh, stale, text = queries[0], fresh_kv[0], stale_kv[0], text_kv[0]
    slots, img_rows = queries.shape[:2]
    listed_count = refresh_rows.shape[2]
    hot_rows = 2 * listed_count

    both = range(slots)

    def pass_on(block):
        return [from_behind(block, "grp", half_groups)]

    raw = [fresh_kv[0, slot, :listed_count] for slot in both]
    raw_way = [pass_on(raw[slot]) for slot in both]

    my_list = lax.dynamic_index_in_dim(refresh_rows, my_group, 0, keepdims=False)
    partner_list = lax.dynamic_index_in_dim(refresh_rows, partner, 0, keepdims=False)
    near, far, sources = swap_pairs(jnp.stack([my_list, partner_list]))
    pairs = jnp.stack([near, far], axis=1).reshape(2, -1)

    rest = img_rows - hot_rows
    cuts = [hot_rows, hot_rows + rest // 2, img_rows]
    layers = [[(slot, start, stop) for slot in both] for start, stop in zip(cuts[:-1], cuts[1:])]
    zone, blocks = arrange(pairs[0], fresh_kv, sum(layers, []), raw)
    zone_way = [pass_on(zone[slot]) for slot in both]
    w_t = w_velocity.T
    text_own = [project_text(text[slot, :, 0], text[slot, :, 1], w_t, zone[slot]) for slot in both]
    text_way = [pass_on(text_own[slot]) for slot in both]
    layer_way = []
    for index in range(len(layers)):
        ways = []
        for slot in both:
            gate = (raw_way, text_way)[index][slot][0]
            ways.append(pass_on(hold(blocks[index * slots + slot], gate)))
        layer_way.append(ways)

    my_live = lax.dynamic_index_in_dim(live_counts, my_group, 0, keepdims=False)
    partner_live = lax.dynamic_index_in_dim(live_counts, partner, 0, keepdims=False)
    row_ids = jnp.arange(img_rows, dtype=jnp.int32)
    hot_source = jnp.concatenate(
        [jnp.broadcast_to(row_ids[:listed_count], partner_list.shape), sources[1]], axis=1
    )
    stale_listed = jnp.any(partner_list[:, :, None] == row_ids, axis=1)
    hot_listed = jnp.any(partner_list[:, :, None] == hot_source[:, None, :], axis=1)
    live = jnp.concatenate(
        [
            row_ids < my_live[:, None],
            (row_ids < partner_live[:, None]) & jnp.logical_not(stale_listed),
            (hot_source < partner_live[:, None]) & hot_listed,
            jnp.ones((slots, 2 * text.shape[1]), dtype=bool),
        ],
        axis=1,
    )
    bias = jnp.where(live, 0.0, -jnp.inf).astype(jnp.float32)[:, :, None]
    partials = []
    for slot in both:
        hot = join_head(
            [raw_way[slot][-1], zone_way[slot][-1]], [(0, 0), (0, listed_count)], (1, hot_rows) + fresh.shape[2:]
        )
        partials.append(
            attention(
                queries[slot],
                fresh[slot, :, 0],
                fresh[slot, :, 1],
                stale[slot, :, 0],
                stale[slot, :, 1],
                hot[0, :, 0],
                hot[0, :, 1],
                text_own[slot],
                text_way[slot][-1],
                w_t,
                bias[slot],
            )
        )
    partial = jnp.stack(partials)

    tp_count = lax.axis_size("tp")
    tp_index = lax.axis_index("tp")
    share = img_rows // tp_count
    if tp_count == 2:
        mine = lax.dynamic_slice_in_dim(partial, tp_index * share, share, 2)
        theirs = lax.dynamic_slice_in_dim(partial, (1 - tp_index) * share, share, 2)
        summed = mine + from_behind(theirs, "tp", 1)
    else:
        summed = lax.psum_scatter(partial, "tp", scatter_dimension=2, tiled=True)
    summed = jnp.swapaxes(summed, 1, 2)
    share_ids = tp_index * share + jnp.arange(share, dtype=jnp.int32)
    live_rows = share_ids[None, :] < my_live[:, None]
    velocity = jnp.where(live_rows[:, :, None], summed, 0.0)
    pair_index = my_group % half_groups
    request_ids = lax.dynamic_slice_in_dim(request_list, pair_index * slots, slots)
    matches = (
        request_ids[:, None] == jnp.arange(timesteps.shape[0], dtype=jnp.int32)[None, :]
    ).astype(jnp.int32)
    times = jnp.sum(matches[:, :, None] * timesteps[None], axis=1)
    step_size = (times[:, 1] - times[:, 0]).astype(jnp.float32) / 1000.0
    latent_next = latent[0] + step_size[:, None, None] * velocity

    next_stale = join_head(
        [raw_way[slot][-1] for slot in both] + [zone_way[slot][-1] for slot in both],
        [(slot, 0) for slot in both] + [(slot, listed_count) for slot in both],
        fresh.shape,
    )
    for pieces, ways in zip(layers, layer_way):
        next_stale = restore(pairs[1], [way[-1] for way in ways], next_stale, pieces)
    return (next_stale[None], velocity[None], latent_next[None])


def solution(mesh):
    return jax.shard_map(
        shards,
        mesh=mesh,
        in_specs=(
            P("grp", None, None, "tp"),
            P("grp", None, None, None, "tp"),
            P("grp", None, None, None, "tp"),
            P("grp", None, None, None, "tp"),
            P("tp", None),
            P("grp", None, "tp", None),
            P(),
            P(),
            P(),
            P(),
        ),
        out_specs=(
            P("grp", None, None, None, "tp"),
            P("grp", None, "tp", None),
            P("grp", None, "tp", None),
        ),
        check_vma=False,
    )
```

```python
import functools
import math

import jax
import jax.numpy as jnp
from jax import lax
from jax.experimental import pallas as pl
from jax.experimental.pallas import tpu as pltpu
from jax.sharding import PartitionSpec as P

HD = 128
HBM = pltpu.MemorySpace.HBM
SMEM = pltpu.MemorySpace.SMEM
VMEM_LIMIT = 32 * 1024 * 1024
WIDE_LIMIT = 60 * 1024 * 1024


def from_behind(block, axis, distance):
    devices = range(lax.axis_size(axis))
    route = [((i - distance) % len(devices), i) for i in devices]
    return lax.ppermute(block, axis, route)


def swap_pairs(lists, first):
    count = lists.shape[2]
    zone = first + jnp.arange(count, dtype=jnp.int32)
    order = jnp.arange(count, dtype=jnp.int32)
    earlier = order[:, None] >= order[None, :]
    free = jnp.logical_not(jnp.any(lists[..., :, None] == zone, axis=2))
    outside = lists >= first + count
    free_rank = jnp.sum((earlier & free[..., None, :]).astype(jnp.int32), axis=3)
    outside_rank = jnp.sum((earlier & outside[..., None, :]).astype(jnp.int32), axis=3)
    match = (
        outside[..., :, None]
        & free[..., None, :]
        & (outside_rank[..., :, None] == free_rank[..., None, :])
    )
    near = jnp.sum(jnp.where(match, order, 0), axis=3)
    sources = jnp.sum(jnp.where(match, lists[..., :, None], 0), axis=2)
    return near, jnp.where(outside, lists, -1), jnp.where(sources > 0, sources, zone)


def swap_rows(pairs, slots, slot, zone, piece, start, stop):
    count = zone.shape[0] - 1

    def step(k, carry):
        far = pairs[(slots + slot) * count + k]
        here = jnp.logical_and(far >= start, far < stop)
        near_row = jnp.where(here, pairs[slot * count + k], count)
        far_row = jnp.where(here, far - start, stop - start)
        moved = zone[near_row]
        zone[near_row] = piece[far_row]
        piece[far_row] = moved
        return carry

    lax.fori_loop(0, count, step, 0, unroll=8)


def relay(copies, sems):
    inner = [pltpu.make_async_copy(c[0], c[1], sems.at[0, i]) for i, c in enumerate(copies)]
    outer = [pltpu.make_async_copy(c[1], c[2], sems.at[1, i]) for i, c in enumerate(copies)]
    for copy in inner:
        copy.start()
    for arrive, leave in zip(inner, outer):
        arrive.wait()
        leave.start()
    for copy in outer:
        copy.wait()


def arrange_kernel(slots, pieces, pairs_ref, fresh_ref, after_ref, *refs):
    zone_out, piece_outs = refs[0], refs[1 : 1 + len(pieces)]
    pairs, zones, rests, sems = refs[1 + len(pieces) :]
    count = zones.shape[1] - 1
    rest_rows = rests.shape[1] - 1
    below = fresh_ref.shape[2] - rest_rows
    copy_pairs = pltpu.make_async_copy(pairs_ref, pairs, sems.at[3 * slots + len(pieces)])
    copy_pairs.start()
    copies_in = []
    for slot in range(slots):
        copies_in.append(
            (
                pltpu.make_async_copy(
                    fresh_ref.at[0, slot, below - count : below], zones.at[slot, :count], sems.at[slot]
                ),
                pltpu.make_async_copy(
                    fresh_ref.at[0, slot, below:], rests.at[slot, :rest_rows], sems.at[slots + slot]
                ),
            )
        )
        for copy in copies_in[-1]:
            copy.start()
    copy_pairs.wait()
    copies_out = []
    for slot in range(slots):
        for copy in copies_in[slot]:
            copy.wait()
        swap_rows(pairs, slots, slot, zones.at[slot], rests.at[slot], below, below + rest_rows)
        copies_out.append(
            pltpu.make_async_copy(zones.at[slot, :count], zone_out.at[slot], sems.at[2 * slots + slot])
        )
        copies_out[-1].start()
        for index, (piece_slot, start, stop) in enumerate(pieces):
            if piece_slot == slot:
                source = rests.at[slot, start - below : stop - below]
                copies_out.append(
                    pltpu.make_async_copy(source, piece_outs[index], sems.at[3 * slots + index])
                )
                copies_out[-1].start()
    for copy in copies_out:
        copy.wait()


def arrange(pairs, fresh_kv, pieces, below, after):
    slots, rows = fresh_kv.shape[1:3]
    tail = fresh_kv.shape[3:]
    count = pairs.shape[0] // (2 * slots)
    outs = pl.pallas_call(
        functools.partial(arrange_kernel, slots, pieces),
        out_shape=[jax.ShapeDtypeStruct((slots, count) + tail, fresh_kv.dtype)]
        + [jax.ShapeDtypeStruct((stop - start,) + tail, fresh_kv.dtype) for _, start, stop in pieces],
        in_specs=[pl.BlockSpec(memory_space=HBM)] * 3,
        out_specs=[pl.BlockSpec(memory_space=HBM)] * (1 + len(pieces)),
        scratch_shapes=[
            pltpu.SMEM(pairs.shape, pairs.dtype),
            pltpu.VMEM((slots, count + 1) + tail, fresh_kv.dtype),
            pltpu.VMEM((slots, rows - below + 1) + tail, fresh_kv.dtype),
            pltpu.SemaphoreType.DMA((3 * slots + len(pieces) + 1,)),
        ],
        cost_estimate=pl.CostEstimate(flops=0, bytes_accessed=4 * fresh_kv.size, transcendentals=0),
        compiler_params=pltpu.CompilerParams(vmem_limit_bytes=WIDE_LIMIT),
        name="arrange",
    )(pairs, fresh_kv, after)
    return outs[0], outs[1:]


def join_kernel(raw_ref, zone_ref, out_ref, raw, zone, sems):
    first, count = raw.shape[1], zone.shape[1]
    inner = [
        pltpu.make_async_copy(raw_ref, raw, sems.at[0]),
        pltpu.make_async_copy(zone_ref, zone, sems.at[1]),
    ]
    outer = [
        pltpu.make_async_copy(raw, out_ref.at[:, :first], sems.at[2]),
        pltpu.make_async_copy(zone, out_ref.at[:, first : first + count], sems.at[3]),
    ]
    for copy in inner:
        copy.start()
    for arrive, leave in zip(inner, outer):
        arrive.wait()
        leave.start()
    for copy in outer:
        copy.wait()


def join_head(raw, zone, shape):
    return pl.pallas_call(
        join_kernel,
        out_shape=jax.ShapeDtypeStruct(shape, raw.dtype),
        in_specs=[pl.BlockSpec(memory_space=HBM)] * 2,
        out_specs=pl.BlockSpec(memory_space=HBM),
        scratch_shapes=[
            pltpu.VMEM(raw.shape, raw.dtype),
            pltpu.VMEM(zone.shape, raw.dtype),
            pltpu.SemaphoreType.DMA((4,)),
        ],
        cost_estimate=pl.CostEstimate(flops=0, bytes_accessed=8 * zone.size, transcendentals=0),
        compiler_params=pltpu.CompilerParams(vmem_limit_bytes=VMEM_LIMIT),
        name="join_head",
    )(raw, zone)


def restore_kernel(slot, start, stop, first, pairs_ref, piece_ref, whole_ref, *refs):
    out_ref, pairs, zone, piece, sems = refs[-5:]
    count = zone.shape[0] - 1
    inner = [
        pltpu.make_async_copy(pairs_ref, pairs, sems.at[4]),
        pltpu.make_async_copy(piece_ref, piece.at[: stop - start], sems.at[0]),
        pltpu.make_async_copy(out_ref.at[slot, first : first + count], zone.at[:count], sems.at[1]),
    ]
    for copy in inner:
        copy.start()
    for copy in inner:
        copy.wait()
    swap_rows(pairs, out_ref.shape[0], slot, zone, piece, start, stop)
    outer = [
        pltpu.make_async_copy(piece.at[: stop - start], out_ref.at[slot, start:stop], sems.at[2]),
        pltpu.make_async_copy(zone.at[:count], out_ref.at[slot, first : first + count], sems.at[3]),
    ]
    for copy in outer:
        copy.start()
    for copy in outer:
        copy.wait()


def restore(pairs, block, whole, piece, first, after=()):
    slot, start, stop = piece
    tail = whole.shape[2:]
    count = pairs.shape[0] // (2 * whole.shape[0])
    return pl.pallas_call(
        functools.partial(restore_kernel, slot, start, stop, first),
        out_shape=jax.ShapeDtypeStruct(whole.shape, whole.dtype),
        in_specs=[pl.BlockSpec(memory_space=HBM)] * (3 + len(after)),
        out_specs=pl.BlockSpec(memory_space=HBM),
        scratch_shapes=[
            pltpu.SMEM(pairs.shape, pairs.dtype),
            pltpu.VMEM((count + 1,) + tail, whole.dtype),
            pltpu.VMEM((stop - start + 1,) + tail, whole.dtype),
            pltpu.SemaphoreType.DMA((5,)),
        ],
        input_output_aliases={2: 0},
        cost_estimate=pl.CostEstimate(flops=0, bytes_accessed=4 * block.size, transcendentals=0),
        compiler_params=pltpu.CompilerParams(vmem_limit_bytes=VMEM_LIMIT),
        name="restore",
    )(pairs, block, whole, *after)


def hold_kernel(block_ref, after_ref, out_ref):
    del block_ref, after_ref, out_ref


def hold(block, after):
    return pl.pallas_call(
        hold_kernel,
        out_shape=jax.ShapeDtypeStruct(block.shape, block.dtype),
        in_specs=[pl.BlockSpec(memory_space=HBM)] * 2,
        out_specs=pl.BlockSpec(memory_space=HBM),
        input_output_aliases={0: 0},
        cost_estimate=pl.CostEstimate(flops=0, bytes_accessed=0, transcendentals=0),
        name="hold",
    )(block, after)


def across(a, b):
    return lax.dot_general(a, b, (((1,), (1,)), ((), ())), preferred_element_type=jnp.float32)


def text_kernel(k_ref, v_ref, w_ref, after_ref, out_ref):
    rows = k_ref.shape[1]
    channels = w_ref.shape[0]
    out_ref[0, 0, :rows, :] = k_ref[0]
    projected = across(w_ref[...], v_ref[0]).astype(out_ref.dtype)
    for part in range(rows // HD):
        start = rows + part * channels
        out_ref[0, 0, start : start + channels, :] = projected[:, part * HD : (part + 1) * HD]


def project_text(keys, values, w_t, after):
    slots, rows, width = keys.shape
    heads = width // HD
    channels = w_t.shape[0]
    packed = rows + channels * rows // HD
    block = pl.BlockSpec((1, rows, HD), lambda s, h: (s, 0, h))
    return pl.pallas_call(
        text_kernel,
        grid=(slots, heads),
        out_shape=jax.ShapeDtypeStruct((slots, heads, packed, HD), keys.dtype),
        in_specs=[block, block, pl.BlockSpec((channels, HD), lambda s, h: (0, h)), pl.BlockSpec(memory_space=HBM)],
        out_specs=pl.BlockSpec((1, 1, packed, HD), lambda s, h: (s, h, 0, 0)),
        cost_estimate=pl.CostEstimate(
            flops=2 * slots * rows * width * channels, bytes_accessed=4 * keys.size * 2, transcendentals=0
        ),
        name="project_text",
    )(keys, values, w_t, after)


def attention_kernel(text_rows, *refs):
    (q_ref, kf_ref, vf_ref, ks_ref, vs_ref, kh_ref, vh_ref, own_ref, other_ref, w_ref, bias_ref) = refs[:11]
    out_ref, scores_ref = refs[11], refs[12]
    head = pl.program_id(1)
    query = q_ref[0]
    w_t = w_ref[...]
    channels = w_t.shape[0]
    scale = 1.0 / math.sqrt(HD)
    pieces = []
    for k_ref, v_ref in ((kf_ref, vf_ref), (ks_ref, vs_ref), (kh_ref, vh_ref)):
        rows = k_ref.shape[1]
        step = min(rows, 256)
        for start in range(0, rows, step):
            pieces.append((k_ref.at[0, start : start + step], v_ref.at[0, start : start + step], step))
    for t_ref in (own_ref, other_ref):
        pieces.append((t_ref.at[0, 0, :text_rows], t_ref, text_rows))
    top = None
    at = 0
    for k_ref, _, rows in pieces:
        scores = across(k_ref[...], query) * scale + bias_ref[0, at : at + rows]
        scores_ref[at : at + rows, :] = scores
        piece_top = jnp.max(scores, axis=0, keepdims=True)
        top = piece_top if top is None else jnp.maximum(top, piece_top)
        at += rows
    total = jnp.zeros_like(top)
    blended = jnp.zeros((channels, query.shape[0]), jnp.float32)
    at = 0
    for _, v_ref, rows in pieces:
        weights = jnp.exp(scores_ref[at : at + rows, :] - top)
        total += jnp.sum(weights, axis=0, keepdims=True)
        rounded = weights.astype(jnp.bfloat16)
        if v_ref.shape[-2] == rows and len(v_ref.shape) == 2:
            projected = across(w_t, v_ref[...]).astype(jnp.bfloat16)
            blended += jnp.dot(projected, rounded, preferred_element_type=jnp.float32)
        else:
            for part in range(rows // HD):
                start = rows + part * channels
                blended += jnp.dot(
                    v_ref[0, 0, start : start + channels, :],
                    rounded[part * HD : (part + 1) * HD],
                    preferred_element_type=jnp.float32,
                )
        at += rows
    term = blended / total

    @pl.when(head == 0)
    def _():
        out_ref[0] = term

    @pl.when(head != 0)
    def _():
        out_ref[0] += term


def attention(queries, fresh_k, fresh_v, stale_k, stale_v, hot_k, hot_v, text_own, text_other, w_t, bias):
    slots, rows, width = queries.shape
    heads = width // HD
    channels = w_t.shape[0]
    key_rows = bias.shape[1]
    text_rows = (text_own.shape[2] * HD) // (HD + channels)

    def wide(array):
        return pl.BlockSpec((1, array.shape[1], HD), lambda s, h: (s, 0, h))

    packed = pl.BlockSpec((1, 1) + text_own.shape[2:], lambda s, h: (s, h, 0, 0))
    many = slots * heads * rows * key_rows
    return pl.pallas_call(
        functools.partial(attention_kernel, text_rows),
        grid=(slots, heads),
        out_shape=jax.ShapeDtypeStruct((slots, channels, rows), jnp.float32),
        in_specs=[wide(a) for a in (queries, fresh_k, fresh_v, stale_k, stale_v, hot_k, hot_v)]
        + [
            packed,
            packed,
            pl.BlockSpec((channels, HD), lambda s, h: (0, h)),
            pl.BlockSpec((1, key_rows, 1), lambda s, h: (s, 0, 0)),
        ],
        out_specs=pl.BlockSpec((1, channels, rows), lambda s, h: (s, 0, 0)),
        scratch_shapes=[pltpu.VMEM((key_rows, rows), jnp.float32)],
        cost_estimate=pl.CostEstimate(
            flops=2 * many * (HD + channels), bytes_accessed=24 * 1024 * 1024, transcendentals=many
        ),
        compiler_params=pltpu.CompilerParams(vmem_limit_bytes=VMEM_LIMIT),
        name="attention",
    )(queries, fresh_k, fresh_v, stale_k, stale_v, hot_k, hot_v, text_own, text_other, w_t, bias)


def shards(
    queries,
    fresh_kv,
    stale_kv,
    text_kv,
    w_velocity,
    latent,
    live_counts,
    refresh_rows,
    request_list,
    timesteps,
):
    half_groups = lax.axis_size("grp") // 2
    my_group = lax.axis_index("grp")
    partner = (my_group + half_groups) % (2 * half_groups)
    queries, fresh, stale, text = queries[0], fresh_kv[0], stale_kv[0], text_kv[0]
    slots, img_rows = queries.shape[:2]
    listed_count = refresh_rows.shape[2]
    first = listed_count // 2
    hot_rows = first + listed_count

    raw = fresh_kv[0, :, :first]
    raw_in = from_behind(raw, "grp", half_groups)

    my_list = lax.dynamic_index_in_dim(refresh_rows, my_group, 0, keepdims=False)
    partner_list = lax.dynamic_index_in_dim(refresh_rows, partner, 0, keepdims=False)
    near, far, sources = swap_pairs(jnp.stack([my_list, partner_list]), first)
    pairs = jnp.stack([near, far], axis=1).reshape(2, -1)

    first_cut = hot_rows + (img_rows - hot_rows) * 5 // 8
    last_cut = img_rows - listed_count
    final = slots - 1
    pieces = [(slot, hot_rows, img_rows) for slot in range(final)]
    pieces += [(final, hot_rows, first_cut), (final, first_cut, last_cut), (final, last_cut, img_rows)]
    zone, blocks = arrange(pairs[0], fresh_kv, pieces, hot_rows, raw)
    zone_in = from_behind(zone, "grp", half_groups)
    w_t = w_velocity.T
    text_own = project_text(text[:, :, 0], text[:, :, 1], w_t, zone)
    text_in = from_behind(text_own, "grp", half_groups)
    arrived, held = [], []
    for index, block in enumerate(blocks):
        if index < final:
            gate = raw_in
        elif index == final:
            gate = text_in
        else:
            gate = arrived[index - 2]
        held.append(hold(block, gate))
        arrived.append(from_behind(held[-1], "grp", half_groups))

    my_live = lax.dynamic_index_in_dim(live_counts, my_group, 0, keepdims=False)
    partner_live = lax.dynamic_index_in_dim(live_counts, partner, 0, keepdims=False)
    row_ids = jnp.arange(img_rows, dtype=jnp.int32)
    hot_source = jnp.concatenate(
        [jnp.broadcast_to(row_ids[:first], (slots, first)), sources[1]], axis=1
    )
    stale_listed = jnp.any(partner_list[:, :, None] == row_ids, axis=1)
    hot_listed = jnp.any(partner_list[:, :, None] == hot_source[:, None, :], axis=1)
    live = jnp.concatenate(
        [
            row_ids < my_live[:, None],
            (row_ids < partner_live[:, None]) & jnp.logical_not(stale_listed),
            (hot_source < partner_live[:, None]) & hot_listed,
            jnp.ones((slots, 2 * text.shape[1]), dtype=bool),
        ],
        axis=1,
    )
    bias = jnp.where(live, 0.0, -jnp.inf).astype(jnp.float32)[:, :, None]
    hot = join_head(raw_in, zone_in, (slots, hot_rows) + fresh.shape[2:])
    partial = attention(
        queries,
        fresh[:, :, 0],
        fresh[:, :, 1],
        stale[:, :, 0],
        stale[:, :, 1],
        hot[:, :, 0],
        hot[:, :, 1],
        text_own,
        text_in,
        w_t,
        bias,
    )

    tp_count = lax.axis_size("tp")
    tp_index = lax.axis_index("tp")
    share = img_rows // tp_count
    if tp_count == 2:
        mine = lax.dynamic_slice_in_dim(partial, tp_index * share, share, 2)
        theirs = lax.dynamic_slice_in_dim(partial, (1 - tp_index) * share, share, 2)
        summed = mine + from_behind(theirs, "tp", 1)
    else:
        summed = lax.psum_scatter(partial, "tp", scatter_dimension=2, tiled=True)
    summed = jnp.swapaxes(summed, 1, 2)
    share_ids = tp_index * share + jnp.arange(share, dtype=jnp.int32)
    live_rows = share_ids[None, :] < my_live[:, None]
    velocity = jnp.where(live_rows[:, :, None], summed, 0.0)
    pair_index = my_group % half_groups
    request_ids = lax.dynamic_slice_in_dim(request_list, pair_index * slots, slots)
    matches = (
        request_ids[:, None] == jnp.arange(timesteps.shape[0], dtype=jnp.int32)[None, :]
    ).astype(jnp.int32)
    times = jnp.sum(matches[:, :, None] * timesteps[None], axis=1)
    step_size = (times[:, 1] - times[:, 0]).astype(jnp.float32) / 1000.0
    latent_next = latent[0] + step_size[:, None, None] * velocity

    next_stale = join_head(raw_in, zone_in, fresh.shape)
    for index, piece in enumerate(pieces):
        next_stale = restore(pairs[1], arrived[index], next_stale, piece, first, held[index + 2 : index + 3])
    return (next_stale[None], velocity[None], latent_next[None])


def solution(mesh):
    return jax.shard_map(
        shards,
        mesh=mesh,
        in_specs=(
            P("grp", None, None, "tp"),
            P("grp", None, None, None, "tp"),
            P("grp", None, None, None, "tp"),
            P("grp", None, None, None, "tp"),
            P("tp", None),
            P("grp", None, "tp", None),
            P(),
            P(),
            P(),
            P(),
        ),
        out_specs=(
            P("grp", None, None, None, "tp"),
            P("grp", None, "tp", None),
            P("grp", None, "tp", None),
        ),
        check_vma=False,
    )
```

```python
import functools
import math

import jax
import jax.numpy as jnp
from jax import lax
from jax.experimental import pallas as pl
from jax.experimental.pallas import tpu as pltpu
from jax.sharding import PartitionSpec as P

HD = 128
HBM = pltpu.MemorySpace.HBM
SMEM = pltpu.MemorySpace.SMEM
VMEM_LIMIT = 32 * 1024 * 1024
WIDE_LIMIT = 60 * 1024 * 1024


def from_behind(block, axis, distance):
    devices = range(lax.axis_size(axis))
    route = [((i - distance) % len(devices), i) for i in devices]
    return lax.ppermute(block, axis, route)


def swap_pairs(lists, first):
    count = lists.shape[2]
    zone = first + jnp.arange(count, dtype=jnp.int32)
    order = jnp.arange(count, dtype=jnp.int32)
    earlier = order[:, None] >= order[None, :]
    free = jnp.logical_not(jnp.any(lists[..., :, None] == zone, axis=2))
    outside = lists >= first + count
    free_rank = jnp.sum((earlier & free[..., None, :]).astype(jnp.int32), axis=3)
    outside_rank = jnp.sum((earlier & outside[..., None, :]).astype(jnp.int32), axis=3)
    match = (
        outside[..., :, None]
        & free[..., None, :]
        & (outside_rank[..., :, None] == free_rank[..., None, :])
    )
    near = jnp.sum(jnp.where(match, order, 0), axis=3)
    sources = jnp.sum(jnp.where(match, lists[..., :, None], 0), axis=2)
    return near, jnp.where(outside, lists, -1), jnp.where(sources > 0, sources, zone)


def swap_rows(pairs, slots, slot, zone, piece, start, stop):
    count = zone.shape[0] - 1

    def step(k, carry):
        far = pairs[(slots + slot) * count + k]
        here = jnp.logical_and(far >= start, far < stop)
        near_row = jnp.where(here, pairs[slot * count + k], count)
        far_row = jnp.where(here, far - start, stop - start)
        moved = zone[near_row]
        zone[near_row] = piece[far_row]
        piece[far_row] = moved
        return carry

    lax.fori_loop(0, count, step, 0, unroll=8)


def relay(copies, sems):
    inner = [pltpu.make_async_copy(c[0], c[1], sems.at[0, i]) for i, c in enumerate(copies)]
    outer = [pltpu.make_async_copy(c[1], c[2], sems.at[1, i]) for i, c in enumerate(copies)]
    for copy in inner:
        copy.start()
    for arrive, leave in zip(inner, outer):
        arrive.wait()
        leave.start()
    for copy in outer:
        copy.wait()


def arrange_kernel(slots, pieces, pairs_ref, fresh_ref, after_ref, *refs):
    zone_out, piece_outs = refs[0], refs[1 : 1 + len(pieces)]
    pairs, zones, rests, sems = refs[1 + len(pieces) :]
    count = zones.shape[1] - 1
    rest_rows = rests.shape[1] - 1
    below = fresh_ref.shape[2] - rest_rows
    copy_pairs = pltpu.make_async_copy(pairs_ref, pairs, sems.at[3 * slots + len(pieces)])
    copy_pairs.start()
    copies_in = []
    for slot in range(slots):
        copies_in.append(
            (
                pltpu.make_async_copy(
                    fresh_ref.at[0, slot, below - count : below], zones.at[slot, :count], sems.at[slot]
                ),
                pltpu.make_async_copy(
                    fresh_ref.at[0, slot, below:], rests.at[slot, :rest_rows], sems.at[slots + slot]
                ),
            )
        )
        for copy in copies_in[-1]:
            copy.start()
    copy_pairs.wait()
    copies_out = []
    for slot in range(slots):
        for copy in copies_in[slot]:
            copy.wait()
        swap_rows(pairs, slots, slot, zones.at[slot], rests.at[slot], below, below + rest_rows)
        copies_out.append(
            pltpu.make_async_copy(zones.at[slot, :count], zone_out.at[slot], sems.at[2 * slots + slot])
        )
        copies_out[-1].start()
        for index, (piece_slot, start, stop) in enumerate(pieces):
            if piece_slot == slot:
                source = rests.at[slot, start - below : stop - below]
                copies_out.append(
                    pltpu.make_async_copy(source, piece_outs[index], sems.at[3 * slots + index])
                )
                copies_out[-1].start()
    for copy in copies_out:
        copy.wait()


def arrange(pairs, fresh_kv, pieces, below, after):
    slots, rows = fresh_kv.shape[1:3]
    tail = fresh_kv.shape[3:]
    count = pairs.shape[0] // (2 * slots)
    outs = pl.pallas_call(
        functools.partial(arrange_kernel, slots, pieces),
        out_shape=[jax.ShapeDtypeStruct((slots, count) + tail, fresh_kv.dtype)]
        + [jax.ShapeDtypeStruct((stop - start,) + tail, fresh_kv.dtype) for _, start, stop in pieces],
        in_specs=[pl.BlockSpec(memory_space=HBM)] * 3,
        out_specs=[pl.BlockSpec(memory_space=HBM)] * (1 + len(pieces)),
        scratch_shapes=[
            pltpu.SMEM(pairs.shape, pairs.dtype),
            pltpu.VMEM((slots, count + 1) + tail, fresh_kv.dtype),
            pltpu.VMEM((slots, rows - below + 1) + tail, fresh_kv.dtype),
            pltpu.SemaphoreType.DMA((3 * slots + len(pieces) + 1,)),
        ],
        cost_estimate=pl.CostEstimate(flops=0, bytes_accessed=4 * fresh_kv.size, transcendentals=0),
        compiler_params=pltpu.CompilerParams(vmem_limit_bytes=WIDE_LIMIT),
        name="arrange",
    )(pairs, fresh_kv, after)
    return outs[0], outs[1:]


def join_kernel(raw_ref, zone_ref, out_ref, raw, zone, sems):
    first, count = raw.shape[1], zone.shape[1]
    inner = [
        pltpu.make_async_copy(raw_ref, raw, sems.at[0]),
        pltpu.make_async_copy(zone_ref, zone, sems.at[1]),
    ]
    outer = [
        pltpu.make_async_copy(raw, out_ref.at[:, :first], sems.at[2]),
        pltpu.make_async_copy(zone, out_ref.at[:, first : first + count], sems.at[3]),
    ]
    for copy in inner:
        copy.start()
    for arrive, leave in zip(inner, outer):
        arrive.wait()
        leave.start()
    for copy in outer:
        copy.wait()


def join_head(raw, zone, shape):
    return pl.pallas_call(
        join_kernel,
        out_shape=jax.ShapeDtypeStruct(shape, raw.dtype),
        in_specs=[pl.BlockSpec(memory_space=HBM)] * 2,
        out_specs=pl.BlockSpec(memory_space=HBM),
        scratch_shapes=[
            pltpu.VMEM(raw.shape, raw.dtype),
            pltpu.VMEM(zone.shape, raw.dtype),
            pltpu.SemaphoreType.DMA((4,)),
        ],
        cost_estimate=pl.CostEstimate(flops=0, bytes_accessed=8 * zone.size, transcendentals=0),
        compiler_params=pltpu.CompilerParams(vmem_limit_bytes=VMEM_LIMIT),
        name="join_head",
    )(raw, zone)


def restore_kernel(slot, start, stop, first, pairs_ref, piece_ref, whole_ref, *refs):
    out_ref, zone_out, pairs, zone, piece, sems = refs[-6:]
    count = zone.shape[0] - 1
    inner = [
        pltpu.make_async_copy(pairs_ref, pairs, sems.at[4]),
        pltpu.make_async_copy(piece_ref, piece.at[: stop - start], sems.at[0]),
        pltpu.make_async_copy(out_ref.at[slot, first : first + count], zone.at[:count], sems.at[1]),
    ]
    for copy in inner:
        copy.start()
    for copy in inner:
        copy.wait()
    swap_rows(pairs, out_ref.shape[0], slot, zone, piece, start, stop)
    outer = [
        pltpu.make_async_copy(piece.at[: stop - start], out_ref.at[slot, start:stop], sems.at[2]),
        pltpu.make_async_copy(zone.at[:count], out_ref.at[slot, first : first + count], sems.at[3]),
        pltpu.make_async_copy(zone.at[:count], zone_out, sems.at[5]),
    ]
    for copy in outer:
        copy.start()
    for copy in outer:
        copy.wait()


def restore(pairs, block, whole, piece, first, after=()):
    slot, start, stop = piece
    tail = whole.shape[2:]
    count = pairs.shape[0] // (2 * whole.shape[0])
    return pl.pallas_call(
        functools.partial(restore_kernel, slot, start, stop, first),
        out_shape=[
            jax.ShapeDtypeStruct(whole.shape, whole.dtype),
            jax.ShapeDtypeStruct((count,) + tail, whole.dtype),
        ],
        in_specs=[pl.BlockSpec(memory_space=HBM)] * (3 + len(after)),
        out_specs=[pl.BlockSpec(memory_space=HBM)] * 2,
        scratch_shapes=[
            pltpu.SMEM(pairs.shape, pairs.dtype),
            pltpu.VMEM((count + 1,) + tail, whole.dtype),
            pltpu.VMEM((stop - start + 1,) + tail, whole.dtype),
            pltpu.SemaphoreType.DMA((6,)),
        ],
        input_output_aliases={2: 0},
        cost_estimate=pl.CostEstimate(flops=0, bytes_accessed=4 * block.size, transcendentals=0),
        compiler_params=pltpu.CompilerParams(vmem_limit_bytes=VMEM_LIMIT),
        name="restore",
    )(pairs, block, whole, *after)


def finish_kernel(slot, start, stop, first, pairs_ref, piece_ref, zone_ref, whole_ref, out_ref, pairs, zone, piece, sems):
    count, rows = zone.shape[0] - 1, stop - start
    copy_pairs = pltpu.make_async_copy(pairs_ref, pairs, sems.at[0])
    copy_pairs.start()
    zone[:count] = zone_ref[...]
    piece[:rows] = piece_ref[...]
    copy_pairs.wait()
    swap_rows(pairs, out_ref.shape[0], slot, zone, piece, start, stop)
    outer = [
        pltpu.make_async_copy(piece.at[:rows], out_ref.at[slot, start:stop], sems.at[1]),
        pltpu.make_async_copy(zone.at[:count], out_ref.at[slot, first : first + count], sems.at[2]),
    ]
    for copy in outer:
        copy.start()
    for copy in outer:
        copy.wait()


def finish(pairs, block, zone, whole, piece, first):
    slot, start, stop = piece
    tail = whole.shape[2:]
    count = zone.shape[0]
    return pl.pallas_call(
        functools.partial(finish_kernel, slot, start, stop, first),
        out_shape=jax.ShapeDtypeStruct(whole.shape, whole.dtype),
        in_specs=[
            pl.BlockSpec(memory_space=HBM),
            pl.BlockSpec(memory_space=pltpu.VMEM),
            pl.BlockSpec(memory_space=pltpu.VMEM),
            pl.BlockSpec(memory_space=HBM),
        ],
        out_specs=pl.BlockSpec(memory_space=HBM),
        scratch_shapes=[
            pltpu.SMEM(pairs.shape, pairs.dtype),
            pltpu.VMEM((count + 1,) + tail, whole.dtype),
            pltpu.VMEM((stop - start + 1,) + tail, whole.dtype),
            pltpu.SemaphoreType.DMA((3,)),
        ],
        input_output_aliases={3: 0},
        cost_estimate=pl.CostEstimate(flops=0, bytes_accessed=4 * block.size, transcendentals=0),
        compiler_params=pltpu.CompilerParams(vmem_limit_bytes=VMEM_LIMIT),
        name="finish",
    )(pairs, block, zone, whole)


def hold_kernel(block_ref, after_ref, out_ref):
    del block_ref, after_ref, out_ref


def hold(block, after):
    return pl.pallas_call(
        hold_kernel,
        out_shape=jax.ShapeDtypeStruct(block.shape, block.dtype),
        in_specs=[pl.BlockSpec(memory_space=HBM)] * 2,
        out_specs=pl.BlockSpec(memory_space=HBM),
        input_output_aliases={0: 0},
        cost_estimate=pl.CostEstimate(flops=0, bytes_accessed=0, transcendentals=0),
        name="hold",
    )(block, after)


def across(a, b):
    return lax.dot_general(a, b, (((1,), (1,)), ((), ())), preferred_element_type=jnp.float32)


def text_kernel(k_ref, v_ref, w_ref, after_ref, out_ref):
    rows = k_ref.shape[1]
    channels = w_ref.shape[0]
    out_ref[0, 0, :rows, :] = k_ref[0]
    projected = across(w_ref[...], v_ref[0]).astype(out_ref.dtype)
    for part in range(rows // HD):
        start = rows + part * channels
        out_ref[0, 0, start : start + channels, :] = projected[:, part * HD : (part + 1) * HD]


def project_text(keys, values, w_t, after):
    slots, rows, width = keys.shape
    heads = width // HD
    channels = w_t.shape[0]
    packed = rows + channels * rows // HD
    block = pl.BlockSpec((1, rows, HD), lambda s, h: (s, 0, h))
    return pl.pallas_call(
        text_kernel,
        grid=(slots, heads),
        out_shape=jax.ShapeDtypeStruct((slots, heads, packed, HD), keys.dtype),
        in_specs=[block, block, pl.BlockSpec((channels, HD), lambda s, h: (0, h)), pl.BlockSpec(memory_space=HBM)],
        out_specs=pl.BlockSpec((1, 1, packed, HD), lambda s, h: (s, h, 0, 0)),
        cost_estimate=pl.CostEstimate(
            flops=2 * slots * rows * width * channels, bytes_accessed=4 * keys.size * 2, transcendentals=0
        ),
        name="project_text",
    )(keys, values, w_t, after)


def attention_kernel(text_rows, *refs):
    (q_ref, kf_ref, vf_ref, ks_ref, vs_ref, kh_ref, vh_ref, own_ref, other_ref, w_ref, bias_ref) = refs[:11]
    out_ref, scores_ref = refs[11], refs[12]
    head = pl.program_id(1)
    query = q_ref[0]
    w_t = w_ref[...]
    channels = w_t.shape[0]
    scale = 1.0 / math.sqrt(HD)
    pieces = []
    for k_ref, v_ref in ((kf_ref, vf_ref), (ks_ref, vs_ref), (kh_ref, vh_ref)):
        rows = k_ref.shape[1]
        step = min(rows, 256)
        for start in range(0, rows, step):
            pieces.append((k_ref.at[0, start : start + step], v_ref.at[0, start : start + step], step))
    for t_ref in (own_ref, other_ref):
        pieces.append((t_ref.at[0, 0, :text_rows], t_ref, text_rows))
    top = None
    at = 0
    for k_ref, _, rows in pieces:
        scores = across(k_ref[...], query) * scale + bias_ref[0, at : at + rows]
        scores_ref[at : at + rows, :] = scores
        piece_top = jnp.max(scores, axis=0, keepdims=True)
        top = piece_top if top is None else jnp.maximum(top, piece_top)
        at += rows
    total = jnp.zeros_like(top)
    blended = jnp.zeros((channels, query.shape[0]), jnp.float32)
    at = 0
    for _, v_ref, rows in pieces:
        weights = jnp.exp(scores_ref[at : at + rows, :] - top)
        total += jnp.sum(weights, axis=0, keepdims=True)
        rounded = weights.astype(jnp.bfloat16)
        if v_ref.shape[-2] == rows and len(v_ref.shape) == 2:
            projected = across(w_t, v_ref[...]).astype(jnp.bfloat16)
            blended += jnp.dot(projected, rounded, preferred_element_type=jnp.float32)
        else:
            for part in range(rows // HD):
                start = rows + part * channels
                blended += jnp.dot(
                    v_ref[0, 0, start : start + channels, :],
                    rounded[part * HD : (part + 1) * HD],
                    preferred_element_type=jnp.float32,
                )
        at += rows
    term = blended / total

    @pl.when(head == 0)
    def _():
        out_ref[0] = term

    @pl.when(head != 0)
    def _():
        out_ref[0] += term


def attention(queries, fresh_k, fresh_v, stale_k, stale_v, hot_k, hot_v, text_own, text_other, w_t, bias):
    slots, rows, width = queries.shape
    heads = width // HD
    channels = w_t.shape[0]
    key_rows = bias.shape[1]
    text_rows = (text_own.shape[2] * HD) // (HD + channels)

    def wide(array):
        return pl.BlockSpec((1, array.shape[1], HD), lambda s, h: (s, 0, h))

    packed = pl.BlockSpec((1, 1) + text_own.shape[2:], lambda s, h: (s, h, 0, 0))
    many = slots * heads * rows * key_rows
    return pl.pallas_call(
        functools.partial(attention_kernel, text_rows),
        grid=(slots, heads),
        out_shape=jax.ShapeDtypeStruct((slots, channels, rows), jnp.float32),
        in_specs=[wide(a) for a in (queries, fresh_k, fresh_v, stale_k, stale_v, hot_k, hot_v)]
        + [
            packed,
            packed,
            pl.BlockSpec((channels, HD), lambda s, h: (0, h)),
            pl.BlockSpec((1, key_rows, 1), lambda s, h: (s, 0, 0)),
        ],
        out_specs=pl.BlockSpec((1, channels, rows), lambda s, h: (s, 0, 0)),
        scratch_shapes=[pltpu.VMEM((key_rows, rows), jnp.float32)],
        cost_estimate=pl.CostEstimate(
            flops=2 * many * (HD + channels), bytes_accessed=24 * 1024 * 1024, transcendentals=many
        ),
        compiler_params=pltpu.CompilerParams(vmem_limit_bytes=VMEM_LIMIT),
        name="attention",
    )(queries, fresh_k, fresh_v, stale_k, stale_v, hot_k, hot_v, text_own, text_other, w_t, bias)


def shards(
    queries,
    fresh_kv,
    stale_kv,
    text_kv,
    w_velocity,
    latent,
    live_counts,
    refresh_rows,
    request_list,
    timesteps,
):
    half_groups = lax.axis_size("grp") // 2
    my_group = lax.axis_index("grp")
    partner = (my_group + half_groups) % (2 * half_groups)
    queries, fresh, stale, text = queries[0], fresh_kv[0], stale_kv[0], text_kv[0]
    slots, img_rows = queries.shape[:2]
    listed_count = refresh_rows.shape[2]
    first = listed_count // 2
    hot_rows = first + listed_count

    raw = fresh_kv[0, :, :first]
    raw_in = from_behind(raw, "grp", half_groups)

    my_list = lax.dynamic_index_in_dim(refresh_rows, my_group, 0, keepdims=False)
    partner_list = lax.dynamic_index_in_dim(refresh_rows, partner, 0, keepdims=False)
    near, far, sources = swap_pairs(jnp.stack([my_list, partner_list]), first)
    pairs = jnp.stack([near, far], axis=1).reshape(2, -1)

    first_cut = hot_rows + (img_rows - hot_rows) * 5 // 8
    last_cut = img_rows - listed_count
    final = slots - 1
    pieces = [(slot, hot_rows, img_rows) for slot in range(final)]
    pieces += [(final, hot_rows, first_cut), (final, first_cut, last_cut), (final, last_cut, img_rows)]
    zone, blocks = arrange(pairs[0], fresh_kv, pieces, hot_rows, raw)
    zone_in = from_behind(zone, "grp", half_groups)
    w_t = w_velocity.T
    text_own = project_text(text[:, :, 0], text[:, :, 1], w_t, zone)
    text_in = from_behind(text_own, "grp", half_groups)
    arrived, held = [], []
    for index, block in enumerate(blocks):
        if index < final:
            gate = raw_in
        elif index == final:
            gate = text_in
        else:
            gate = arrived[index - 2]
        held.append(hold(block, gate))
        arrived.append(from_behind(held[-1], "grp", half_groups))

    my_live = lax.dynamic_index_in_dim(live_counts, my_group, 0, keepdims=False)
    partner_live = lax.dynamic_index_in_dim(live_counts, partner, 0, keepdims=False)
    row_ids = jnp.arange(img_rows, dtype=jnp.int32)
    hot_source = jnp.concatenate(
        [jnp.broadcast_to(row_ids[:first], (slots, first)), sources[1]], axis=1
    )
    stale_listed = jnp.any(partner_list[:, :, None] == row_ids, axis=1)
    hot_listed = jnp.any(partner_list[:, :, None] == hot_source[:, None, :], axis=1)
    live = jnp.concatenate(
        [
            row_ids < my_live[:, None],
            (row_ids < partner_live[:, None]) & jnp.logical_not(stale_listed),
            (hot_source < partner_live[:, None]) & hot_listed,
            jnp.ones((slots, 2 * text.shape[1]), dtype=bool),
        ],
        axis=1,
    )
    bias = jnp.where(live, 0.0, -jnp.inf).astype(jnp.float32)[:, :, None]
    hot = join_head(raw_in, zone_in, (slots, hot_rows) + fresh.shape[2:])
    partial = attention(
        queries,
        fresh[:, :, 0],
        fresh[:, :, 1],
        stale[:, :, 0],
        stale[:, :, 1],
        hot[:, :, 0],
        hot[:, :, 1],
        text_own,
        text_in,
        w_t,
        bias,
    )

    tp_count = lax.axis_size("tp")
    tp_index = lax.axis_index("tp")
    share = img_rows // tp_count
    if tp_count == 2:
        mine = lax.dynamic_slice_in_dim(partial, tp_index * share, share, 2)
        theirs = lax.dynamic_slice_in_dim(partial, (1 - tp_index) * share, share, 2)
        summed = mine + from_behind(theirs, "tp", 1)
    else:
        summed = lax.psum_scatter(partial, "tp", scatter_dimension=2, tiled=True)
    summed = jnp.swapaxes(summed, 1, 2)
    share_ids = tp_index * share + jnp.arange(share, dtype=jnp.int32)
    live_rows = share_ids[None, :] < my_live[:, None]
    velocity = jnp.where(live_rows[:, :, None], summed, 0.0)
    pair_index = my_group % half_groups
    request_ids = lax.dynamic_slice_in_dim(request_list, pair_index * slots, slots)
    matches = (
        request_ids[:, None] == jnp.arange(timesteps.shape[0], dtype=jnp.int32)[None, :]
    ).astype(jnp.int32)
    times = jnp.sum(matches[:, :, None] * timesteps[None], axis=1)
    step_size = (times[:, 1] - times[:, 0]).astype(jnp.float32) / 1000.0
    latent_next = latent[0] + step_size[:, None, None] * velocity

    next_stale = join_head(raw_in, zone_in, fresh.shape)
    for index, piece in enumerate(pieces[:-1]):
        next_stale, zone_now = restore(
            pairs[1], arrived[index], next_stale, piece, first, held[index + 2 : index + 3]
        )
    next_stale = finish(pairs[1], arrived[-1], zone_now, next_stale, pieces[-1], first)
    return (next_stale[None], velocity[None], latent_next[None])


def solution(mesh):
    return jax.shard_map(
        shards,
        mesh=mesh,
        in_specs=(
            P("grp", None, None, "tp"),
            P("grp", None, None, None, "tp"),
            P("grp", None, None, None, "tp"),
            P("grp", None, None, None, "tp"),
            P("tp", None),
            P("grp", None, "tp", None),
            P(),
            P(),
            P(),
            P(),
        ),
        out_specs=(
            P("grp", None, None, None, "tp"),
            P("grp", None, "tp", None),
            P("grp", None, "tp", None),
        ),
        check_vma=False,
    )
```
